128 devices in a mesh: sp: 16 (over z, y), hd: 8 (over x, core).
Axes of the slice: x: 4, y: 4, z: 4, core: 2. Of those that a mesh axis runs over, the one named last changes fastest.
Arguments:
- latent: bfloat16 [8, 64, 64, 320], P(None, 'sp', 'hd'), may hold values from -6 to 6
- condition: bfloat16 [8, 64, 64, 192], P(None, 'sp', 'hd'), may hold values from -6 to 6
- text_states: bfloat16 [8, 77, 768], replicated, may hold values from -6 to 6
- valid_rows: int32 [8], replicated, may hold values from 16 to 64, as said below
- text_lengths: int32 [8], replicated, may hold values from 8 to 77, as said below
- w_in: bfloat16 [192, 320], replicated, may hold values from -0.4375 to 0.4375
- b_in: float32 [320], replicated, may hold values from -3 to 3
- w_conv: bfloat16 [3, 3, 320, 320], replicated, may hold values from -0.109375 to 0.109375
- b_conv: float32 [320], replicated, may hold values from -3 to 3
- w_out: bfloat16 [320, 320], replicated, may hold values from -0.3125 to 0.3125
- b_out: float32 [320], replicated, may hold values from -3 to 3
- w_query: bfloat16 [320, 320], replicated, may hold values from -0.3125 to 0.3125
- w_key: bfloat16 [320, 320], replicated, may hold values from -0.3125 to 0.3125
- w_value: bfloat16 [320, 320], replicated, may hold values from -0.3125 to 0.3125
- w_attn_out: bfloat16 [320, 320], replicated, may hold values from -6 to 6
- b_attn_out: float32 [320], replicated, may hold values from -3 to 3
- w_cross_query: bfloat16 [320, 320], replicated, may hold values from -0.3125 to 0.3125
- w_cross_key: bfloat16 [768, 320], replicated, may hold values from -0.21875 to 0.21875
- w_cross_value: bfloat16 [768, 320], replicated, may hold values from -0.21875 to 0.21875
- w_cross_out: bfloat16 [320, 320], replicated, may hold values from -2 to 2
- b_cross_out: float32 [320], replicated, may hold values from -3 to 3
- w_ff_in: bfloat16 [320, 2560], replicated, may hold values from -0.3125 to 0.3125
- b_ff_in: float32 [2560], replicated, may hold values from -3 to 3
- w_ff_out: bfloat16 [1280, 320], replicated, may hold values from -0.15625 to 0.15625
- b_ff_out: float32 [320], replicated, may hold values from -3 to 3
- cotangent: bfloat16 [8, 64, 64, 320], P(None, 'sp', 'hd'), may hold values from -6 to 6
Outputs:
- mixed_out: bfloat16 [8, 64, 64, 320], P(None, 'sp', 'hd')
- latent_grad: float32 [8, 64, 64, 320], P(None, 'sp', 'hd')
- grad_w_in: float32 [192, 320], replicated
- grad_b_in: float32 [320], replicated
- grad_w_conv: float32 [3, 3, 320, 320], replicated
- grad_b_conv: float32 [320], replicated
- grad_w_out: float32 [320, 320], replicated
- grad_b_out: float32 [320], replicated
The draws below stay inside these ranges and needn't reach their ends.
Inputs may be any that keep to these rules, and one draw needn't show every extreme that they name: `valid_rows`: some item has all 64 rows valid. The first text_lengths[item] tokens are valid; some item has all 77.
All inputs are finite; a program needn't handle non-finite values.
Results may differ from the reference program's by a relative error of at most 0.012.
Values may be sent and summed in bfloat16 or wider, within the bound.
No kernel may reach another device: no remote copies, remote signals or barrier semaphores. Data moves between devices by JAX's collectives and lax.ppermute only.
A program may use at most 128 MiB of HBM per device.

```python
import jax
import jax.numpy as jnp
from jax import lax

C = 320
CIN = 192
HEADS = 8
FF = 1280
TEXT_LEN = 77
TEXT_D = 768
ITEMS = 8
H = 64
W = 64


def draw_valid_rows(key, part):
    key = jax.random.fold_in(key, 11)
    key_rows, key_pick = jax.random.split(key)
    counts = jax.random.randint(key_rows, (ITEMS,), H // 4, H + 1)
    chosen = jax.random.randint(key_pick, (), 0, ITEMS)
    return jnp.where(jnp.arange(ITEMS) == chosen, H, counts).astype(jnp.int32)


def draw_text_lengths(key, part):
    key = jax.random.fold_in(key, 23)
    key_rows, key_pick = jax.random.split(key)
    counts = jax.random.randint(key_rows, (ITEMS,), 8, TEXT_LEN + 1)
    chosen = jax.random.randint(key_pick, (), 0, ITEMS)
    return jnp.where(jnp.arange(ITEMS) == chosen, TEXT_LEN, counts).astype(jnp.int32)


def shard_levels(stream_key, extent, cuts, low, largest):
    gain = 1.0
    for axis_at, shards_of in cuts:
        draws = jax.random.uniform(jax.random.fold_in(jax.random.fold_in(stream_key, 6), axis_at), (shards_of,), jnp.float32, low / len(cuts), largest / len(cuts))
        gain = gain * jnp.repeat(jnp.exp(draws), extent[axis_at] // shards_of).reshape((-1,) + (1,) * (len(extent) - 1 - axis_at))
    return gain


def bell_draw(rng, shape, scale, reach, cuts=(), kind=jnp.bfloat16):
    gain = shard_levels(rng, shape, cuts, -0.22, 0.18) if cuts else 1.0
    array = jax.random.normal(rng, shape, jnp.float32) * scale * gain
    return jnp.minimum(jnp.maximum(array, -reach), reach).astype(kind)


def setup_inputs(seed: int = 0) -> dict:
    key_list = jax.random.split(jax.random.key(seed), 27)
    return {
        "latent": bell_draw(key_list[0], (ITEMS, H, W, C), 1.0, 6.0, ((1, 16), (2, 8))),
        "condition": bell_draw(key_list[1], (ITEMS, H, W, CIN), 1.0, 6.0, ((1, 16), (2, 8))),
        "text_states": bell_draw(key_list[2], (ITEMS, TEXT_LEN, TEXT_D), 1.0, 6.0),
        "valid_rows": draw_valid_rows(jax.random.fold_in(key_list[26], 71), 0),
        "text_lengths": draw_text_lengths(jax.random.fold_in(key_list[26], 71), 0),
        "w_in": bell_draw(key_list[5], (CIN, C), CIN ** -0.5, 0.4375),
        "b_in": bell_draw(key_list[6], (C,), 0.5, 3.0, (), jnp.float32),
        "w_conv": bell_draw(key_list[7], (3, 3, C, C), (9 * C) ** -0.5, 0.109375),
        "b_conv": bell_draw(key_list[8], (C,), 0.5, 3.0, (), jnp.float32),
        "w_out": bell_draw(key_list[9], (C, C), C ** -0.5, 0.3125),
        "b_out": bell_draw(key_list[10], (C,), 0.5, 3.0, (), jnp.float32),
        "w_query": bell_draw(key_list[11], (C, C), C ** -0.5, 0.3125),
        "w_key": bell_draw(key_list[12], (C, C), C ** -0.5, 0.3125),
        "w_value": bell_draw(key_list[13], (C, C), C ** -0.5, 0.3125),
        "w_attn_out": bell_draw(key_list[14], (C, C), 1 ** -0.5, 6.0),
        "b_attn_out": bell_draw(key_list[15], (C,), 0.5, 3.0, (), jnp.float32),
        "w_cross_query": bell_draw(key_list[16], (C, C), C ** -0.5, 0.3125),
        "w_cross_key": bell_draw(key_list[17], (TEXT_D, C), TEXT_D ** -0.5, 0.21875),
        "w_cross_value": bell_draw(key_list[18], (TEXT_D, C), TEXT_D ** -0.5, 0.21875),
        "w_cross_out": bell_draw(key_list[19], (C, C), (C // 32) ** -0.5, 2.0),
        "b_cross_out": bell_draw(key_list[20], (C,), 0.5, 3.0, (), jnp.float32),
        "w_ff_in": bell_draw(key_list[21], (C, 2 * FF), C ** -0.5, 0.3125),
        "b_ff_in": bell_draw(key_list[22], (2 * FF,), 0.5, 3.0, (), jnp.float32),
        "w_ff_out": bell_draw(key_list[23], (FF, C), FF ** -0.5, 0.15625),
        "b_ff_out": bell_draw(key_list[24], (C,), 0.5, 3.0, (), jnp.float32),
        "cotangent": bell_draw(key_list[25], (ITEMS, H, W, C), 1.0, 6.0, ((1, 16), (2, 8))),
    }


@jax.custom_vjp
def low(v):
    return lax.optimization_barrier(v.astype(jnp.bfloat16)).astype(jnp.float32)

@jax.custom_vjp
def low_back(v):
    return v

def low_keep(v):
    return (low(v), None)

def low_pass(kept, grad):
    return (grad,)

def back_keep(v):
    return (v, None)

def back_low(kept, grad):
    return (low(grad),)
low.defvjp(low_keep, low_pass)
low_back.defvjp(back_keep, back_low)
epsilon = 1e-05
masked_score = -1e+30
precise = lax.Precision.HIGHEST

def matmul(left, right):
    return jnp.matmul(left, right, precision=precise)

def normalize(values):
    center = values - lax.optimization_barrier(jnp.mean(values, -1, keepdims=True))
    variance = lax.optimization_barrier(jnp.mean(center * center, -1, keepdims=True))
    return center * lax.rsqrt(variance + epsilon)

def conv_three(source, weight):
    padded = jnp.pad(source, ((0, 0), (1, 1), (1, 1), (0, 0)))
    result = jnp.zeros(source.shape[:3] + (weight.shape[3],), jnp.float32)
    for row_shift in range(3):
        for col_shift in range(3):
            window = padded[:, row_shift:row_shift + H, col_shift:col_shift + W]
            result = result + jnp.einsum('bhwc,cd->bhwd', window, weight[row_shift, col_shift], precision=precise)
    return result

def self_attention(queries, keys_all, values_all, valid_rows):
    scaling = (C // HEADS) ** (-0.5)

    def item_attend(item_args):
        item_q, item_k, item_v, item_valid = item_args
        key_keep = jnp.arange(H * W) // W < item_valid

        def head_attend(head_args):
            head_q, head_k, head_v = head_args
            scores = low_back(scaling * matmul(head_q, head_k.T))
            scores = jnp.where(key_keep[None, :], scores, masked_score)
            probs = jax.nn.softmax(scores, axis=-1)
            return matmul(low(probs), head_v)
        heads_out = lax.map(jax.checkpoint(head_attend), (item_q.transpose(1, 0, 2), item_k.transpose(1, 0, 2), item_v.transpose(1, 0, 2)))
        return heads_out.transpose(1, 0, 2)
    return lax.map(jax.checkpoint(item_attend), (queries, keys_all, values_all, valid_rows))

def reference(latent, condition, text_states, valid_rows, text_lengths, w_in, b_in, w_conv, b_conv, w_out, b_out, w_query, w_key, w_value, w_attn_out, b_attn_out, w_cross_query, w_cross_key, w_cross_value, w_cross_out, b_cross_out, w_ff_in, b_ff_in, w_ff_out, b_ff_out, cotangent):
    head_size = C // HEADS
    scaling = head_size ** (-0.5)
    cond_float = condition.astype(jnp.float32)
    text_float = text_states.astype(jnp.float32)
    query_w = w_query.astype(jnp.float32)
    key_w = w_key.astype(jnp.float32)
    value_w = w_value.astype(jnp.float32)
    attn_w = w_attn_out.astype(jnp.float32)
    cross_qw = w_cross_query.astype(jnp.float32)
    cross_ow = w_cross_out.astype(jnp.float32)
    ff_in_w = w_ff_in.astype(jnp.float32)
    ff_out_w = w_ff_out.astype(jnp.float32)
    text_keys = low(matmul(text_float, w_cross_key.astype(jnp.float32))).reshape(ITEMS, TEXT_LEN, HEADS, head_size)
    text_values = low(matmul(text_float, w_cross_value.astype(jnp.float32))).reshape(ITEMS, TEXT_LEN, HEADS, head_size)
    text_keep = jnp.arange(TEXT_LEN)[None, :] < text_lengths[:, None]

    def in_heads(values):
        return low(low_back(values)).reshape(ITEMS, H * W, HEADS, head_size)

    def forward(latent_float, weight_in, bias_in, weight_conv, bias_conv, weight_out, bias_out):
        start = low(low_back(matmul(cond_float, weight_in) + bias_in))
        inner = low_back(conv_three(start, weight_conv) + bias_conv)
        smooth = low(jax.nn.silu(inner))
        mixed = latent_float + (start + low_back(matmul(smooth, weight_out)) + bias_out)
        tokens = mixed.reshape(ITEMS, H * W, C)
        normed = low(normalize(tokens))
        queries = in_heads(matmul(normed, query_w))
        keys_all = in_heads(matmul(normed, key_w))
        values_all = in_heads(matmul(normed, value_w))
        attended = self_attention(queries, keys_all, values_all, valid_rows).reshape(ITEMS, H * W, C)
        attended = low(low_back(attended))
        first = tokens + low_back(matmul(attended, attn_w)) + b_attn_out
        normed_two = low(normalize(first))
        cross_q = in_heads(matmul(normed_two, cross_qw))
        cross_scores = low_back(scaling * jnp.einsum('bqhd,bkhd->bhqk', cross_q, text_keys, precision=precise))
        cross_scores = jnp.where(text_keep[:, None, None, :], cross_scores, masked_score)
        cross_probs = jax.nn.softmax(cross_scores, axis=-1)
        cross_out = jnp.einsum('bhqk,bkhd->bqhd', low(cross_probs), text_values, precision=precise).reshape(ITEMS, H * W, C)
        cross_out = low(low_back(cross_out))
        second = first + low_back(matmul(cross_out, cross_ow)) + b_cross_out
        normed_three = low(normalize(second))
        gate_up = low_back(matmul(normed_three, ff_in_w) + b_ff_in)
        activated = low(gate_up[..., :FF] * jax.nn.gelu(gate_up[..., FF:], approximate=False))
        result = second + low_back(matmul(activated, ff_out_w)) + b_ff_out
        return result.reshape(ITEMS, H, W, C)
    output, pull = jax.vjp(forward, latent.astype(jnp.float32), w_in.astype(jnp.float32), b_in, w_conv.astype(jnp.float32), b_conv, w_out.astype(jnp.float32), b_out)
    grads = pull(cotangent.astype(jnp.float32))
    return (output.astype(jnp.bfloat16), grads[0], grads[1], grads[2], grads[3], grads[4], grads[5], grads[6])
```

```python
import jax
import jax.numpy as jnp
from jax import lax
from jax.experimental import pallas as pl
from jax.experimental.pallas import tpu as pltpu
from jax.sharding import Mesh
from jax.sharding import PartitionSpec as P

ITEMS, ROWS, COLS, C, CIN, HEADS, HEAD, FF = 8, 4, 8, 320, 192, 8, 40, 1280
CELLS = ITEMS * ROWS * COLS
PART = ROWS * COLS
CHIPS = 64
HALF = CHIPS * PART
TEXT = 80
LANES = 128
WIDE = 256
SCALE = HEAD**-0.5
LOG2E = 1.4426950408889634
EPS = 1e-5
MASKED = -1e30
KEY, VALUE, MASK = HEAD, 2 * HEAD, 3 * HEAD
ACROSS = ("sp", "x")
SUM_ROWS = 4096

bf16, f32 = jnp.bfloat16, jnp.float32
NT = (((1,), (1,)), ((), ()))


def dot(left, right):
    return jnp.dot(left, right, preferred_element_type=f32)


def dot_nt(left, right):
    return lax.dot_general(left, right, NT, preferred_element_type=f32)


def lane_of(shape):
    return lax.broadcasted_iota(jnp.int32, shape, len(shape) - 1)


def moments(values):
    center = values - jnp.mean(values, -1, keepdims=True)
    rate = lax.rsqrt(jnp.mean(center * center, -1, keepdims=True) + EPS)
    return center * rate, rate


def norm_back(unit, rate, grads):
    return rate * (
        grads
        - jnp.mean(grads, -1, keepdims=True)
        - unit * jnp.mean(grads * unit, -1, keepdims=True)
    )


def call(kernel, outs, ins, name, scalars=0, scratch=(), vmem=48):
    return pl.pallas_call(
        kernel,
        out_shape=outs,
        in_specs=[
            pl.BlockSpec(memory_space=pltpu.SMEM if i < scalars else pltpu.VMEM)
            for i in range(len(ins))
        ],
        scratch_shapes=list(scratch),
        compiler_params=pltpu.CompilerParams(vmem_limit_bytes=vmem << 20),
        name=name,
    )(*ins)


def out(*shape, dtype=bf16):
    return jax.ShapeDtypeStruct(shape, dtype)


def adapter_kernel(
    place, valid, center, top, bottom, left, right, latent, w_in, w_conv, b_conv, w_out, b_out,
    w_qkv, rows_out, mixed_out, smooth_out, slope_out, cond_out,
):
    span = ITEMS * (ROWS + 2)
    block = jnp.concatenate(
        [top[...].astype(f32), center[...].astype(f32), bottom[...].astype(f32)], axis=1
    ).reshape(span, COLS, WIDE)
    col = lax.broadcasted_iota(jnp.int32, (span, COLS, WIDE), 1)
    near = jnp.where(
        col == 0, left[...].astype(f32).reshape(span, 1, WIDE), pltpu.roll(block, 1, 1)
    )
    far = jnp.where(
        col == COLS - 1,
        right[...].astype(f32).reshape(span, 1, WIDE),
        pltpu.roll(block, COLS - 1, 1),
    )
    inner = jnp.zeros((CELLS, C), f32)
    start_here = None
    for j, moved in enumerate((near, block, far)):
        start = dot(moved.reshape(span * COLS, WIDE).astype(bf16), w_in[...])
        start = start.reshape(ITEMS, ROWS + 2, COLS, C)
        moved = moved.reshape(ITEMS, ROWS + 2, COLS, WIDE)
        for i in range(3):
            patch = start[:, i : i + ROWS].reshape(CELLS, C).astype(bf16)
            if i == 1 and j == 1:
                start_here = patch.astype(f32)
            inner += dot(patch, w_conv[3 * i + j])
            cond_out[3 * i + j] = moved[:, i : i + ROWS].reshape(CELLS, WIDE).astype(bf16)
    inner += b_conv[...]
    gate = jax.nn.sigmoid(inner)
    smooth = (inner * gate).astype(bf16)
    smooth_out[...] = smooth
    slope_out[...] = gate * (1.0 + inner * (1.0 - gate))
    mixed = latent[...].astype(f32) + (start_here + dot(smooth, w_out[...]) + b_out[...])
    mixed_out[...] = mixed
    normed = moments(mixed)[0].astype(bf16)
    rows = dot(normed, w_qkv[...])
    lane = lane_of((PART, LANES))
    row = lax.broadcasted_iota(jnp.int32, (PART, LANES), 0) // COLS + ROWS * place[0]
    for item in range(ITEMS):
        hidden = jnp.where(row >= valid[item], MASKED, 0.0)
        extra = jnp.where(lane == MASK, hidden, jnp.where(lane > MASK, 1.0, 0.0))
        for head in range(HEADS):
            piece = rows[item * PART : (item + 1) * PART, head * LANES : (head + 1) * LANES]
            rows_out[item, head] = (piece + extra).astype(bf16)


def attend_kernel(own, other, packed_out, query_out, full_out, scores):
    block, step = scores.shape[0], 512
    chunks = [(ref, at) for ref in (own, other) for at in range(0, HALF, step)]

    def body(b, carry):
        rows = pl.ds(pl.multiple_of(b * block, block), block)
        lane = lane_of((block, LANES))
        query = pltpu.roll(own[rows, :].astype(f32), KEY, 1)
        query = jnp.where(
            (lane >= KEY) & (lane < VALUE), query, jnp.where(lane == MASK, 1.0, 0.0)
        )
        query_low = query.astype(bf16)
        peak = None
        for n, (ref, at) in enumerate(chunks):
            part = dot_nt(query_low, ref[at : at + step, :])
            scores[:, n * step : (n + 1) * step] = part
            for t in range(0, step, LANES):
                piece = part[:, t : t + LANES]
                peak = piece if peak is None else jnp.maximum(peak, piece)
        peak = jnp.max(peak, axis=1, keepdims=True)
        shift = peak * (SCALE * LOG2E)
        total = jnp.zeros((block, LANES), f32)
        for n, (ref, at) in enumerate(chunks):
            part = scores[:, n * step : (n + 1) * step]
            probs = jnp.exp2(part * (SCALE * LOG2E) - shift).astype(bf16)
            total += dot(probs, ref[at : at + step, :])
        mass = jnp.sum(jnp.where(lane == MASK + 1, total, 0.0), axis=1, keepdims=True)
        total = total / mass
        logsum = peak + jnp.log(mass) * (1.0 / SCALE)
        first = logsum.astype(bf16).astype(f32)
        second = (logsum - first).astype(bf16).astype(f32)
        third = logsum - first - second
        for n, piece in enumerate((first, second, third)):
            query = jnp.where(lane == MASK + 1 + n, -piece, query)
        query_out[rows, :] = query.astype(bf16)
        full_out[rows, :] = total
        pairs = total.reshape(block // PART, 2, PART // 2, LANES)
        lane = lane_of((block // 2, LANES))
        low = pltpu.roll(pairs[:, 0].reshape(block // 2, LANES), LANES - VALUE, 1)
        high = pltpu.roll(pairs[:, 1].reshape(block // 2, LANES), LANES - VALUE + HEAD, 1)
        packed = jnp.where(lane < HEAD, low, jnp.where(lane < 2 * HEAD, high, 0.0))
        packed = packed.astype(bf16).reshape(block // PART, PART // 2, LANES)
        packed_out[pl.ds(b * (block // PART), block // PART)] = packed
        return carry

    lax.fori_loop(0, HALF // block, body, 0)


def middle_kernel(
    lengths, heads_in, mixed, cotangent, text_keys, text_values, w_attn, b_attn, w_cross_query,
    w_cross_out, b_cross, w_ff_in, b_ff_in, w_ff_out, b_ff_out, result_out, grad_out, heads_out,
    probs_keep,
):
    half = CELLS // 2
    split = w_attn.shape[1] // 2
    packed = jnp.concatenate(
        [heads_in[:, head].reshape(half, LANES) for head in range(HEADS)], axis=1
    )
    both = dot(packed, w_attn[...])
    shape = (ITEMS, 1, PART // 2, C)
    attended = jnp.concatenate(
        [both[:, :C].reshape(shape), both[:, split : split + C].reshape(shape)], axis=1
    ).reshape(CELLS, C)
    first = mixed[...] + attended + b_attn[...]
    unit_two, rate_two = moments(first)
    cross_query = dot(unit_two.astype(bf16), w_cross_query[...]).astype(bf16)
    lane = lane_of((PART, C))
    in_head = [(lane >= HEAD * h) & (lane < HEAD * (h + 1)) for h in range(HEADS)]

    def spread(values):
        return jnp.concatenate(
            [jnp.where(mask, values, jnp.zeros_like(values)) for mask in in_head], axis=0
        )

    def gather(values):
        total = jnp.zeros((PART, C), f32)
        for h, mask in enumerate(in_head):
            total = jnp.where(mask, values[h * PART : (h + 1) * PART], total)
        return total

    token = lane_of((HEADS * PART, TEXT))
    outs = []
    for item in range(ITEMS):
        cells = slice(item * PART, (item + 1) * PART)
        scores = dot_nt(spread(cross_query[cells]), text_keys[item]) * SCALE
        scores = jnp.where(token < lengths[item], scores, MASKED)
        weights = jnp.exp(scores - jnp.max(scores, -1, keepdims=True))
        probs = weights / jnp.sum(weights, -1, keepdims=True)
        probs_keep[item] = probs
        outs.append(gather(dot(probs.astype(bf16), text_values[item])))
    cross = jnp.concatenate(outs, axis=0).astype(bf16)
    second = first + dot(cross, w_cross_out[...]) + b_cross[...]
    unit_three, rate_three = moments(second)
    normed_three = unit_three.astype(bf16)
    upstream = cotangent[...]
    result = second + b_ff_out[...]
    grad_normed = jnp.zeros((CELLS, C), f32)
    step = 256
    for at in range(0, FF, step):
        values, gates = slice(at, at + step), slice(FF + at, FF + at + step)
        value = dot(normed_three, w_ff_in[:, values]) + b_ff_in[:, values]
        gate = dot(normed_three, w_ff_in[:, gates]) + b_ff_in[:, gates]
        normal = 0.5 + 0.5 * lax.erf(gate * (0.5**0.5))
        density = jnp.exp(gate * gate * -0.5) * 0.3989422804014327
        gelu = gate * normal
        result += dot((value * gelu).astype(bf16), w_ff_out[values, :])
        grad_act = dot_nt(upstream, w_ff_out[values, :])
        grad_value = (grad_act * gelu).astype(bf16)
        grad_gate = (grad_act * value * (normal + gate * density)).astype(bf16)
        grad_normed += dot_nt(grad_value, w_ff_in[:, values])
        grad_normed += dot_nt(grad_gate, w_ff_in[:, gates])
    result_out[...] = result.astype(bf16)
    grad_second = upstream.astype(f32) + norm_back(unit_three, rate_three, grad_normed)
    grad_cross = dot_nt(grad_second.astype(bf16), w_cross_out[...]).astype(bf16)
    outs = []
    for item in range(ITEMS):
        cells = slice(item * PART, (item + 1) * PART)
        grad_probs = dot_nt(spread(grad_cross[cells]), text_values[item])
        probs = probs_keep[item]
        weighted = jnp.sum(probs * grad_probs, -1, keepdims=True)
        grad_scores = (probs * (grad_probs - weighted)).astype(bf16)
        outs.append(gather(dot(grad_scores, text_keys[item])))
    grad_query = (jnp.concatenate(outs, axis=0) * SCALE).astype(bf16)
    grad_first = grad_second + norm_back(
        unit_two, rate_two, dot_nt(grad_query, w_cross_query[...])
    )
    grad_out[...] = grad_first
    pairs = grad_first.reshape(ITEMS, 2, PART // 2, C)
    gap = jnp.zeros((half, split - C), f32)
    both = jnp.concatenate(
        [pairs[:, 0].reshape(half, C), gap, pairs[:, 1].reshape(half, C), gap], axis=1
    ).astype(bf16)
    packed = dot_nt(both, w_attn[...]).astype(bf16)
    for head in range(HEADS):
        piece = packed[:, head * LANES : (head + 1) * LANES]
        heads_out[:, head] = piece.reshape(ITEMS, PART // 2, LANES)


def attend_back_kernel(own, other, query, full, packed, own_out, other_out, grads, turned, sums):
    block, step = 512, 512
    half = HALF // 2
    lane = lane_of((half, LANES))
    value_lane = (lane >= VALUE) & (lane < MASK)
    pairs = packed[...].reshape(half, LANES).astype(f32)
    low = jnp.where(value_lane, pltpu.roll(pairs, VALUE, 1), 0.0)
    high = jnp.where(value_lane, pltpu.roll(pairs, VALUE - HEAD, 1), 0.0)
    shape = (CHIPS, 1, PART // 2, LANES)
    upstream = jnp.concatenate([low.reshape(shape), high.reshape(shape)], axis=1)
    upstream = upstream.reshape(HALF, LANES)
    lane = lane_of((HALF, LANES))
    weighted = jnp.sum(upstream * full[...], axis=1, keepdims=True)
    first = weighted.astype(bf16).astype(f32)
    upstream = jnp.where(lane == MASK + 4, -first, upstream)
    upstream = jnp.where(lane == MASK + 5, first - weighted, upstream)
    grads[...] = upstream.astype(bf16)
    turned[:, :HALF] = jnp.transpose(own[...])
    turned[:, HALF:] = jnp.transpose(other[...])
    sums[...] = jnp.zeros_like(sums)
    chunks = [(ref, at) for ref in (own, other) for at in range(0, HALF, step)]

    def body(b, carry):
        rows = pl.ds(pl.multiple_of(b * block, block), block)
        queries, upstream = query[rows, :], grads[rows, :]
        right = jnp.concatenate([queries, upstream], axis=0)
        grad_query = jnp.zeros((LANES, block), f32)
        for n, (ref, at) in enumerate(chunks):
            keys = ref[at : at + step, :]
            probs = jnp.exp2(dot_nt(keys, queries) * (SCALE * LOG2E))
            grad_scores = (probs * dot_nt(keys, upstream)).astype(bf16)
            both = jnp.concatenate([grad_scores, probs.astype(bf16)], axis=1)
            sums[n * step : (n + 1) * step, :] += dot(both, right)
            grad_query += dot(turned[:, n * step : (n + 1) * step], grad_scores)
        grad_query = jnp.transpose(grad_query) * SCALE
        own_out[rows, :] = pltpu.roll(grad_query, LANES - KEY, 1)
        return carry

    lax.fori_loop(0, HALF // block, body, 0)
    scale = jnp.where(lane < VALUE, SCALE, 1.0)
    rest = jnp.where(lane < MASK, sums[:HALF, :] * scale, 0.0)
    own_out[...] = jnp.where(lane < KEY, own_out[...], rest)
    rest = jnp.where((lane >= KEY) & (lane < MASK), sums[HALF:, :] * scale, 0.0)
    other_out[...] = rest.astype(bf16)


def finish_kernel(
    place, rows, w_qkv, mixed, grad_first, slope, smooth, cond, w_out, latent_out, parts_out
):
    joined = jnp.concatenate(
        [rows[:, head].reshape(CELLS, LANES) for head in range(HEADS)], axis=1
    )
    unit, rate = moments(mixed[...])
    latent = grad_first[...] + norm_back(unit, rate, dot_nt(joined, w_qkv[...]))
    latent_out[...] = latent
    branch = latent.astype(bf16)
    inner = (dot_nt(branch, w_out[...]) * slope[...]).astype(bf16)
    inner_turned = jnp.transpose(inner)
    branch_turned = jnp.transpose(branch)
    here, there = place[1], 1 - place[1]

    def put(side, at, values):
        values = values.astype(bf16)
        for t in range(0, values.shape[1], LANES):
            parts_out[side, at : at + C, :] = values[:, t : t + LANES]
            at += C
        return at

    at = 0
    for n in range(6):
        at = put(here, at, dot(inner_turned, cond[n]))
    parts_out[here, at:, :] = jnp.zeros((SUM_ROWS - at, LANES), bf16)
    at = 0
    for n in range(6, 9):
        at = put(there, at, dot(inner_turned, cond[n]))
    at = put(there, at, dot(branch_turned, cond[4]))
    last = jnp.concatenate([smooth[...], jnp.zeros((CELLS, 384 - C), bf16)], axis=1)
    at = put(there, at, dot(branch_turned, last))
    parts_out[there, at:, :] = jnp.zeros((SUM_ROWS - at, LANES), bf16)


def weights_kernel(
    place, mine, theirs, w_in, w_conv, win_out, bin_out, wconv_out, bconv_out, wout_out, bout_out,
    total,
):
    here = place[1]
    total[here] = mine[...]
    total[1 - here] = theirs[...]

    def take(side, at, count):
        return jnp.concatenate(
            [total[side, at + C * t : at + C * (t + 1), :] for t in range(count)], axis=1
        )

    grad_in = jnp.zeros((C, WIDE), f32)
    for n in range(9):
        moment = take(n // 6, 2 * C * (n % 6), 2)
        wconv_out[n] = dot_nt(w_in[...], moment)
        grad_in += dot(w_conv[n], moment)
        if n == 4:
            bconv_out[...] = jnp.transpose(moment.astype(f32))[CIN : CIN + 1, :]
    moment = jnp.transpose(take(1, 6 * C, 2).astype(f32))
    grad_in = jnp.transpose(grad_in) + moment
    win_out[...] = grad_in[:CIN]
    bin_out[...] = grad_in[CIN : CIN + 1]
    bout_out[...] = moment[CIN : CIN + 1]
    wout_out[...] = jnp.transpose(take(1, 8 * C, 3).astype(f32))[:C]


def swap(array):
    return lax.ppermute(array, "c", [(0, 1), (1, 0)])


def across(blocks):
    return lax.all_to_all(blocks, ACROSS, 0, 0, tiled=True)


def pieces(values, count):
    kept = []
    for _ in range(count):
        piece = values.astype(bf16)
        kept.append(piece)
        values = values - piece.astype(f32)
    return kept


def per_device(
    latent, condition, text_states, valid_rows, text_lengths, w_in, b_in, w_conv, b_conv, w_out,
    b_out, w_query, w_key, w_value, w_attn_out, b_attn_out, w_cross_query, w_cross_key,
    w_cross_value, w_cross_out, b_cross_out, w_ff_in, b_ff_in, w_ff_out, b_ff_out, cotangent,
):
    place = jnp.stack([lax.axis_index("sp"), lax.axis_index("c")]).astype(jnp.int32)

    ones = jnp.ones(condition.shape[:3] + (3,), bf16)
    center = jnp.pad(
        jnp.concatenate([condition, ones], axis=-1), ((0, 0),) * 3 + ((0, WIDE - CIN - 3),)
    )
    down = [(i, i + 1) for i in range(15)]
    top = lax.ppermute(center[:, ROWS - 1 :], "sp", down)
    bottom = lax.ppermute(center[:, :1], "sp", [(b, a) for a, b in down])
    tall = jnp.concatenate([top, center, bottom], axis=1)
    right_way = [(i, i + 1) for i in range(7)]
    span = ITEMS * (ROWS + 2)
    left = lax.ppermute(tall[:, :, COLS - 1].reshape(span, WIDE), ("x", "c"), right_way)
    right = lax.ppermute(
        tall[:, :, 0].reshape(span, WIDE), ("x", "c"), [(b, a) for a, b in right_way]
    )

    w_in_wide = jnp.concatenate(
        [w_in] + [piece[None] for piece in pieces(b_in, 3)], axis=0
    )
    w_in_wide = jnp.pad(w_in_wide, ((0, WIDE - CIN - 3), (0, 0)))
    w_qkv = jnp.concatenate(
        [w.reshape(C, HEADS, HEAD) for w in (w_query, w_key, w_value)], axis=-1
    )
    w_qkv = jnp.pad(w_qkv, ((0, 0), (0, 0), (0, LANES - 3 * HEAD))).reshape(C, HEADS * LANES)
    by_head = w_attn_out.reshape(HEADS, HEAD, C)
    w_attn = jnp.concatenate(
        [
            jnp.pad(by_head, ((0, 0), (at, LANES - HEAD - at), (0, 384 - C)))
            for at in (0, HEAD)
        ],
        axis=-1,
    ).reshape(HEADS * LANES, 768)
    text = jnp.pad(text_states, ((0, 0), (0, TEXT - text_states.shape[1]), (0, 0)))
    text_keys = jnp.einsum("btc,cd->btd", text, w_cross_key, preferred_element_type=f32)
    text_values = jnp.einsum("btc,cd->btd", text, w_cross_value, preferred_element_type=f32)
    text_keys, text_values = text_keys.astype(bf16), text_values.astype(bf16)
    taps = w_conv.reshape(9, C, C)

    rows, mixed, smooth, slope, cond = call(
        adapter_kernel,
        (
            out(ITEMS, HEADS, PART, LANES),
            out(CELLS, C, dtype=f32),
            out(CELLS, C),
            out(CELLS, C, dtype=f32),
            out(9, CELLS, WIDE),
        ),
        (
            place, valid_rows, center, top, bottom, left, right, latent.reshape(CELLS, C),
            w_in_wide, taps, b_conv[None], w_out, b_out[None], w_qkv,
        ),
        "adapter",
        scalars=2,
    )

    own = across(rows.reshape(CHIPS, PART, LANES)).reshape(HALF, LANES)
    other = swap(own)
    packed, query, full = call(
        attend_kernel,
        (out(CHIPS, PART // 2, LANES), out(HALF, LANES), out(HALF, LANES, dtype=f32)),
        (own, other),
        "attend",
        scratch=[pltpu.VMEM((256, 2 * HALF), f32)],
    )
    heads_in = across(packed).reshape(ITEMS, HEADS, PART // 2, LANES)

    result, grad_first, heads_out = call(
        middle_kernel,
        (out(CELLS, C), out(CELLS, C, dtype=f32), out(ITEMS, HEADS, PART // 2, LANES)),
        (
            text_lengths, heads_in, mixed, cotangent.reshape(CELLS, C), text_keys, text_values,
            w_attn, b_attn_out[None], w_cross_query, w_cross_out, b_cross_out[None], w_ff_in,
            b_ff_in[None], w_ff_out, b_ff_out[None],
        ),
        "middle",
        scalars=1,
        scratch=[pltpu.VMEM((ITEMS, HEADS * PART, TEXT), f32)],
    )

    grads_in = across(heads_out.reshape(CHIPS, PART // 2, LANES))
    own_grads, other_grads = call(
        attend_back_kernel,
        (out(HALF, LANES, dtype=f32), out(HALF, LANES)),
        (own, other, query, full, grads_in),
        "attend_back",
        scratch=[
            pltpu.VMEM((HALF, LANES), bf16),
            pltpu.VMEM((LANES, 2 * HALF), bf16),
            pltpu.VMEM((2 * HALF, LANES), f32),
        ],
    )
    row_grads = (own_grads + swap(other_grads).astype(f32)).astype(bf16)
    row_grads = across(row_grads.reshape(CHIPS, PART, LANES))

    latent_grad, parts = call(
        finish_kernel,
        (out(CELLS, C, dtype=f32), out(2, SUM_ROWS, LANES)),
        (
            place, row_grads.reshape(ITEMS, HEADS, PART, LANES), w_qkv, mixed, grad_first, slope,
            smooth, cond, w_out,
        ),
        "finish",
        scalars=1,
    )

    shares = (parts[0].astype(f32) + swap(parts[1]).astype(f32)).astype(bf16)
    shares = across(shares.reshape(CHIPS, SUM_ROWS // CHIPS, LANES))
    share = jnp.sum(shares.astype(f32), axis=0).astype(bf16)
    mine = across(jnp.broadcast_to(share[None], shares.shape)).reshape(SUM_ROWS, LANES)
    theirs = swap(mine)
    grad_w_in, grad_b_in, grad_w_conv, grad_b_conv, grad_w_out, grad_b_out = call(
        weights_kernel,
        (
            out(CIN, C, dtype=f32),
            out(1, C, dtype=f32),
            out(9, C, C, dtype=f32),
            out(1, C, dtype=f32),
            out(C, C, dtype=f32),
            out(1, C, dtype=f32),
        ),
        (place, mine, theirs, w_in_wide.T, taps),
        "weights",
        scalars=1,
        scratch=[pltpu.VMEM((2, SUM_ROWS, LANES), bf16)],
    )
    grid = (ITEMS, ROWS, COLS, C)
    return (
        result.reshape(grid),
        latent_grad.reshape(grid),
        grad_w_in,
        grad_b_in[0],
        grad_w_conv.reshape(3, 3, C, C),
        grad_b_conv[0],
        grad_w_out,
        grad_b_out[0],
    )


def solution(mesh):
    split = Mesh(mesh.devices.reshape(16, 4, 2), ("sp", "x", "c"))
    cells = P(None, "sp", ("x", "c"), None)
    in_specs = (cells, cells) + (P(),) * 23 + (cells,)
    out_specs = (cells, cells) + (P(),) * 6
    return jax.shard_map(
        per_device, mesh=split, in_specs=in_specs, out_specs=out_specs, check_vma=False
    )
```

```python
import jax
import jax.numpy as jnp
from jax import lax
from jax.experimental import pallas as pl
from jax.experimental.pallas import tpu as pltpu
from jax.sharding import Mesh
from jax.sharding import PartitionSpec as P

ITEMS, ROWS, COLS, C, CIN, HEADS, HEAD, FF = 8, 4, 8, 320, 192, 8, 40, 1280
CELLS = ITEMS * ROWS * COLS
PART = ROWS * COLS
CHIPS = 64
HALF = CHIPS * PART
TEXT = 80
LANES = 128
WIDE = 256
SCALE = HEAD**-0.5
LOG2E = 1.4426950408889634
EPS = 1e-5
MASKED = -1e30
KEY, VALUE, MASK = HEAD, 2 * HEAD, 3 * HEAD
ACROSS = ("sp", "x")
SUM_ROWS = 3072

bf16, f32 = jnp.bfloat16, jnp.float32
NT = (((1,), (1,)), ((), ()))


def dot(left, right):
    return jnp.dot(left, right, preferred_element_type=f32)


def dot_nt(left, right):
    return lax.dot_general(left, right, NT, preferred_element_type=f32)


def lane_of(shape):
    return lax.broadcasted_iota(jnp.int32, shape, len(shape) - 1)


def moments(values):
    center = values - jnp.mean(values, -1, keepdims=True)
    rate = lax.rsqrt(jnp.mean(center * center, -1, keepdims=True) + EPS)
    return center * rate, rate


def norm_back(unit, rate, grads):
    return rate * (
        grads
        - jnp.mean(grads, -1, keepdims=True)
        - unit * jnp.mean(grads * unit, -1, keepdims=True)
    )


class Fetched:
    def __init__(self, source, buffer, semaphore):
        self.copy = pltpu.make_async_copy(source, buffer, semaphore)
        self.buffer, self.shape, self.here = buffer, buffer.shape, False
        self.copy.start()

    def __getitem__(self, index):
        if not self.here:
            self.copy.wait()
            self.here = True
        return self.buffer[index]


class Stored:
    def __init__(self, target, buffer, semaphore):
        self.copy = pltpu.make_async_copy(buffer, target, semaphore)
        self.buffer, self.started = buffer, False

    def __setitem__(self, index, values):
        self.buffer[index] = values
        if index is Ellipsis:
            self.start()

    def start(self):
        if not self.started:
            self.copy.start()
            self.started = True


def call(kernel, outs, ins, name, scalars=0, scratch=(), vmem=16, fetch=(), store=(), far=()):
    fetch, store = list(fetch), list(store)
    far_in = [i for i in far if i < len(ins)]
    far_out = [i - len(ins) for i in far if i >= len(ins)]

    def body(*refs):
        refs = list(refs)
        given, refs = refs[: len(ins)], refs[len(ins) :]
        made, refs = refs[: len(outs)], refs[len(outs) :]
        own, refs = refs[: len(scratch)], refs[len(scratch) :]
        buffers, semaphores = refs[:-1], refs[-1] if refs else None
        for n, i in enumerate(fetch):
            given[i] = Fetched(given[i], buffers[n], semaphores.at[n])
        kept = []
        for n, i in enumerate(store, len(fetch)):
            made[i] = Stored(made[i], buffers[n], semaphores.at[n])
            kept.append(made[i])
        kernel(*given, *made, *own)
        for part in given:
            if isinstance(part, Fetched) and not part.here:
                part.copy.wait()
        for part in kept:
            part.start()
        for part in kept:
            part.copy.wait()

    def in_spec(i):
        if i < scalars:
            return pl.BlockSpec(memory_space=pltpu.SMEM)
        space = pltpu.HBM if i in fetch or i in far_in else pltpu.VMEM
        return pl.BlockSpec(memory_space=space)

    def out_spec(i):
        space = pltpu.HBM if i in store or i in far_out else pltpu.VMEM
        return pl.BlockSpec(memory_space=space)

    extra = [pltpu.VMEM(ins[i].shape, ins[i].dtype) for i in fetch]
    extra += [pltpu.VMEM(outs[i].shape, outs[i].dtype) for i in store]
    if extra:
        extra.append(pltpu.SemaphoreType.DMA((len(extra),)))
    return pl.pallas_call(
        body,
        out_shape=tuple(
            pltpu.HBM(made.shape, made.dtype) if i in store or i in far_out else made
            for i, made in enumerate(outs)
        ),
        in_specs=[in_spec(i) for i in range(len(ins))],
        out_specs=tuple(out_spec(i) for i in range(len(outs))),
        scratch_shapes=list(scratch) + extra,
        compiler_params=pltpu.CompilerParams(vmem_limit_bytes=vmem << 20),
        name=name,
    )(
        *(
            pltpu.with_memory_space_constraint(x, pltpu.HBM) if i in fetch or i in far_in else x
            for i, x in enumerate(ins)
        )
    )


def out(*shape, dtype=bf16):
    return jax.ShapeDtypeStruct(shape, dtype)


def bias_rows(bias):
    row = lax.broadcasted_iota(jnp.int32, (WIDE - CIN, C), 0)
    rest = jnp.broadcast_to(bias, (WIDE - CIN, C))
    rows = jnp.zeros((WIDE - CIN, C), f32)
    for n in range(3):
        piece = rest.astype(bf16).astype(f32)
        rows = jnp.where(row == n, piece, rows)
        rest = rest - piece
    return rows.astype(bf16)


def adapter_kernel(
    place, valid, center, top, bottom, left, right, latent, w_in, b_in, w_conv, b_conv, w_out,
    b_out, w_query, w_key, w_value, rows_out, mixed_out, smooth_out, slope_out, cond_out,
    w_wide,
):
    span = ITEMS * (ROWS + 2)
    w_wide[:CIN, :] = w_in[...]
    w_wide[CIN:, :] = bias_rows(b_in[...])

    def widen(values):
        blank = jnp.zeros(values.shape[:-1] + (WIDE - CIN,), f32)
        return jnp.concatenate([values.astype(f32), blank], axis=-1)

    block = jnp.concatenate([top[...], center[...], bottom[...]], axis=1)
    block = widen(block.reshape(span, COLS, CIN))
    shape = (ITEMS, ROWS + 2, COLS, WIDE)
    row = lax.broadcasted_iota(jnp.int32, shape, 1) + ROWS * place[0] - 1
    inside = (row >= 0) & (row < ROWS * 16)
    inside = jnp.where(inside, 1.0, 0.0).reshape(span, COLS, WIDE)
    lane = lane_of((span, COLS, WIDE))
    col = lax.broadcasted_iota(jnp.int32, (span, COLS, WIDE), 1)
    at = COLS * place[2]
    edges = []
    for n, side in enumerate((left, right)):
        there = (at > 0) if n == 0 else (at < COLS * 7)
        edges.append((widen(side[...]).reshape(span, 1, WIDE), jnp.where(there, inside, 0.0)))
    near = jnp.where(col == 0, edges[0][0], pltpu.roll(block, 1, 1))
    near_inside = jnp.where(col == 0, edges[0][1], inside)
    far = jnp.where(col == COLS - 1, edges[1][0], pltpu.roll(block, COLS - 1, 1))
    far_inside = jnp.where(col == COLS - 1, edges[1][1], inside)
    inner = jnp.zeros((CELLS, C), f32)
    start_here = None
    one = (lane >= CIN) & (lane < CIN + 3)
    moves = ((near, near_inside), (block, inside), (far, far_inside))
    for j, (moved, present) in enumerate(moves):
        moved = jnp.where(one, present, moved)
        start = dot(moved.reshape(span * COLS, WIDE).astype(bf16), w_wide[...])
        start = start.reshape(ITEMS, ROWS + 2, COLS, C)
        moved = moved.reshape(ITEMS, ROWS + 2, COLS, WIDE)
        for i in range(3):
            patch = start[:, i : i + ROWS].reshape(CELLS, C).astype(bf16)
            if i == 1 and j == 1:
                start_here = patch.astype(f32)
            inner += dot(patch, w_conv[3 * i + j])
            cond_out[3 * i + j] = moved[:, i : i + ROWS].reshape(CELLS, WIDE).astype(bf16)
    inner += b_conv[...]
    gate = jax.nn.sigmoid(inner)
    smooth = (inner * gate).astype(bf16)
    smooth_out[...] = smooth
    slope_out[...] = gate * (1.0 + inner * (1.0 - gate))
    mixed = latent[...].astype(f32) + (start_here + dot(smooth, w_out[...]) + b_out[...])
    mixed_out[...] = mixed
    normed = moments(mixed)[0].astype(bf16)
    projected = [dot(normed, w[...]) for w in (w_query, w_key, w_value)]
    lane = lane_of((PART, LANES - MASK))
    row = lax.broadcasted_iota(jnp.int32, (PART, LANES - MASK), 0) // COLS + ROWS * place[0]
    extras = []
    for item in range(ITEMS):
        hidden = jnp.where(row >= valid[item], MASKED, 0.0)
        extras.append(jnp.where(lane == 0, hidden, 1.0))
    extras = jnp.concatenate(extras, axis=0)
    for head in range(HEADS):
        at = slice(head * HEAD, (head + 1) * HEAD)
        joined = jnp.concatenate([part[:, at] for part in projected] + [extras], axis=1)
        rows_out[:, head] = joined.astype(bf16).reshape(ITEMS, PART, LANES)


def text_kernel(text, w_key_turned, w_value_turned, keys_out, values_out):
    count = text.shape[0]
    token = lax.broadcasted_iota(jnp.int32, (TEXT, count), 0)
    place = lane_of((TEXT, count))
    for item in range(ITEMS):
        pick = jnp.where(place == token * ITEMS + item, 1.0, 0.0).astype(bf16)
        states = dot(pick, text[...]).astype(bf16)
        keys_out[item] = dot_nt(states, w_key_turned[...]).astype(bf16)
        values_out[item] = dot_nt(states, w_value_turned[...]).astype(bf16)


BLOCK = 256
STEP = 512


def attend_kernel(
    own, other, packed_out, full_out, probs_out,
    scores_a, scores_b, probs_a, probs_b, turned_a, turned_b, keys_turned, query, output, sems,
):
    count = HALF // BLOCK
    keys_turned[:, :HALF] = jnp.transpose(own[...])
    keys_turned[:, HALF:] = jnp.transpose(other[...])
    lane = lane_of((HALF, LANES))
    rows = pltpu.roll(own[...].astype(f32), KEY, 1)
    rows = jnp.where((lane >= KEY) & (lane < VALUE), rows, jnp.where(lane == MASK, 1.0, 0.0))
    query[...] = jnp.transpose(rows.astype(bf16))
    chunks = [(ref, at) for ref in (own, other) for at in range(0, HALF, STEP)]

    def columns(b):
        return pl.ds(pl.multiple_of(b * BLOCK, BLOCK), BLOCK)

    def score(queries, n, scores, peak):
        ref, at = chunks[n]
        part = dot(ref[at : at + STEP, :], queries)
        scores[n * STEP : (n + 1) * STEP, :] = part
        part = jnp.max(part.reshape(STEP // 8, 8, BLOCK), axis=0)
        return part if peak is None else jnp.maximum(peak, part)

    def sent(b, turned, n):
        return pltpu.make_async_copy(turned, probs_out.at[columns(b)], sems.at[n])

    def half(b, peak, following, scores, probs, turned):
        shift = jnp.max(peak, axis=0, keepdims=True) * (SCALE * LOG2E)
        queries = query[:, columns(jnp.minimum(b + 1, count - 1))]
        ahead = None
        for n in range(len(chunks)):
            ahead = score(queries, n, following, ahead)
            keys = slice(n * STEP, (n + 1) * STEP)
            part = jnp.exp2(scores[keys, :] * (SCALE * LOG2E) - shift).astype(bf16)
            probs[keys, :] = part
            turned[:, keys] = jnp.transpose(part)
        output[:, columns(b)] = dot(keys_turned[...], probs[...])
        return ahead

    peak = None
    for n in range(len(chunks)):
        peak = score(query[:, :BLOCK], n, scores_a, peak)

    def body(i, peak):
        @pl.when(i > 0)
        def _():
            sent(2 * i - 2, turned_a, 0).wait()

        peak = half(2 * i, peak, scores_b, scores_a, probs_a, turned_a)
        sent(2 * i, turned_a, 0).start()

        @pl.when(i > 0)
        def _():
            sent(2 * i - 1, turned_b, 1).wait()

        peak = half(2 * i + 1, peak, scores_a, scores_b, probs_b, turned_b)
        sent(2 * i + 1, turned_b, 1).start()
        return peak

    lax.fori_loop(0, count // 2, body, peak)
    total = output[...]
    inverse = 1.0 / total[MASK + 1 : MASK + 2, :]
    row = lax.broadcasted_iota(jnp.int32, (LANES, HALF), 0)
    total = jnp.transpose(jnp.where(row == 0, inverse, total * inverse))
    full_out[...] = total
    pairs = total.reshape(CHIPS, 2, PART // 2, LANES)
    lane = lane_of((HALF // 2, LANES))
    low = pltpu.roll(pairs[:, 0].reshape(HALF // 2, LANES), LANES - VALUE, 1)
    high = pltpu.roll(pairs[:, 1].reshape(HALF // 2, LANES), LANES - VALUE + HEAD, 1)
    packed = jnp.where(lane < HEAD, low, jnp.where(lane < 2 * HEAD, high, 0.0))
    packed_out[...] = packed.astype(bf16).reshape(CHIPS, PART // 2, LANES)
    sent(count - 2, turned_a, 0).wait()
    sent(count - 1, turned_b, 1).wait()


def middle_kernel(
    lengths, heads_in, mixed, cotangent, text_keys, text_values, w_attn, b_attn, w_cross_query,
    w_cross_out, b_cross, w_ff_in, b_ff_in, w_ff_turned, b_ff_out, result_out, grad_out, heads_out,
    probs_keep,
):
    half = CELLS // 2
    split = w_attn.shape[1] // 2
    packed = jnp.concatenate(
        [heads_in[:, head].reshape(half, LANES) for head in range(HEADS)], axis=1
    )
    both = dot(packed, w_attn[...])
    shape = (ITEMS, 1, PART // 2, C)
    attended = jnp.concatenate(
        [both[:, :C].reshape(shape), both[:, split : split + C].reshape(shape)], axis=1
    ).reshape(CELLS, C)
    first = mixed[...] + attended + b_attn[...]
    unit_two, rate_two = moments(first)
    cross_query = dot(unit_two.astype(bf16), w_cross_query[...]).astype(bf16)
    lane = lane_of((PART, C))
    in_head = [(lane >= HEAD * h) & (lane < HEAD * (h + 1)) for h in range(HEADS)]

    def spread(values):
        return jnp.concatenate(
            [jnp.where(mask, values, jnp.zeros_like(values)) for mask in in_head], axis=0
        )

    def gather(values):
        total = jnp.zeros((PART, C), f32)
        for h, mask in enumerate(in_head):
            total = jnp.where(mask, values[h * PART : (h + 1) * PART], total)
        return total

    token = lane_of((HEADS * PART, TEXT))
    outs = []
    for item in range(ITEMS):
        cells = slice(item * PART, (item + 1) * PART)
        scores = dot_nt(spread(cross_query[cells]), text_keys[item]) * SCALE
        scores = jnp.where(token < lengths[item], scores, MASKED)
        weights = jnp.exp(scores - jnp.max(scores, -1, keepdims=True))
        probs = weights / jnp.sum(weights, -1, keepdims=True)
        probs_keep[item] = probs
        outs.append(gather(dot(probs.astype(bf16), text_values[item])))
    cross = jnp.concatenate(outs, axis=0).astype(bf16)
    second = first + dot(cross, w_cross_out[...]) + b_cross[...]
    unit_three, rate_three = moments(second)
    normed_three = unit_three.astype(bf16)
    upstream = cotangent[...]
    result = second + b_ff_out[...]
    grad_normed = jnp.zeros((CELLS, C), f32)
    step = 256
    for at in range(0, FF, step):
        values, gates = slice(at, at + step), slice(FF + at, FF + at + step)
        value = dot(normed_three, w_ff_in[:, values]) + b_ff_in[:, values]
        gate = dot(normed_three, w_ff_in[:, gates]) + b_ff_in[:, gates]
        normal = 0.5 + 0.5 * lax.erf(gate * (0.5**0.5))
        density = jnp.exp(gate * gate * -0.5) * 0.3989422804014327
        gelu = gate * normal
        result += dot_nt((value * gelu).astype(bf16), w_ff_turned[:, values])
        grad_act = dot(upstream, w_ff_turned[:, values])
        grad_value = (grad_act * gelu).astype(bf16)
        grad_gate = (grad_act * value * (normal + gate * density)).astype(bf16)
        grad_normed += dot_nt(grad_value, w_ff_in[:, values])
        grad_normed += dot_nt(grad_gate, w_ff_in[:, gates])
    result_out[...] = result.astype(bf16)
    grad_second = upstream.astype(f32) + norm_back(unit_three, rate_three, grad_normed)
    grad_cross = dot_nt(grad_second.astype(bf16), w_cross_out[...]).astype(bf16)
    outs = []
    for item in range(ITEMS):
        cells = slice(item * PART, (item + 1) * PART)
        grad_probs = dot_nt(spread(grad_cross[cells]), text_values[item])
        probs = probs_keep[item]
        weighted = jnp.sum(probs * grad_probs, -1, keepdims=True)
        grad_scores = (probs * (grad_probs - weighted)).astype(bf16)
        outs.append(gather(dot(grad_scores, text_keys[item])))
    grad_query = (jnp.concatenate(outs, axis=0) * SCALE).astype(bf16)
    grad_first = grad_second + norm_back(
        unit_two, rate_two, dot_nt(grad_query, w_cross_query[...])
    )
    grad_out[...] = grad_first
    pairs = grad_first.reshape(ITEMS, 2, PART // 2, C)
    gap = jnp.zeros((half, split - C), f32)
    both = jnp.concatenate(
        [pairs[:, 0].reshape(half, C), gap, pairs[:, 1].reshape(half, C), gap], axis=1
    ).astype(bf16)
    packed = dot_nt(both, w_attn[...]).astype(bf16)
    for head in range(HEADS):
        piece = packed[:, head * LANES : (head + 1) * LANES]
        heads_out[:, head] = piece.reshape(ITEMS, PART // 2, LANES)


WIDE_BLOCK = 512
WIDE_STEP = 1024


def attend_back_kernel(
    own, other, full, packed, probs_in, own_out, other_out,
    grads, left, keys_turned, sums, scores, probs_a, probs_b, sems,
):
    half, count = HALF // 2, HALF // WIDE_BLOCK

    def block(b):
        return pl.ds(pl.multiple_of(b * WIDE_BLOCK, WIDE_BLOCK), WIDE_BLOCK)

    def fetched(b, probs, n):
        return pltpu.make_async_copy(probs_in.at[block(b)], probs, sems.at[n])

    fetched(0, probs_a, 0).start()
    fetched(1, probs_b, 1).start()
    lane = lane_of((half, LANES))
    value_lane = (lane >= VALUE) & (lane < MASK)
    pairs = packed[...].reshape(half, LANES).astype(f32)
    low = jnp.where(value_lane, pltpu.roll(pairs, VALUE, 1), 0.0)
    high = jnp.where(value_lane, pltpu.roll(pairs, VALUE - HEAD, 1), 0.0)
    shape = (CHIPS, 1, PART // 2, LANES)
    upstream = jnp.concatenate([low.reshape(shape), high.reshape(shape)], axis=1)
    upstream = upstream.reshape(HALF, LANES)
    lane = lane_of((HALF, LANES))
    outputs = full[...]
    upstream *= jnp.sum(jnp.where(lane == 0, outputs, 0.0), axis=1, keepdims=True)
    weighted = jnp.sum(upstream * outputs, axis=1, keepdims=True)
    first = weighted.astype(bf16).astype(f32)
    upstream = jnp.where(lane == MASK + 4, -first, upstream)
    upstream = jnp.where(lane == MASK + 5, first - weighted, upstream).astype(bf16)
    grads[...] = upstream
    query = pltpu.roll(own[...].astype(f32), KEY, 1)
    query = jnp.where((lane >= KEY) & (lane < VALUE), query, 0.0).astype(bf16)
    for b in range(count):
        rows, at = slice(b * WIDE_BLOCK, (b + 1) * WIDE_BLOCK), 2 * b * WIDE_BLOCK
        left[:, at : at + WIDE_BLOCK] = jnp.transpose(query[rows])
        left[:, at + WIDE_BLOCK : at + 2 * WIDE_BLOCK] = jnp.transpose(upstream[rows])
    keys_turned[:, :HALF] = jnp.transpose(own[...])
    keys_turned[:, HALF:] = jnp.transpose(other[...])
    sums[...] = jnp.zeros_like(sums)
    chunks = [(ref, at) for ref in (own, other) for at in range(0, HALF, WIDE_STEP)]

    def work(b, probs):
        rows = block(b)
        upstream = grads[rows, :]
        both = left[:, pl.ds(pl.multiple_of(2 * b * WIDE_BLOCK, 2 * WIDE_BLOCK), 2 * WIDE_BLOCK)]
        for n, (ref, at) in enumerate(chunks):
            keys = slice(n * WIDE_STEP, (n + 1) * WIDE_STEP)
            part = probs[:, keys]
            grad = dot_nt(upstream, ref[at : at + WIDE_STEP, :])
            grad = (part.astype(f32) * grad).astype(bf16)
            sums[:, keys] += dot(both, jnp.concatenate([grad, part], axis=0))
            scores[keys, :] = jnp.transpose(grad)
        grad_query = jnp.transpose(dot(keys_turned[...], scores[...])) * SCALE
        own_out[rows, :] = pltpu.roll(grad_query, LANES - KEY, 1)

    def body(i, carry):
        fetched(2 * i, probs_a, 0).wait()
        work(2 * i, probs_a)

        @pl.when(2 * i + 2 < count)
        def _():
            fetched(2 * i + 2, probs_a, 0).start()

        fetched(2 * i + 1, probs_b, 1).wait()
        work(2 * i + 1, probs_b)

        @pl.when(2 * i + 3 < count)
        def _():
            fetched(2 * i + 3, probs_b, 1).start()

        return carry

    lax.fori_loop(0, count // 2, body, 0)
    scale = jnp.where(lane < VALUE, SCALE, 1.0)
    rest = jnp.where(lane < MASK, jnp.transpose(sums[:, :HALF]) * scale, 0.0)
    own_out[...] = jnp.where(lane < KEY, own_out[...], rest)
    rest = jnp.where(
        (lane >= KEY) & (lane < MASK), jnp.transpose(sums[:, HALF:]) * scale, 0.0
    )
    other_out[...] = rest.astype(bf16)


def finish_kernel(
    place, rows, w_qkv, mixed, grad_first, slope, smooth, cond, w_out, latent_out, parts_out
):
    joined = jnp.concatenate(
        [rows[:, head].reshape(CELLS, LANES) for head in range(HEADS)], axis=1
    )
    unit, rate = moments(mixed[...])
    latent = grad_first[...] + norm_back(unit, rate, dot_nt(joined, w_qkv[...]))
    latent_out[...] = latent
    branch = latent.astype(bf16)
    inner = (dot_nt(branch, w_out[...]) * slope[...]).astype(bf16)
    inner_turned = jnp.transpose(inner)
    branch_turned = jnp.transpose(branch)
    here, there = place[1], 1 - place[1]

    def put(side, at, values):
        values = values.astype(bf16)
        for t in range(0, 3 * LANES, LANES):
            parts_out[side, at : at + C, :] = values[:, t : t + LANES]
            at += C

    lane = lane_of((C, LANES))
    ones = jnp.zeros((C, LANES), f32)
    kept = None
    for n in range(10):
        moment = dot(inner_turned, cond[n]) if n < 9 else dot(branch_turned, cond[4])
        one = pltpu.roll(moment[:, LANES:], n, 1)
        ones = jnp.where(lane == 64 + n, one, ones)
        if n % 2 == 0:
            kept = moment[:, :CIN]
            continue
        both = jnp.concatenate([kept, moment[:, :CIN]], axis=1)
        pair = n // 2
        put(here if pair < 3 else there, 3 * C * (pair % 3), both)
    values = dot(branch_turned, smooth[...])
    last = jnp.concatenate([values[:, 2 * LANES :], ones[:, 64:]], axis=1)
    put(there, 6 * C, jnp.concatenate([values[:, : 2 * LANES], last], axis=1))
    for side in range(2):
        parts_out[side, 9 * C :, :] = jnp.zeros((SUM_ROWS - 9 * C, LANES), bf16)


def weights_kernel(
    place, mine, theirs, w_in, b_in, w_conv, win_out, bin_out, wconv_out, bconv_out, wout_out,
    bout_out, total, taps, sems,
):
    here = place[1]
    total[here] = mine[...]
    total[1 - here] = theirs[...]
    w_turned = jnp.transpose(jnp.concatenate([w_in[...], bias_rows(b_in[...])], axis=0))

    def take(half, at):
        return jnp.concatenate(
            [total[half, at + C * t : at + C * (t + 1), :] for t in range(3)], axis=1
        )

    last = take(1, 6 * C).astype(f32)
    ones = last[:, 2 * LANES :]
    lane = lane_of((C, LANES))

    def moment_of(n):
        pair = n // 2
        both = take(pair // 3, 3 * C * (pair % 3)).astype(f32)
        both = both[:, CIN * (n % 2) : CIN * (n % 2 + 1)]
        one = jnp.sum(jnp.where(lane == 64 + n, ones, 0.0), axis=1, keepdims=True)
        spare = lane_of((C, WIDE - CIN))
        return jnp.concatenate([both, jnp.where(spare < 3, one, 0.0)], axis=1).astype(bf16)

    grad_in = jnp.zeros((C, WIDE), f32)
    copies = []
    for n in range(9):
        moment = moment_of(n)
        taps[n] = dot_nt(w_turned, moment)
        copy = pltpu.make_async_copy(taps.at[n], wconv_out.at[n], sems.at[n])
        copy.start()
        copies.append(copy)
        grad_in += dot(w_conv[n], moment)
        if n == 4:
            bconv_out[...] = jnp.transpose(moment.astype(f32))[CIN]
    moment = jnp.transpose(moment_of(9).astype(f32))
    grad_in = jnp.transpose(grad_in) + moment
    win_out[...] = grad_in[:CIN]
    bin_out[...] = grad_in[CIN]
    bout_out[...] = moment[CIN]
    wout_out[...] = jnp.transpose(last)[:C]
    for copy in copies:
        copy.wait()


def swap(array):
    return lax.ppermute(array, "c", [(0, 1), (1, 0)])


def across(blocks):
    return lax.all_to_all(blocks, ACROSS, 0, 0, tiled=True)


def per_device(
    latent, condition, text_states, valid_rows, text_lengths, w_in, b_in, w_conv, b_conv, w_out,
    b_out, w_query, w_key, w_value, w_attn_out, b_attn_out, w_cross_query, w_cross_key,
    w_cross_value, w_cross_out, b_cross_out, w_ff_in, b_ff_in, w_ff_out, b_ff_out, cotangent,
):
    core = lax.axis_index("c")
    place = jnp.stack([lax.axis_index("sp"), core, 2 * lax.axis_index("x") + core])
    place = place.astype(jnp.int32)

    down = [(i, i + 1) for i in range(15)]
    top = lax.ppermute(condition[:, ROWS - 1 :], "sp", down)
    bottom = lax.ppermute(condition[:, :1], "sp", [(b, a) for a, b in down])
    right_way = [(i, i + 1) for i in range(7)]

    def edge(col):
        tall = jnp.concatenate([top[:, :, col], condition[:, :, col], bottom[:, :, col]], axis=1)
        return tall.reshape(ITEMS * (ROWS + 2), CIN)

    left = lax.ppermute(edge(COLS - 1), ("x", "c"), right_way)
    right = lax.ppermute(edge(0), ("x", "c"), [(b, a) for a, b in right_way])
    taps = w_conv.reshape(9, C, C)

    rows, mixed, smooth, slope, cond = call(
        adapter_kernel,
        (
            out(ITEMS, HEADS, PART, LANES),
            out(CELLS, C, dtype=f32),
            out(CELLS, C),
            out(CELLS, C, dtype=f32),
            out(9, CELLS, WIDE),
        ),
        (
            place, valid_rows, condition, top, bottom, left, right, latent.reshape(CELLS, C),
            w_in, b_in, taps, b_conv, w_out, b_out, w_query, w_key, w_value,
        ),
        "adapter",
        scalars=2,
        scratch=[pltpu.VMEM((WIDE, C), bf16)],
        vmem=24,
        fetch=(8, 9, 10, 2, 7, 11, 12, 13, 14, 15, 16),
        store=(0, 1, 2, 3, 4),
    )

    text, key_weight, value_weight, rows = lax.optimization_barrier(
        (text_states, w_cross_key, w_cross_value, rows)
    )
    text_keys, text_values = call(
        text_kernel,
        (out(ITEMS, TEXT, C), out(ITEMS, TEXT, C)),
        (text.transpose(1, 0, 2).reshape(-1, text.shape[2]), key_weight.T, value_weight.T),
        "text",
        fetch=(0, 1, 2),
        store=(0, 1),
    )
    own = across(rows.reshape(CHIPS, PART, LANES)).reshape(HALF, LANES)
    other = swap(own)
    packed, full, probs = call(
        attend_kernel,
        (
            out(CHIPS, PART // 2, LANES),
            out(HALF, LANES, dtype=f32),
            out(HALF, 2 * HALF),
        ),
        (own, other),
        "attend",
        scratch=[
            pltpu.VMEM((2 * HALF, BLOCK), f32),
            pltpu.VMEM((2 * HALF, BLOCK), f32),
            pltpu.VMEM((2 * HALF, BLOCK), bf16),
            pltpu.VMEM((2 * HALF, BLOCK), bf16),
            pltpu.VMEM((BLOCK, 2 * HALF), bf16),
            pltpu.VMEM((BLOCK, 2 * HALF), bf16),
            pltpu.VMEM((LANES, 2 * HALF), bf16),
            pltpu.VMEM((LANES, HALF), bf16),
            pltpu.VMEM((LANES, HALF), f32),
            pltpu.SemaphoreType.DMA((2,)),
        ],
        vmem=32,
        store=(0, 1),
        far=(4,),
    )

    attn_weight, query_weight, key_weight, value_weight, packed = lax.optimization_barrier(
        (w_attn_out, w_query, w_key, w_value, packed)
    )
    w_qkv = jnp.concatenate(
        [w.reshape(C, HEADS, HEAD) for w in (query_weight, key_weight, value_weight)], axis=-1
    )
    w_qkv = jnp.pad(w_qkv, ((0, 0), (0, 0), (0, LANES - 3 * HEAD))).reshape(C, HEADS * LANES)
    by_head = attn_weight.reshape(HEADS, HEAD, C)
    w_attn = jnp.concatenate(
        [
            jnp.pad(by_head, ((0, 0), (at, LANES - HEAD - at), (0, 384 - C)))
            for at in (0, HEAD)
        ],
        axis=-1,
    ).reshape(HEADS * LANES, 768)
    heads_in = across(packed).reshape(ITEMS, HEADS, PART // 2, LANES)

    result, grad_first, heads_out = call(
        middle_kernel,
        (out(CELLS, C), out(CELLS, C, dtype=f32), out(ITEMS, HEADS, PART // 2, LANES)),
        (
            text_lengths, heads_in, mixed, cotangent.reshape(CELLS, C), text_keys, text_values,
            w_attn, b_attn_out, w_cross_query, w_cross_out, b_cross_out, w_ff_in, b_ff_in[None],
            w_ff_out.T, b_ff_out,
        ),
        "middle",
        scalars=1,
        scratch=[pltpu.VMEM((ITEMS, HEADS * PART, TEXT), f32)],
        vmem=32,
        fetch=(6, 2, 7, 8, 4, 5, 9, 10, 3, 11, 12, 13, 14),
        store=(0, 1),
    )

    grads_in = across(heads_out.reshape(CHIPS, PART // 2, LANES))
    own_grads, other_grads = call(
        attend_back_kernel,
        (out(HALF, LANES, dtype=f32), out(HALF, LANES)),
        (own, other, full, grads_in, probs),
        "attend_back",
        scratch=[
            pltpu.VMEM((HALF, LANES), bf16),
            pltpu.VMEM((LANES, 2 * HALF), bf16),
            pltpu.VMEM((LANES, 2 * HALF), bf16),
            pltpu.VMEM((LANES, 2 * HALF), f32),
            pltpu.VMEM((2 * HALF, WIDE_BLOCK), bf16),
            pltpu.VMEM((WIDE_BLOCK, 2 * HALF), bf16),
            pltpu.VMEM((WIDE_BLOCK, 2 * HALF), bf16),
            pltpu.SemaphoreType.DMA((2,)),
        ],
        vmem=36,
        fetch=(2,),
        far=(4,),
    )
    row_grads = (own_grads + swap(other_grads).astype(f32)).astype(bf16)
    row_grads = across(row_grads.reshape(CHIPS, PART, LANES))

    latent_grad, parts = call(
        finish_kernel,
        (out(CELLS, C, dtype=f32), out(2, SUM_ROWS, LANES)),
        (
            place, row_grads.reshape(ITEMS, HEADS, PART, LANES), w_qkv, mixed, grad_first, slope,
            smooth, cond, w_out,
        ),
        "finish",
        scalars=1,
        fetch=(2, 3, 4, 8, 5, 7, 6),
        store=(0,),
    )

    shares = (parts[0].astype(f32) + swap(parts[1]).astype(f32)).astype(bf16)
    shares = across(shares.reshape(CHIPS, SUM_ROWS // CHIPS, LANES))
    share = jnp.sum(shares.astype(f32), axis=0).astype(bf16)
    mine = across(jnp.broadcast_to(share[None], shares.shape)).reshape(SUM_ROWS, LANES)
    theirs = swap(mine)
    grad_w_in, grad_b_in, grad_w_conv, grad_b_conv, grad_w_out, grad_b_out = call(
        weights_kernel,
        (
            out(CIN, C, dtype=f32),
            out(C, dtype=f32),
            out(9, C, C, dtype=f32),
            out(C, dtype=f32),
            out(C, C, dtype=f32),
            out(C, dtype=f32),
        ),
        (place, mine, theirs, w_in, b_in, taps),
        "weights",
        scalars=1,
        scratch=[
            pltpu.VMEM((2, SUM_ROWS, LANES), bf16),
            pltpu.VMEM((9, C, C), f32),
            pltpu.SemaphoreType.DMA((9,)),
        ],
        vmem=24,
        fetch=(3, 4, 5),
        store=(0, 4),
        far=(8,),
    )
    grid = (ITEMS, ROWS, COLS, C)
    return (
        result.reshape(grid),
        latent_grad.reshape(grid),
        grad_w_in,
        grad_b_in,
        grad_w_conv.reshape(3, 3, C, C),
        grad_b_conv,
        grad_w_out,
        grad_b_out,
    )


def solution(mesh):
    split = Mesh(mesh.devices.reshape(16, 4, 2), ("sp", "x", "c"))
    cells = P(None, "sp", ("x", "c"), None)
    in_specs = (cells, cells) + (P(),) * 23 + (cells,)
    out_specs = (cells, cells) + (P(),) * 6
    return jax.shard_map(
        per_device, mesh=split, in_specs=in_specs, out_specs=out_specs, check_vma=False
    )
```

```python
import jax
import jax.numpy as jnp
from jax import lax
from jax.experimental import pallas as pl
from jax.experimental.pallas import tpu as pltpu
from jax.sharding import Mesh
from jax.sharding import PartitionSpec as P

ITEMS, ROWS, COLS, C, CIN, HEADS, HEAD, FF = 8, 4, 8, 320, 192, 8, 40, 1280
CELLS = ITEMS * ROWS * COLS
PART = ROWS * COLS
CHIPS = 64
HALF = CHIPS * PART
TEXT = 80
LANES = 128
WIDE = 256
SCALE = HEAD**-0.5
LOG2E = 1.4426950408889634
EPS = 1e-5
MASKED = -1e30
KEY, VALUE, MASK = HEAD, 2 * HEAD, 3 * HEAD
ACROSS = ("sp", "x")
SUM_ROWS = 3072

bf16, f32 = jnp.bfloat16, jnp.float32
NT = (((1,), (1,)), ((), ()))


def dot(left, right):
    return jnp.dot(left, right, preferred_element_type=f32)


def dot_nt(left, right):
    return lax.dot_general(left, right, NT, preferred_element_type=f32)


def lane_of(shape):
    return lax.broadcasted_iota(jnp.int32, shape, len(shape) - 1)


def moments(values):
    center = values - jnp.mean(values, -1, keepdims=True)
    rate = lax.rsqrt(jnp.mean(center * center, -1, keepdims=True) + EPS)
    return center * rate, rate


def norm_back(unit, rate, grads):
    return rate * (
        grads
        - jnp.mean(grads, -1, keepdims=True)
        - unit * jnp.mean(grads * unit, -1, keepdims=True)
    )


class Fetched:
    def __init__(self, source, buffer, semaphore):
        self.copy = pltpu.make_async_copy(source, buffer, semaphore)
        self.buffer, self.shape, self.here = buffer, buffer.shape, False
        self.copy.start()

    def __getitem__(self, index):
        if not self.here:
            self.copy.wait()
            self.here = True
        return self.buffer[index]


class Stored:
    def __init__(self, target, buffer, semaphore):
        self.copy = pltpu.make_async_copy(buffer, target, semaphore)
        self.buffer, self.started = buffer, False

    def __setitem__(self, index, values):
        self.buffer[index] = values
        if index is Ellipsis:
            self.start()

    def start(self):
        if not self.started:
            self.copy.start()
            self.started = True


def call(kernel, outs, ins, name, scalars=0, scratch=(), vmem=16, fetch=(), store=(), far=(),
    near=(), held=(),
):
    fetch, store = list(fetch), list(store)
    far_in = [i for i in far if i < len(ins)]
    far_out = [i - len(ins) for i in far if i >= len(ins)]

    def body(*refs):
        refs = list(refs)
        given, refs = refs[: len(ins)], refs[len(ins) :]
        made, refs = refs[: len(outs)], refs[len(outs) :]
        own, refs = refs[: len(scratch)], refs[len(scratch) :]
        buffers, semaphores = refs[:-1], refs[-1] if refs else None
        for n, i in enumerate(fetch):
            given[i] = Fetched(given[i], buffers[n], semaphores.at[n])
        kept = []
        for n, i in enumerate(store, len(fetch)):
            made[i] = Stored(made[i], buffers[n], semaphores.at[n])
            kept.append(made[i])
        kernel(*given, *made, *own)
        for part in given:
            if isinstance(part, Fetched) and not part.here:
                part.copy.wait()
        for part in kept:
            part.start()
        for part in kept:
            part.copy.wait()

    def made_as(i, made):
        if i in store or i in far_out:
            return pltpu.HBM(made.shape, made.dtype)
        return pltpu.VMEM(made.shape, made.dtype) if i in near else made

    def in_spec(i):
        if i < scalars:
            return pl.BlockSpec(memory_space=pltpu.SMEM)
        space = pltpu.HBM if i in fetch or i in far_in else pltpu.VMEM
        return pl.BlockSpec(memory_space=space)

    def out_spec(i):
        space = pltpu.HBM if i in store or i in far_out else pltpu.VMEM
        return pl.BlockSpec(memory_space=space)

    extra = [pltpu.VMEM(ins[i].shape, ins[i].dtype) for i in fetch]
    extra += [pltpu.VMEM(outs[i].shape, outs[i].dtype) for i in store]
    if extra:
        extra.append(pltpu.SemaphoreType.DMA((len(extra),)))
    return pl.pallas_call(
        body,
        out_shape=tuple(made_as(i, made) for i, made in enumerate(outs)),
        in_specs=[in_spec(i) for i in range(len(ins))],
        out_specs=tuple(out_spec(i) for i in range(len(outs))),
        scratch_shapes=list(scratch) + extra,
        compiler_params=pltpu.CompilerParams(vmem_limit_bytes=vmem << 20),
        name=name,
    )(
        *(
            pltpu.with_memory_space_constraint(x, pltpu.HBM)
            if i in fetch or i in far_in
            else (pltpu.with_memory_space_constraint(x, pltpu.VMEM) if i in held else x)
            for i, x in enumerate(ins)
        )
    )


def bring(arrays, name, kernel=None, made=(), near=()):
    count, given = len(arrays), len(near)

    def body(*refs):
        sources, inputs = refs[:count], refs[count : count + given]
        targets = refs[count + given : -1]
        copies = [
            pltpu.make_async_copy(sources[n], targets[n], refs[-1].at[n]) for n in range(count)
        ]
        for copy in copies:
            copy.start()
        if kernel is not None:
            kernel(*inputs, *targets[count:])
        for copy in copies:
            copy.wait()

    shapes = [jax.ShapeDtypeStruct(x.shape, x.dtype) for x in arrays] + list(made)
    return pl.pallas_call(
        body,
        out_shape=tuple(pltpu.VMEM(x.shape, x.dtype) for x in shapes),
        in_specs=[pl.BlockSpec(memory_space=pltpu.HBM)] * count
        + [pl.BlockSpec(memory_space=pltpu.VMEM)] * given,
        out_specs=(pl.BlockSpec(memory_space=pltpu.VMEM),) * len(shapes),
        scratch_shapes=[pltpu.SemaphoreType.DMA((max(count, 1),))],
        compiler_params=pltpu.CompilerParams(vmem_limit_bytes=8 << 20),
        name=name,
    )(*(pltpu.with_memory_space_constraint(x, pltpu.HBM) for x in arrays), *near)


def after(value, *arrays):
    return lax.optimization_barrier((value,) + arrays)


def out(*shape, dtype=bf16):
    return jax.ShapeDtypeStruct(shape, dtype)


def bias_rows(bias):
    row = lax.broadcasted_iota(jnp.int32, (WIDE - CIN, C), 0)
    rest = jnp.broadcast_to(bias, (WIDE - CIN, C))
    rows = jnp.zeros((WIDE - CIN, C), f32)
    for n in range(3):
        piece = rest.astype(bf16).astype(f32)
        rows = jnp.where(row == n, piece, rows)
        rest = rest - piece
    return rows.astype(bf16)


def adapter_kernel(
    place, valid, center, top, bottom, left, right, latent, w_in, b_in, w_conv, b_conv, w_out,
    b_out, w_query, w_key, w_value, rows_out, mixed_out, smooth_out, slope_out, cond_out,
    w_wide,
):
    span = ITEMS * (ROWS + 2)
    w_wide[:CIN, :] = w_in[...]
    w_wide[CIN:, :] = bias_rows(b_in[...])

    def widen(values):
        blank = jnp.zeros(values.shape[:-1] + (WIDE - CIN,), f32)
        return jnp.concatenate([values.astype(f32), blank], axis=-1)

    block = jnp.concatenate([top[...], center[...], bottom[...]], axis=1)
    block = widen(block.reshape(span, COLS, CIN))
    shape = (ITEMS, ROWS + 2, COLS, WIDE)
    row = lax.broadcasted_iota(jnp.int32, shape, 1) + ROWS * place[0] - 1
    inside = (row >= 0) & (row < ROWS * 16)
    inside = jnp.where(inside, 1.0, 0.0).reshape(span, COLS, WIDE)
    lane = lane_of((span, COLS, WIDE))
    col = lax.broadcasted_iota(jnp.int32, (span, COLS, WIDE), 1)
    at = COLS * place[2]
    edges = []
    for n, side in enumerate((left, right)):
        there = (at > 0) if n == 0 else (at < COLS * 7)
        edges.append((widen(side[...]).reshape(span, 1, WIDE), jnp.where(there, inside, 0.0)))
    near = jnp.where(col == 0, edges[0][0], pltpu.roll(block, 1, 1))
    near_inside = jnp.where(col == 0, edges[0][1], inside)
    far = jnp.where(col == COLS - 1, edges[1][0], pltpu.roll(block, COLS - 1, 1))
    far_inside = jnp.where(col == COLS - 1, edges[1][1], inside)
    inner = jnp.zeros((CELLS, C), f32)
    start_here = None
    one = (lane >= CIN) & (lane < CIN + 3)
    moves = ((near, near_inside), (block, inside), (far, far_inside))
    for j, (moved, present) in enumerate(moves):
        moved = jnp.where(one, present, moved)
        start = dot(moved.reshape(span * COLS, WIDE).astype(bf16), w_wide[...])
        start = start.reshape(ITEMS, ROWS + 2, COLS, C)
        moved = moved.reshape(ITEMS, ROWS + 2, COLS, WIDE)
        for i in range(3):
            patch = start[:, i : i + ROWS].reshape(CELLS, C).astype(bf16)
            if i == 1 and j == 1:
                start_here = patch.astype(f32)
            inner += dot(patch, w_conv[3 * i + j])
            cond_out[3 * i + j] = moved[:, i : i + ROWS].reshape(CELLS, WIDE).astype(bf16)
    inner += b_conv[...]
    gate = jax.nn.sigmoid(inner)
    smooth = (inner * gate).astype(bf16)
    smooth_out[...] = smooth
    slope_out[...] = gate * (1.0 + inner * (1.0 - gate))
    mixed = latent[...].astype(f32) + (start_here + dot(smooth, w_out[...]) + b_out[...])
    mixed_out[...] = mixed
    normed = moments(mixed)[0].astype(bf16)
    projected = [dot(normed, w[...]) for w in (w_query, w_key, w_value)]
    lane = lane_of((PART, LANES - MASK))
    row = lax.broadcasted_iota(jnp.int32, (PART, LANES - MASK), 0) // COLS + ROWS * place[0]
    extras = []
    for item in range(ITEMS):
        hidden = jnp.where(row >= valid[item], MASKED, 0.0)
        extras.append(jnp.where(lane == 0, hidden, 1.0))
    extras = jnp.concatenate(extras, axis=0)
    for head in range(HEADS):
        at = slice(head * HEAD, (head + 1) * HEAD)
        joined = jnp.concatenate([part[:, at] for part in projected] + [extras], axis=1)
        rows_out[:, head] = joined.astype(bf16).reshape(ITEMS, PART, LANES)


def text_kernel(text, w_key_turned, w_value_turned, keys_out, values_out):
    count = text.shape[0]
    token = lax.broadcasted_iota(jnp.int32, (TEXT, count), 0)
    place = lane_of((TEXT, count))
    text[:1], w_key_turned[:1], w_value_turned[:1]

    def body(item, carry):
        pick = jnp.where(place == token * ITEMS + item, 1.0, 0.0).astype(bf16)
        states = dot(pick, text[...]).astype(bf16)
        keys_out[item] = dot_nt(states, w_key_turned[...]).astype(bf16)
        values_out[item] = dot_nt(states, w_value_turned[...]).astype(bf16)
        return carry

    lax.fori_loop(0, ITEMS, body, 0)


BLOCK = 256
STEP = 512


def attend_kernel(
    own, other, packed_out, full_out, probs_out,
    scores_a, scores_b, probs_a, probs_b, turned_a, turned_b, keys_turned, query, output, sems,
):
    count = HALF // BLOCK
    keys_turned[:, :HALF] = jnp.transpose(own[...])
    keys_turned[:, HALF:] = jnp.transpose(other[...])
    lane = lane_of((HALF, LANES))
    rows = pltpu.roll(own[...].astype(f32), KEY, 1)
    rows = jnp.where((lane >= KEY) & (lane < VALUE), rows, jnp.where(lane == MASK, 1.0, 0.0))
    query[...] = jnp.transpose(rows.astype(bf16))
    chunks = [(ref, at) for ref in (own, other) for at in range(0, HALF, STEP)]

    def columns(b):
        return pl.ds(pl.multiple_of(b * BLOCK, BLOCK), BLOCK)

    def score(queries, n, scores, peak):
        ref, at = chunks[n]
        part = dot(ref[at : at + STEP, :], queries)
        scores[n * STEP : (n + 1) * STEP, :] = part
        part = jnp.max(part.reshape(STEP // 8, 8, BLOCK), axis=0)
        return part if peak is None else jnp.maximum(peak, part)

    def sent(b, turned, n):
        return pltpu.make_async_copy(turned, probs_out.at[columns(b)], sems.at[n])

    def half(b, peak, following, scores, probs, turned):
        shift = jnp.max(peak, axis=0, keepdims=True) * (SCALE * LOG2E)
        queries = query[:, columns(jnp.minimum(b + 1, count - 1))]
        ahead = None
        for n in range(len(chunks)):
            ahead = score(queries, n, following, ahead)
            keys = slice(n * STEP, (n + 1) * STEP)
            part = jnp.exp2(scores[keys, :] * (SCALE * LOG2E) - shift).astype(bf16)
            probs[keys, :] = part
            turned[:, keys] = jnp.transpose(part)
        output[:, columns(b)] = dot(keys_turned[...], probs[...])
        return ahead

    peak = None
    for n in range(len(chunks)):
        peak = score(query[:, :BLOCK], n, scores_a, peak)

    def body(i, peak):
        @pl.when(i > 0)
        def _():
            sent(2 * i - 2, turned_a, 0).wait()

        peak = half(2 * i, peak, scores_b, scores_a, probs_a, turned_a)
        sent(2 * i, turned_a, 0).start()

        @pl.when(i > 0)
        def _():
            sent(2 * i - 1, turned_b, 1).wait()

        peak = half(2 * i + 1, peak, scores_a, scores_b, probs_b, turned_b)
        sent(2 * i + 1, turned_b, 1).start()
        return peak

    lax.fori_loop(0, count // 2, body, peak)
    total = output[...]
    inverse = 1.0 / total[MASK + 1 : MASK + 2, :]
    row = lax.broadcasted_iota(jnp.int32, (LANES, HALF), 0)
    total = jnp.transpose(jnp.where(row == 0, inverse, total * inverse))
    full_out[...] = total
    pairs = total.reshape(CHIPS, 2, PART // 2, LANES)
    lane = lane_of((HALF // 2, LANES))
    low = pltpu.roll(pairs[:, 0].reshape(HALF // 2, LANES), LANES - VALUE, 1)
    high = pltpu.roll(pairs[:, 1].reshape(HALF // 2, LANES), LANES - VALUE + HEAD, 1)
    packed = jnp.where(lane < HEAD, low, jnp.where(lane < 2 * HEAD, high, 0.0))
    packed_out[...] = packed.astype(bf16).reshape(CHIPS, PART // 2, LANES)
    sent(count - 2, turned_a, 0).wait()
    sent(count - 1, turned_b, 1).wait()


def middle_kernel(
    lengths, heads_in, mixed, cotangent, text_keys, text_values, w_attn, b_attn, w_cross_query,
    w_cross_out, b_cross, w_ff_in, b_ff_in, w_ff_turned, b_ff_out, result_out, grad_out, heads_out,
    probs_keep,
):
    half = CELLS // 2
    split = w_attn.shape[1] // 2
    packed = jnp.concatenate(
        [heads_in[:, head].reshape(half, LANES) for head in range(HEADS)], axis=1
    )
    both = dot(packed, w_attn[...])
    shape = (ITEMS, 1, PART // 2, C)
    attended = jnp.concatenate(
        [both[:, :C].reshape(shape), both[:, split : split + C].reshape(shape)], axis=1
    ).reshape(CELLS, C)
    first = mixed[...] + attended + b_attn[...]
    unit_two, rate_two = moments(first)
    cross_query = dot(unit_two.astype(bf16), w_cross_query[...]).astype(bf16)
    lane = lane_of((PART, C))
    in_head = [(lane >= HEAD * h) & (lane < HEAD * (h + 1)) for h in range(HEADS)]

    def spread(values):
        return jnp.concatenate(
            [jnp.where(mask, values, jnp.zeros_like(values)) for mask in in_head], axis=0
        )

    def gather(values):
        total = jnp.zeros((PART, C), f32)
        for h, mask in enumerate(in_head):
            total = jnp.where(mask, values[h * PART : (h + 1) * PART], total)
        return total

    token = lane_of((HEADS * PART, TEXT))
    outs = []
    for item in range(ITEMS):
        cells = slice(item * PART, (item + 1) * PART)
        scores = dot_nt(spread(cross_query[cells]), text_keys[item]) * SCALE
        scores = jnp.where(token < lengths[item], scores, MASKED)
        weights = jnp.exp(scores - jnp.max(scores, -1, keepdims=True))
        probs = weights / jnp.sum(weights, -1, keepdims=True)
        probs_keep[item] = probs
        outs.append(gather(dot(probs.astype(bf16), text_values[item])))
    cross = jnp.concatenate(outs, axis=0).astype(bf16)
    second = first + dot(cross, w_cross_out[...]) + b_cross[...]
    unit_three, rate_three = moments(second)
    normed_three = unit_three.astype(bf16)
    upstream = cotangent[...]
    result = second + b_ff_out[...]
    grad_normed = jnp.zeros((CELLS, C), f32)
    step = 256
    for at in range(0, FF, step):
        values, gates = slice(at, at + step), slice(FF + at, FF + at + step)
        value = dot(normed_three, w_ff_in[:, values]) + b_ff_in[values]
        gate = dot(normed_three, w_ff_in[:, gates]) + b_ff_in[gates]
        normal = 0.5 + 0.5 * lax.erf(gate * (0.5**0.5))
        density = jnp.exp(gate * gate * -0.5) * 0.3989422804014327
        gelu = gate * normal
        result += dot_nt((value * gelu).astype(bf16), w_ff_turned[:, values])
        grad_act = dot(upstream, w_ff_turned[:, values])
        grad_value = (grad_act * gelu).astype(bf16)
        grad_gate = (grad_act * value * (normal + gate * density)).astype(bf16)
        grad_normed += dot_nt(grad_value, w_ff_in[:, values])
        grad_normed += dot_nt(grad_gate, w_ff_in[:, gates])
    result_out[...] = result.astype(bf16)
    grad_second = upstream.astype(f32) + norm_back(unit_three, rate_three, grad_normed)
    grad_cross = dot_nt(grad_second.astype(bf16), w_cross_out[...]).astype(bf16)
    outs = []
    for item in range(ITEMS):
        cells = slice(item * PART, (item + 1) * PART)
        grad_probs = dot_nt(spread(grad_cross[cells]), text_values[item])
        probs = probs_keep[item]
        weighted = jnp.sum(probs * grad_probs, -1, keepdims=True)
        grad_scores = (probs * (grad_probs - weighted)).astype(bf16)
        outs.append(gather(dot(grad_scores, text_keys[item])))
    grad_query = (jnp.concatenate(outs, axis=0) * SCALE).astype(bf16)
    grad_first = grad_second + norm_back(
        unit_two, rate_two, dot_nt(grad_query, w_cross_query[...])
    )
    grad_out[...] = grad_first
    pairs = grad_first.reshape(ITEMS, 2, PART // 2, C)
    gap = jnp.zeros((half, split - C), f32)
    both = jnp.concatenate(
        [pairs[:, 0].reshape(half, C), gap, pairs[:, 1].reshape(half, C), gap], axis=1
    ).astype(bf16)
    packed = dot_nt(both, w_attn[...]).astype(bf16)
    for head in range(HEADS):
        piece = packed[:, head * LANES : (head + 1) * LANES]
        heads_out[:, head] = piece.reshape(ITEMS, PART // 2, LANES)


WIDE_BLOCK = 512
WIDE_STEP = 1024


def turn_kernel(own, other, keys_out, query_out):
    keys_out[:, :HALF] = jnp.transpose(own[...])
    keys_out[:, HALF:] = jnp.transpose(other[...])
    lane = lane_of((HALF, LANES))
    query = pltpu.roll(own[...].astype(f32), KEY, 1)
    query = jnp.where((lane >= KEY) & (lane < VALUE), query, 0.0).astype(bf16)
    query_out[...] = jnp.transpose(query)


def attend_back_kernel(
    keys_turned, query_turned, full, packed, probs_in, own_out, other_out,
    grads, left, sums, scores, probs_a, probs_b, sems,
):
    half, count = HALF // 2, HALF // WIDE_BLOCK

    def block(b):
        return pl.ds(pl.multiple_of(b * WIDE_BLOCK, WIDE_BLOCK), WIDE_BLOCK)

    def fetched(b, probs, n):
        return pltpu.make_async_copy(probs_in.at[block(b)], probs, sems.at[n])

    fetched(0, probs_a, 0).start()
    fetched(1, probs_b, 1).start()
    lane = lane_of((half, LANES))
    value_lane = (lane >= VALUE) & (lane < MASK)
    pairs = packed[...].reshape(half, LANES).astype(f32)
    low = jnp.where(value_lane, pltpu.roll(pairs, VALUE, 1), 0.0)
    high = jnp.where(value_lane, pltpu.roll(pairs, VALUE - HEAD, 1), 0.0)
    shape = (CHIPS, 1, PART // 2, LANES)
    upstream = jnp.concatenate([low.reshape(shape), high.reshape(shape)], axis=1)
    upstream = upstream.reshape(HALF, LANES)
    lane = lane_of((HALF, LANES))
    outputs = full[...]
    upstream *= jnp.sum(jnp.where(lane == 0, outputs, 0.0), axis=1, keepdims=True)
    weighted = jnp.sum(upstream * outputs, axis=1, keepdims=True)
    first = weighted.astype(bf16).astype(f32)
    upstream = jnp.where(lane == MASK + 4, -first, upstream)
    upstream = jnp.where(lane == MASK + 5, first - weighted, upstream).astype(bf16)
    grads[...] = upstream
    for b in range(count):
        rows, at = slice(b * WIDE_BLOCK, (b + 1) * WIDE_BLOCK), 2 * b * WIDE_BLOCK
        left[:, at : at + WIDE_BLOCK] = query_turned[:, rows]
        left[:, at + WIDE_BLOCK : at + 2 * WIDE_BLOCK] = jnp.transpose(upstream[rows])
    sums[...] = jnp.zeros_like(sums)

    def work(b, probs):
        rows = block(b)
        upstream = grads[rows, :]
        both = left[:, pl.ds(pl.multiple_of(2 * b * WIDE_BLOCK, 2 * WIDE_BLOCK), 2 * WIDE_BLOCK)]
        for at in range(0, 2 * HALF, WIDE_STEP):
            keys = slice(at, at + WIDE_STEP)
            part = probs[:, keys]
            grad = dot(upstream, keys_turned[:, keys])
            grad = (part.astype(f32) * grad).astype(bf16)
            sums[:, keys] += dot(both, jnp.concatenate([grad, part], axis=0))
            scores[keys, :] = jnp.transpose(grad)
        grad_query = jnp.transpose(dot(keys_turned[...], scores[...])) * SCALE
        own_out[rows, :] = pltpu.roll(grad_query, LANES - KEY, 1)

    def body(i, carry):
        fetched(2 * i, probs_a, 0).wait()
        work(2 * i, probs_a)

        @pl.when(2 * i + 2 < count)
        def _():
            fetched(2 * i + 2, probs_a, 0).start()

        fetched(2 * i + 1, probs_b, 1).wait()
        work(2 * i + 1, probs_b)

        @pl.when(2 * i + 3 < count)
        def _():
            fetched(2 * i + 3, probs_b, 1).start()

        return carry

    lax.fori_loop(0, count // 2, body, 0)
    scale = jnp.where(lane < VALUE, SCALE, 1.0)
    rest = jnp.where(lane < MASK, jnp.transpose(sums[:, :HALF]) * scale, 0.0)
    own_out[...] = jnp.where(lane < KEY, own_out[...], rest)
    rest = jnp.where(
        (lane >= KEY) & (lane < MASK), jnp.transpose(sums[:, HALF:]) * scale, 0.0
    )
    other_out[...] = rest.astype(bf16)


def join_kernel(w_query, w_key, w_value, joined_out):
    blank = jnp.zeros((C, LANES - MASK), f32)
    parts = [w[...].astype(f32) for w in (w_query, w_key, w_value)]
    for head in range(HEADS):
        at = slice(head * HEAD, (head + 1) * HEAD)
        joined = jnp.concatenate([part[:, at] for part in parts] + [blank], axis=1)
        joined_out[:, head * LANES : (head + 1) * LANES] = joined.astype(bf16)


def spread_kernel(w_attn, spread_out):
    rows = w_attn[...].astype(f32)
    gap = jnp.zeros((HEAD, 384 - C), f32)
    for head in range(HEADS):
        part = jnp.concatenate([rows[head * HEAD : (head + 1) * HEAD], gap], axis=1)
        blank = jnp.zeros_like(part)
        block = jnp.concatenate(
            [
                jnp.concatenate([part, blank], axis=1),
                jnp.concatenate([blank, part], axis=1),
                jnp.zeros((LANES - 2 * HEAD, 768), f32),
            ],
            axis=0,
        )
        spread_out[head * LANES : (head + 1) * LANES, :] = block.astype(bf16)


def widen_kernel(w_in, b_in, turned_out):
    wide = jnp.concatenate([w_in[...], bias_rows(b_in[...])], axis=0)
    turned_out[...] = jnp.transpose(wide)


def finish_kernel(
    place, rows, w_qkv, mixed, grad_first, slope, smooth, cond, w_out, latent_out, parts_out
):
    joined = jnp.concatenate(
        [rows[:, head].reshape(CELLS, LANES) for head in range(HEADS)], axis=1
    )
    unit, rate = moments(mixed[...])
    latent = grad_first[...] + norm_back(unit, rate, dot_nt(joined, w_qkv[...]))
    latent_out[...] = latent
    branch = latent.astype(bf16)
    inner = (dot_nt(branch, w_out[...]) * slope[...]).astype(bf16)
    inner_turned = jnp.transpose(inner)
    branch_turned = jnp.transpose(branch)
    here, there = place[1], 1 - place[1]

    def put(side, at, values):
        values = values.astype(bf16)
        for t in range(0, 3 * LANES, LANES):
            parts_out[side, at : at + C, :] = values[:, t : t + LANES]
            at += C

    lane = lane_of((C, LANES))
    ones = jnp.zeros((C, LANES), f32)
    kept = None
    for n in range(10):
        moment = dot(inner_turned, cond[n]) if n < 9 else dot(branch_turned, cond[4])
        one = pltpu.roll(moment[:, LANES:], n, 1)
        ones = jnp.where(lane == 64 + n, one, ones)
        if n % 2 == 0:
            kept = moment[:, :CIN]
            continue
        both = jnp.concatenate([kept, moment[:, :CIN]], axis=1)
        pair = n // 2
        put(here if pair < 3 else there, 3 * C * (pair % 3), both)
    values = dot(branch_turned, smooth[...])
    last = jnp.concatenate([values[:, 2 * LANES :], ones[:, 64:]], axis=1)
    put(there, 6 * C, jnp.concatenate([values[:, : 2 * LANES], last], axis=1))
    for side in range(2):
        parts_out[side, 9 * C :, :] = jnp.zeros((SUM_ROWS - 9 * C, LANES), bf16)


def weights_kernel(
    place, mine, theirs, w_turned, w_conv, win_out, bin_out, wconv_out, bconv_out, wout_out,
    bout_out, total, taps, sems,
):
    here = place[1]
    total[here] = mine[...]
    total[1 - here] = theirs[...]

    def take(half, at):
        return jnp.concatenate(
            [total[half, at + C * t : at + C * (t + 1), :] for t in range(3)], axis=1
        )

    last = take(1, 6 * C).astype(f32)
    ones = last[:, 2 * LANES :]
    lane = lane_of((C, LANES))

    def moment_of(n):
        pair = n // 2
        both = take(pair // 3, 3 * C * (pair % 3)).astype(f32)
        both = both[:, CIN * (n % 2) : CIN * (n % 2 + 1)]
        one = jnp.sum(jnp.where(lane == 64 + n, ones, 0.0), axis=1, keepdims=True)
        spare = lane_of((C, WIDE - CIN))
        return jnp.concatenate([both, jnp.where(spare < 3, one, 0.0)], axis=1).astype(bf16)

    grad_in = jnp.zeros((C, WIDE), f32)
    copies = []
    for n in range(9):
        moment = moment_of(n)
        taps[n] = dot_nt(w_turned[...], moment)
        copy = pltpu.make_async_copy(taps.at[n], wconv_out.at[n], sems.at[n])
        copy.start()
        copies.append(copy)
        grad_in += dot(w_conv[n], moment)
        if n == 4:
            bconv_out[...] = jnp.transpose(moment.astype(f32))[CIN]
    moment = jnp.transpose(moment_of(9).astype(f32))
    grad_in = jnp.transpose(grad_in) + moment
    win_out[...] = grad_in[:CIN]
    bin_out[...] = grad_in[CIN]
    bout_out[...] = moment[CIN]
    wout_out[...] = jnp.transpose(last)[:C]
    for copy in copies:
        copy.wait()


def swap(array):
    return lax.ppermute(array, "c", [(0, 1), (1, 0)])


def across(blocks):
    return lax.all_to_all(blocks, ACROSS, 0, 0, tiled=True)


def per_device(
    latent, condition, text_states, valid_rows, text_lengths, w_in, b_in, w_conv, b_conv, w_out,
    b_out, w_query, w_key, w_value, w_attn_out, b_attn_out, w_cross_query, w_cross_key,
    w_cross_value, w_cross_out, b_cross_out, w_ff_in, b_ff_in, w_ff_out, b_ff_out, cotangent,
):
    core = lax.axis_index("c")
    place = jnp.stack([lax.axis_index("sp"), core, 2 * lax.axis_index("x") + core])
    place = place.astype(jnp.int32)

    down = [(i, i + 1) for i in range(15)]
    top = lax.ppermute(condition[:, ROWS - 1 :], "sp", down)
    bottom = lax.ppermute(condition[:, :1], "sp", [(b, a) for a, b in down])
    right_way = [(i, i + 1) for i in range(7)]

    def edge(col):
        tall = jnp.concatenate([top[:, :, col], condition[:, :, col], bottom[:, :, col]], axis=1)
        return tall.reshape(ITEMS * (ROWS + 2), CIN)

    left = lax.ppermute(edge(COLS - 1), ("x", "c"), right_way)
    right = lax.ppermute(edge(0), ("x", "c"), [(b, a) for a, b in right_way])
    top, first_bias = after(top, b_in)
    adapter_arrays = bring(
        [
            w_in, first_bias, w_conv.reshape(9, C, C), condition, latent.reshape(CELLS, C),
            b_conv, w_out, b_out, w_query, w_key, w_value,
        ],
        "load_adapter",
    )
    (w_in_here, b_in_here, taps_here, condition_here, latent_here, b_conv_here) = adapter_arrays[:6]
    (w_out_here, b_out_here, w_query_here, w_key_here, w_value_here) = adapter_arrays[6:]

    rows, mixed, smooth, slope, cond = call(
        adapter_kernel,
        (
            out(ITEMS, HEADS, PART, LANES),
            out(CELLS, C, dtype=f32),
            out(CELLS, C),
            out(CELLS, C, dtype=f32),
            out(9, CELLS, WIDE),
        ),
        (
            place, valid_rows, condition_here, top, bottom, left, right, latent_here, w_in_here,
            b_in_here, taps_here, b_conv_here, w_out_here, b_out_here, w_query_here, w_key_here,
            w_value_here,
        ),
        "adapter",
        scalars=2,
        scratch=[pltpu.VMEM((WIDE, C), bf16)],
        vmem=24,
        store=(1, 2, 3, 4),
        near=(0,),
        held=(2,) + tuple(range(7, 17)),
    )

    own = across(rows.reshape(CHIPS, PART, LANES)).reshape(HALF, LANES)
    other = swap(own)
    packed, full, probs = call(
        attend_kernel,
        (
            out(CHIPS, PART // 2, LANES),
            out(HALF, LANES, dtype=f32),
            out(HALF, 2 * HALF),
        ),
        (own, other),
        "attend",
        scratch=[
            pltpu.VMEM((2 * HALF, BLOCK), f32),
            pltpu.VMEM((2 * HALF, BLOCK), f32),
            pltpu.VMEM((2 * HALF, BLOCK), bf16),
            pltpu.VMEM((2 * HALF, BLOCK), bf16),
            pltpu.VMEM((BLOCK, 2 * HALF), bf16),
            pltpu.VMEM((BLOCK, 2 * HALF), bf16),
            pltpu.VMEM((LANES, 2 * HALF), bf16),
            pltpu.VMEM((LANES, HALF), bf16),
            pltpu.VMEM((LANES, HALF), f32),
            pltpu.SemaphoreType.DMA((2,)),
        ],
        vmem=32,
        store=(0, 1),
        far=(4,),
    )

    packed, text, attn_weight = after(packed, text_states, w_attn_out)
    text_keys, text_values = call(
        text_kernel,
        (out(ITEMS, TEXT, C), out(ITEMS, TEXT, C)),
        (text.transpose(1, 0, 2).reshape(-1, text.shape[2]), w_cross_key.T, w_cross_value.T),
        "text",
        fetch=(0, 1, 2),
        store=(0, 1),
    )
    (w_attn_spread,) = bring(
        [], "spread", spread_kernel, (out(HEADS * LANES, 768),), (attn_weight,)
    )
    heads_in = across(packed).reshape(ITEMS, HEADS, PART // 2, LANES)
    result, grad_first, heads_out = call(
        middle_kernel,
        (out(CELLS, C), out(CELLS, C, dtype=f32), out(ITEMS, HEADS, PART // 2, LANES)),
        (
            text_lengths, heads_in, mixed, cotangent.reshape(CELLS, C), text_keys, text_values,
            w_attn_spread, b_attn_out, w_cross_query, w_cross_out, b_cross_out, w_ff_in, b_ff_in,
            w_ff_out.T, b_ff_out,
        ),
        "middle",
        scalars=1,
        scratch=[pltpu.VMEM((ITEMS, HEADS * PART, TEXT), f32)],
        vmem=32,
        fetch=(2, 7, 8, 4, 5, 9, 10, 3, 11, 12, 13, 14),
        store=(0, 1, 2),
        held=(6,),
    )

    heads_out, own_again = after(heads_out, own)
    keys_turned, query_turned = bring(
        [],
        "turn",
        turn_kernel,
        (out(LANES, 2 * HALF), out(LANES, HALF)),
        (own_again, other),
    )
    grads_in = across(heads_out.reshape(CHIPS, PART // 2, LANES))
    own_grads, other_grads = call(
        attend_back_kernel,
        (out(HALF, LANES, dtype=f32), out(HALF, LANES)),
        (keys_turned, query_turned, full, grads_in, probs),
        "attend_back",
        scratch=[
            pltpu.VMEM((HALF, LANES), bf16),
            pltpu.VMEM((LANES, 2 * HALF), bf16),
            pltpu.VMEM((LANES, 2 * HALF), f32),
            pltpu.VMEM((2 * HALF, WIDE_BLOCK), bf16),
            pltpu.VMEM((WIDE_BLOCK, 2 * HALF), bf16),
            pltpu.VMEM((WIDE_BLOCK, 2 * HALF), bf16),
            pltpu.SemaphoreType.DMA((2,)),
        ],
        vmem=36,
        near=(0, 1),
        held=(0, 1),
        fetch=(2,),
        far=(4,),
    )
    row_grads = (own_grads + swap(other_grads).astype(f32)).astype(bf16)

    row_grads, query_weight = after(row_grads, w_query)
    mixed_here, grad_here, w_out_here, slope_here, smooth_here, w_joined = bring(
        [mixed, grad_first, w_out, slope, smooth],
        "load_finish",
        join_kernel,
        (out(C, HEADS * LANES),),
        (query_weight, w_key, w_value),
    )
    row_grads = across(row_grads.reshape(CHIPS, PART, LANES))
    latent_grad, parts = call(
        finish_kernel,
        (out(CELLS, C, dtype=f32), out(2, SUM_ROWS, LANES)),
        (
            place, row_grads.reshape(ITEMS, HEADS, PART, LANES), w_joined, mixed_here, grad_here,
            slope_here, smooth_here, cond, w_out_here,
        ),
        "finish",
        scalars=1,
        store=(0,),
        fetch=(7,),
        held=(2, 3, 4, 5, 6, 8),
    )

    shares = (parts[0].astype(f32) + swap(parts[1]).astype(f32)).astype(bf16)
    shares, last_bias = after(shares, b_in)
    taps_last, w_turned = bring(
        [w_conv.reshape(9, C, C)],
        "load_weights",
        widen_kernel,
        (out(C, WIDE),),
        (w_in, last_bias),
    )
    shares = across(shares.reshape(CHIPS, SUM_ROWS // CHIPS, LANES))
    share = jnp.sum(shares.astype(f32), axis=0).astype(bf16)
    mine = across(jnp.broadcast_to(share[None], shares.shape)).reshape(SUM_ROWS, LANES)
    theirs = swap(mine)
    grad_w_in, grad_b_in, grad_w_conv, grad_b_conv, grad_w_out, grad_b_out = call(
        weights_kernel,
        (
            out(CIN, C, dtype=f32),
            out(C, dtype=f32),
            out(9, C, C, dtype=f32),
            out(C, dtype=f32),
            out(C, C, dtype=f32),
            out(C, dtype=f32),
        ),
        (place, mine, theirs, w_turned, taps_last),
        "weights",
        scalars=1,
        scratch=[
            pltpu.VMEM((2, SUM_ROWS, LANES), bf16),
            pltpu.VMEM((9, C, C), f32),
            pltpu.SemaphoreType.DMA((9,)),
        ],
        vmem=24,
        store=(0, 4),
        far=(7,),
        held=(3, 4),
    )
    grid = (ITEMS, ROWS, COLS, C)
    return (
        result.reshape(grid),
        latent_grad.reshape(grid),
        grad_w_in,
        grad_b_in,
        grad_w_conv.reshape(3, 3, C, C),
        grad_b_conv,
        grad_w_out,
        grad_b_out,
    )


def solution(mesh):
    split = Mesh(mesh.devices.reshape(16, 4, 2), ("sp", "x", "c"))
    cells = P(None, "sp", ("x", "c"), None)
    in_specs = (cells, cells) + (P(),) * 23 + (cells,)
    out_specs = (cells, cells) + (P(),) * 6
    return jax.shard_map(
        per_device, mesh=split, in_specs=in_specs, out_specs=out_specs, check_vma=False
    )
```

```python
import jax
import jax.numpy as jnp
from jax import lax
from jax.experimental import pallas as pl
from jax.experimental.pallas import tpu as pltpu
from jax.sharding import Mesh
from jax.sharding import PartitionSpec as P

ITEMS, ROWS, COLS, C, CIN, HEADS, HEAD, FF = 8, 4, 8, 320, 192, 8, 40, 1280
CELLS = ITEMS * ROWS * COLS
PART = ROWS * COLS
CHIPS = 64
HALF = CHIPS * PART
TEXT = 80
LANES = 128
WIDE = 256
GROUP = 160
SCALE = HEAD**-0.5
LOG2E = 1.4426950408889634
EPS = 1e-5
MASKED = -1e30
KEY, VALUE, MASK = HEAD, 2 * HEAD, 3 * HEAD
ACROSS = ("sp", "x")
SUM_ROWS = 3072

bf16, f32 = jnp.bfloat16, jnp.float32
NT = (((1,), (1,)), ((), ()))


def dot(left, right):
    return jnp.dot(left, right, preferred_element_type=f32)


def dot_nt(left, right):
    return lax.dot_general(left, right, NT, preferred_element_type=f32)


def lane_of(shape):
    return lax.broadcasted_iota(jnp.int32, shape, len(shape) - 1)


def moments(values):
    center = values - jnp.mean(values, -1, keepdims=True)
    rate = lax.rsqrt(jnp.mean(center * center, -1, keepdims=True) + EPS)
    return center * rate, rate


def norm_back(unit, rate, grads):
    return rate * (
        grads
        - jnp.mean(grads, -1, keepdims=True)
        - unit * jnp.mean(grads * unit, -1, keepdims=True)
    )


class Fetched:
    def __init__(self, source, buffer, semaphore):
        self.copy = pltpu.make_async_copy(source, buffer, semaphore)
        self.buffer, self.shape, self.here = buffer, buffer.shape, False
        self.copy.start()

    def __getitem__(self, index):
        if not self.here:
            self.copy.wait()
            self.here = True
        return self.buffer[index]


class Stored:
    def __init__(self, target, buffer, semaphore):
        self.copy = pltpu.make_async_copy(buffer, target, semaphore)
        self.buffer, self.started = buffer, False

    def __setitem__(self, index, values):
        self.buffer[index] = values
        if index is Ellipsis:
            self.start()

    def start(self):
        if not self.started:
            self.copy.start()
            self.started = True


def call(kernel, outs, ins, name, scalars=0, scratch=(), vmem=16, fetch=(), store=(), far=(),
    near=(), held=(),
):
    fetch, store = list(fetch), list(store)
    far_in = [i for i in far if i < len(ins)]
    far_out = [i - len(ins) for i in far if i >= len(ins)]

    def body(*refs):
        refs = list(refs)
        given, refs = refs[: len(ins)], refs[len(ins) :]
        made, refs = refs[: len(outs)], refs[len(outs) :]
        own, refs = refs[: len(scratch)], refs[len(scratch) :]
        buffers, semaphores = refs[:-1], refs[-1] if refs else None
        for n, i in enumerate(fetch):
            given[i] = Fetched(given[i], buffers[n], semaphores.at[n])
        kept = []
        for n, i in enumerate(store, len(fetch)):
            made[i] = Stored(made[i], buffers[n], semaphores.at[n])
            kept.append(made[i])
        kernel(*given, *made, *own)
        for part in given:
            if isinstance(part, Fetched) and not part.here:
                part.copy.wait()
        for part in kept:
            part.start()
        for part in kept:
            part.copy.wait()

    def made_as(i, made):
        if i in store or i in far_out:
            return pltpu.HBM(made.shape, made.dtype)
        return pltpu.VMEM(made.shape, made.dtype) if i in near else made

    def in_spec(i):
        if i < scalars:
            return pl.BlockSpec(memory_space=pltpu.SMEM)
        space = pltpu.HBM if i in fetch or i in far_in else pltpu.VMEM
        return pl.BlockSpec(memory_space=space)

    def out_spec(i):
        space = pltpu.HBM if i in store or i in far_out else pltpu.VMEM
        return pl.BlockSpec(memory_space=space)

    extra = [pltpu.VMEM(ins[i].shape, ins[i].dtype) for i in fetch]
    extra += [pltpu.VMEM(outs[i].shape, outs[i].dtype) for i in store]
    if extra:
        extra.append(pltpu.SemaphoreType.DMA((len(extra),)))
    return pl.pallas_call(
        body,
        out_shape=tuple(made_as(i, made) for i, made in enumerate(outs)),
        in_specs=[in_spec(i) for i in range(len(ins))],
        out_specs=tuple(out_spec(i) for i in range(len(outs))),
        scratch_shapes=list(scratch) + extra,
        compiler_params=pltpu.CompilerParams(vmem_limit_bytes=vmem << 20),
        name=name,
    )(
        *(
            pltpu.with_memory_space_constraint(x, pltpu.HBM)
            if i in fetch or i in far_in
            else (pltpu.with_memory_space_constraint(x, pltpu.VMEM) if i in held else x)
            for i, x in enumerate(ins)
        )
    )


def bring(arrays, name, kernel=None, made=(), near=()):
    count, given = len(arrays), len(near)

    def body(*refs):
        sources, inputs = refs[:count], refs[count : count + given]
        targets = refs[count + given : -1]
        copies = [
            pltpu.make_async_copy(sources[n], targets[n], refs[-1].at[n]) for n in range(count)
        ]
        for copy in copies:
            copy.start()
        if kernel is not None:
            kernel(*inputs, *targets[count:])
        for copy in copies:
            copy.wait()

    shapes = [jax.ShapeDtypeStruct(x.shape, x.dtype) for x in arrays] + list(made)
    return pl.pallas_call(
        body,
        out_shape=tuple(pltpu.VMEM(x.shape, x.dtype) for x in shapes),
        in_specs=[pl.BlockSpec(memory_space=pltpu.HBM)] * count
        + [pl.BlockSpec(memory_space=pltpu.VMEM)] * given,
        out_specs=(pl.BlockSpec(memory_space=pltpu.VMEM),) * len(shapes),
        scratch_shapes=[pltpu.SemaphoreType.DMA((max(count, 1),))],
        compiler_params=pltpu.CompilerParams(vmem_limit_bytes=8 << 20),
        name=name,
    )(*(pltpu.with_memory_space_constraint(x, pltpu.HBM) for x in arrays), *near)


def after(value, *arrays):
    return lax.optimization_barrier((value,) + arrays)


def out(*shape, dtype=bf16):
    return jax.ShapeDtypeStruct(shape, dtype)


def bias_rows(bias):
    row = lax.broadcasted_iota(jnp.int32, (WIDE - CIN, C), 0)
    rest = jnp.broadcast_to(bias, (WIDE - CIN, C))
    rows = jnp.zeros((WIDE - CIN, C), f32)
    for n in range(3):
        piece = rest.astype(bf16).astype(f32)
        rows = jnp.where(row == n, piece, rows)
        rest = rest - piece
    return rows.astype(bf16)


def adapter_kernel(
    place, valid, center, top, bottom, left, right, latent, w_in, b_in, w_conv, b_conv, w_out,
    b_out, w_query, w_key, w_value, rows_out, mixed_out, smooth_out, slope_out, cond_out,
    w_wide,
):
    span = ITEMS * (ROWS + 2)
    w_wide[:CIN, :] = w_in[...]
    w_wide[CIN:, :] = bias_rows(b_in[...])

    def widen(values):
        blank = jnp.zeros(values.shape[:-1] + (WIDE - CIN,), f32)
        return jnp.concatenate([values.astype(f32), blank], axis=-1)

    block = jnp.concatenate([top[...], center[...], bottom[...]], axis=1)
    block = widen(block.reshape(span, COLS, CIN))
    shape = (ITEMS, ROWS + 2, COLS, WIDE)
    row = lax.broadcasted_iota(jnp.int32, shape, 1) + ROWS * place[0] - 1
    inside = (row >= 0) & (row < ROWS * 16)
    inside = jnp.where(inside, 1.0, 0.0).reshape(span, COLS, WIDE)
    lane = lane_of((span, COLS, WIDE))
    col = lax.broadcasted_iota(jnp.int32, (span, COLS, WIDE), 1)
    at = COLS * place[2]
    edges = []
    for n, side in enumerate((left, right)):
        there = (at > 0) if n == 0 else (at < COLS * 7)
        edges.append((widen(side[...]).reshape(span, 1, WIDE), jnp.where(there, inside, 0.0)))
    near = jnp.where(col == 0, edges[0][0], pltpu.roll(block, 1, 1))
    near_inside = jnp.where(col == 0, edges[0][1], inside)
    far = jnp.where(col == COLS - 1, edges[1][0], pltpu.roll(block, COLS - 1, 1))
    far_inside = jnp.where(col == COLS - 1, edges[1][1], inside)
    inner = jnp.zeros((CELLS, C), f32)
    start_here = None
    one = (lane >= CIN) & (lane < CIN + 3)
    moves = ((near, near_inside), (block, inside), (far, far_inside))
    for j, (moved, present) in enumerate(moves):
        moved = jnp.where(one, present, moved)
        start = dot(moved.reshape(span * COLS, WIDE).astype(bf16), w_wide[...])
        start = start.reshape(ITEMS, ROWS + 2, COLS, C)
        moved = moved.reshape(ITEMS, ROWS + 2, COLS, WIDE)
        for i in range(3):
            patch = start[:, i : i + ROWS].reshape(CELLS, C).astype(bf16)
            if i == 1 and j == 1:
                start_here = patch.astype(f32)
            inner += dot(patch, w_conv[3 * i + j])
            cond_out[3 * i + j] = moved[:, i : i + ROWS].reshape(CELLS, WIDE).astype(bf16)
    inner += b_conv[...]
    gate = jax.nn.sigmoid(inner)
    smooth = (inner * gate).astype(bf16)
    smooth_out[...] = smooth
    slope_out[...] = gate * (1.0 + inner * (1.0 - gate))
    mixed = latent[...].astype(f32) + (start_here + dot(smooth, w_out[...]) + b_out[...])
    mixed_out[...] = mixed
    normed = moments(mixed)[0].astype(bf16)
    projected = [dot(normed, w[...]) for w in (w_query, w_key, w_value)]
    projected[0] *= SCALE * LOG2E
    lane = lane_of((PART, LANES - MASK))
    row = lax.broadcasted_iota(jnp.int32, (PART, LANES - MASK), 0) // COLS + ROWS * place[0]
    extras = []
    for item in range(ITEMS):
        hidden = jnp.where(row >= valid[item], MASKED, 0.0)
        extras.append(jnp.where(lane == 0, hidden, 1.0))
    extras = jnp.concatenate(extras, axis=0)
    for head in range(HEADS):
        at = slice(head * HEAD, (head + 1) * HEAD)
        joined = jnp.concatenate([part[:, at] for part in projected] + [extras], axis=1)
        rows_out[:, head] = joined.astype(bf16).reshape(ITEMS, PART, LANES)


def text_kernel(
    text, w_key_turned, w_value_turned, keys_out, values_out, wide_key, wide_value
):
    count = text.shape[0]
    token = lax.broadcasted_iota(jnp.int32, (TEXT, count), 0)
    place = lane_of((TEXT, count))
    blank = jnp.zeros((WIDE - GROUP, text.shape[1]), bf16)
    for source, wide in ((w_key_turned, wide_key), (w_value_turned, wide_value)):
        for g in range(2):
            wide[g * WIDE : g * WIDE + GROUP, :] = source[g * GROUP : (g + 1) * GROUP, :]
            wide[g * WIDE + GROUP : (g + 1) * WIDE, :] = blank
    text[:16]

    def body(item, carry):
        pick = jnp.where(place == token * ITEMS + item, 1.0, 0.0).astype(bf16)
        states = dot(pick, text[...]).astype(bf16)
        keys_out.buffer[item] = dot_nt(states, wide_key[...]).astype(bf16)
        values_out.buffer[item] = dot_nt(states, wide_value[...]).astype(bf16)
        return carry

    lax.fori_loop(0, ITEMS, body, 0)
    keys_out.start()
    values_out.start()


def form_kernel(w_query, w_cross_out, w_attn, query_out, cross_out, spread_out):
    rows = w_query[...].astype(f32)
    blank = jnp.zeros((C, WIDE - GROUP), f32)
    rows = [rows[:, :GROUP], blank, rows[:, GROUP:], blank]
    query_out[...] = jnp.concatenate(rows, axis=1).astype(bf16)
    rows = w_cross_out[...]
    blank = jnp.zeros((WIDE - GROUP, C), bf16)
    cross_out[...] = jnp.concatenate([rows[:GROUP], blank, rows[GROUP:], blank], axis=0)
    rows = w_attn[...].astype(f32)
    gap = jnp.zeros((HEAD, 384 - C), f32)
    for head in range(HEADS):
        part = jnp.concatenate([rows[head * HEAD : (head + 1) * HEAD], gap], axis=1)
        blank = jnp.zeros_like(part)
        block = jnp.concatenate(
            [
                jnp.concatenate([part, blank], axis=1),
                jnp.concatenate([blank, part], axis=1),
                jnp.zeros((LANES - 2 * HEAD, 768), f32),
            ],
            axis=0,
        )
        spread_out[head * LANES : (head + 1) * LANES, :] = block.astype(bf16)


BLOCK = 256
STEP = 512


def attend_kernel(
    own, other, packed_out, full_out, probs_out,
    scores_a, scores_b, probs_a, probs_b, turned_a, turned_b, keys_turned, query, output, sems,
):
    count = HALF // BLOCK
    keys_turned[:, :HALF] = jnp.transpose(own[...])
    keys_turned[:, HALF:] = jnp.transpose(other[...])
    lane = lane_of((HALF, LANES))
    rows = pltpu.roll(own[...].astype(f32), KEY, 1)
    rows = jnp.where((lane >= KEY) & (lane < VALUE), rows, jnp.where(lane == MASK, 1.0, 0.0))
    query[...] = jnp.transpose(rows.astype(bf16))
    chunks = [(ref, at) for ref in (own, other) for at in range(0, HALF, STEP)]

    def columns(b):
        return pl.ds(pl.multiple_of(b * BLOCK, BLOCK), BLOCK)

    def score(queries, n, scores, peak):
        ref, at = chunks[n]
        part = dot(ref[at : at + STEP, :], queries)
        scores[n * STEP : (n + 1) * STEP, :] = part
        part = jnp.max(part.reshape(STEP // 8, 8, BLOCK), axis=0)
        return part if peak is None else jnp.maximum(peak, part)

    def sent(b, turned, n):
        return pltpu.make_async_copy(turned, probs_out.at[columns(b)], sems.at[n])

    def half(b, peak, following, scores, probs, turned):
        shift = jnp.max(peak, axis=0, keepdims=True)
        queries = query[:, columns(jnp.minimum(b + 1, count - 1))]
        ahead = None
        for n in range(len(chunks)):
            ahead = score(queries, n, following, ahead)
            keys = slice(n * STEP, (n + 1) * STEP)
            part = jnp.exp2(scores[keys, :] - shift).astype(bf16)
            probs[keys, :] = part
            turned[:, keys] = jnp.transpose(part)
        output[:, columns(b)] = dot(keys_turned[...], probs[...])
        return ahead

    peak = None
    for n in range(len(chunks)):
        peak = score(query[:, :BLOCK], n, scores_a, peak)

    def body(i, peak):
        @pl.when(i > 0)
        def _():
            sent(2 * i - 2, turned_a, 0).wait()

        peak = half(2 * i, peak, scores_b, scores_a, probs_a, turned_a)
        sent(2 * i, turned_a, 0).start()

        @pl.when(i > 0)
        def _():
            sent(2 * i - 1, turned_b, 1).wait()

        peak = half(2 * i + 1, peak, scores_a, scores_b, probs_b, turned_b)
        sent(2 * i + 1, turned_b, 1).start()
        return peak

    lax.fori_loop(0, count // 2, body, peak)
    total = output[...]
    inverse = 1.0 / total[MASK + 1 : MASK + 2, :]
    row = lax.broadcasted_iota(jnp.int32, (LANES, HALF), 0)
    total = jnp.transpose(jnp.where(row == 0, inverse, total * inverse))
    full_out[...] = total
    pairs = total.reshape(CHIPS, 2, PART // 2, LANES)
    lane = lane_of((HALF // 2, LANES))
    low = pltpu.roll(pairs[:, 0].reshape(HALF // 2, LANES), LANES - VALUE, 1)
    high = pltpu.roll(pairs[:, 1].reshape(HALF // 2, LANES), LANES - VALUE + HEAD, 1)
    packed = jnp.where(lane < HEAD, low, jnp.where(lane < 2 * HEAD, high, 0.0))
    packed_out[...] = packed.astype(bf16).reshape(CHIPS, PART // 2, LANES)
    sent(count - 2, turned_a, 0).wait()
    sent(count - 1, turned_b, 1).wait()


def middle_kernel(
    lengths, heads_in, mixed, cotangent, text_keys, text_values, w_attn, b_attn, w_cross_query,
    w_cross_out, b_cross, w_ff_in, b_ff_in, w_ff_turned, b_ff_out, result_out, grad_out, heads_out,
    probs_keep,
):
    half = CELLS // 2
    split = w_attn.shape[1] // 2
    packed = jnp.concatenate(
        [heads_in[:, head].reshape(half, LANES) for head in range(HEADS)], axis=1
    )
    both = dot(packed, w_attn[...])
    shape = (ITEMS, 1, PART // 2, C)
    attended = jnp.concatenate(
        [both[:, :C].reshape(shape), both[:, split : split + C].reshape(shape)], axis=1
    ).reshape(CELLS, C)
    first = mixed[...] + attended + b_attn[...]
    unit_two, rate_two = moments(first)
    cross_query = dot(unit_two.astype(bf16), w_cross_query[...]).astype(bf16)
    lane = lane_of((PART, WIDE))
    in_head = [(lane >= HEAD * h) & (lane < HEAD * (h + 1)) for h in range(HEADS // 2)]
    groups = [slice(0, WIDE), slice(WIDE, 2 * WIDE)]
    half_rows = HEADS * PART // 2

    def by_head(values, others):
        parts = []
        for lanes in groups:
            here = values[:, lanes]
            rows = [jnp.where(mask, here, jnp.zeros_like(here)) for mask in in_head]
            parts.append(dot_nt(jnp.concatenate(rows, axis=0), others[:, lanes]))
        return jnp.concatenate(parts, axis=0)

    def by_cell(weights, others):
        parts = []
        for g, lanes in enumerate(groups):
            rows = dot(weights[g * half_rows : (g + 1) * half_rows], others[:, lanes])
            total = jnp.zeros((PART, WIDE), f32)
            for h, mask in enumerate(in_head):
                total = jnp.where(mask, rows[h * PART : (h + 1) * PART], total)
            parts.append(total)
        return jnp.concatenate(parts, axis=1)

    token = lane_of((HEADS * PART, TEXT))
    outs = []
    for item in range(ITEMS):
        cells = slice(item * PART, (item + 1) * PART)
        scores = by_head(cross_query[cells], text_keys[item]) * SCALE
        scores = jnp.where(token < lengths[item], scores, MASKED)
        weights = jnp.exp(scores - jnp.max(scores, -1, keepdims=True))
        probs = weights / jnp.sum(weights, -1, keepdims=True)
        probs_keep[item] = probs
        outs.append(by_cell(probs.astype(bf16), text_values[item]))
    cross = jnp.concatenate(outs, axis=0).astype(bf16)
    second = first + dot(cross, w_cross_out[...]) + b_cross[...]
    unit_three, rate_three = moments(second)
    normed_three = unit_three.astype(bf16)
    upstream = cotangent[...]
    result = second + b_ff_out[...]
    grad_normed = jnp.zeros((CELLS, C), f32)
    step = 256
    for at in range(0, FF, step):
        values, gates = slice(at, at + step), slice(FF + at, FF + at + step)
        value = dot(normed_three, w_ff_in[:, values]) + b_ff_in[values]
        gate = dot(normed_three, w_ff_in[:, gates]) + b_ff_in[gates]
        normal = 0.5 + 0.5 * lax.erf(gate * (0.5**0.5))
        density = jnp.exp(gate * gate * -0.5) * 0.3989422804014327
        gelu = gate * normal
        result += dot_nt((value * gelu).astype(bf16), w_ff_turned[:, values])
        grad_act = dot(upstream, w_ff_turned[:, values])
        grad_value = (grad_act * gelu).astype(bf16)
        grad_gate = (grad_act * value * (normal + gate * density)).astype(bf16)
        grad_normed += dot_nt(grad_value, w_ff_in[:, values])
        grad_normed += dot_nt(grad_gate, w_ff_in[:, gates])
    result_out[...] = result.astype(bf16)
    grad_second = upstream.astype(f32) + norm_back(unit_three, rate_three, grad_normed)
    grad_cross = dot_nt(grad_second.astype(bf16), w_cross_out[...]).astype(bf16)
    outs = []
    for item in range(ITEMS):
        cells = slice(item * PART, (item + 1) * PART)
        grad_probs = by_head(grad_cross[cells], text_values[item])
        probs = probs_keep[item]
        weighted = jnp.sum(probs * grad_probs, -1, keepdims=True)
        grad_scores = (probs * (grad_probs - weighted)).astype(bf16)
        outs.append(by_cell(grad_scores, text_keys[item]))
    grad_query = (jnp.concatenate(outs, axis=0) * SCALE).astype(bf16)
    grad_first = grad_second + norm_back(
        unit_two, rate_two, dot_nt(grad_query, w_cross_query[...])
    )
    grad_out[...] = grad_first
    pairs = grad_first.reshape(ITEMS, 2, PART // 2, C)
    gap = jnp.zeros((half, split - C), f32)
    both = jnp.concatenate(
        [pairs[:, 0].reshape(half, C), gap, pairs[:, 1].reshape(half, C), gap], axis=1
    ).astype(bf16)
    packed = dot_nt(both, w_attn[...]).astype(bf16)
    for head in range(HEADS):
        piece = packed[:, head * LANES : (head + 1) * LANES]
        heads_out[:, head] = piece.reshape(ITEMS, PART // 2, LANES)


WIDE_BLOCK = 512
WIDE_STEP = 1024


def turn_kernel(own, other, keys_out, query_out):
    keys_out[:, :HALF] = jnp.transpose(own[...])
    keys_out[:, HALF:] = jnp.transpose(other[...])
    lane = lane_of((HALF, LANES))
    query = pltpu.roll(own[...].astype(f32), KEY, 1)
    query = jnp.where((lane >= KEY) & (lane < VALUE), query, 0.0).astype(bf16)
    query_out[...] = jnp.transpose(query)


def attend_back_kernel(
    keys_turned, query_turned, full, packed, probs_in, own_out, other_out,
    grads, left, sums, scores, probs_a, probs_b, sems,
):
    half, count = HALF // 2, HALF // WIDE_BLOCK

    def block(b):
        return pl.ds(pl.multiple_of(b * WIDE_BLOCK, WIDE_BLOCK), WIDE_BLOCK)

    def fetched(b, probs, n):
        return pltpu.make_async_copy(probs_in.at[block(b)], probs, sems.at[n])

    fetched(0, probs_a, 0).start()
    fetched(1, probs_b, 1).start()
    lane = lane_of((half, LANES))
    value_lane = (lane >= VALUE) & (lane < MASK)
    pairs = packed[...].reshape(half, LANES).astype(f32)
    low = jnp.where(value_lane, pltpu.roll(pairs, VALUE, 1), 0.0)
    high = jnp.where(value_lane, pltpu.roll(pairs, VALUE - HEAD, 1), 0.0)
    shape = (CHIPS, 1, PART // 2, LANES)
    upstream = jnp.concatenate([low.reshape(shape), high.reshape(shape)], axis=1)
    upstream = upstream.reshape(HALF, LANES)
    lane = lane_of((HALF, LANES))
    outputs = full[...]
    upstream *= jnp.sum(jnp.where(lane == 0, outputs, 0.0), axis=1, keepdims=True)
    weighted = jnp.sum(upstream * outputs, axis=1, keepdims=True)
    first = weighted.astype(bf16).astype(f32)
    upstream = jnp.where(lane == MASK + 4, -first, upstream)
    upstream = jnp.where(lane == MASK + 5, first - weighted, upstream).astype(bf16)
    grads[...] = upstream
    for b in range(count):
        rows, at = slice(b * WIDE_BLOCK, (b + 1) * WIDE_BLOCK), 2 * b * WIDE_BLOCK
        left[:, at : at + WIDE_BLOCK] = query_turned[:, rows]
        left[:, at + WIDE_BLOCK : at + 2 * WIDE_BLOCK] = jnp.transpose(upstream[rows])
    sums[...] = jnp.zeros_like(sums)

    def work(b, probs):
        rows = block(b)
        upstream = grads[rows, :]
        both = left[:, pl.ds(pl.multiple_of(2 * b * WIDE_BLOCK, 2 * WIDE_BLOCK), 2 * WIDE_BLOCK)]
        for at in range(0, 2 * HALF, WIDE_STEP):
            keys = slice(at, at + WIDE_STEP)
            part = probs[:, keys]
            grad = dot(upstream, keys_turned[:, keys])
            grad = (part.astype(f32) * grad).astype(bf16)
            sums[:, keys] += dot(both, jnp.concatenate([grad, part], axis=0))
            scores[keys, :] = jnp.transpose(grad)
        grad_query = jnp.transpose(dot(keys_turned[...], scores[...])) * SCALE
        own_out[rows, :] = pltpu.roll(grad_query, LANES - KEY, 1)

    def body(i, carry):
        fetched(2 * i, probs_a, 0).wait()
        work(2 * i, probs_a)

        @pl.when(2 * i + 2 < count)
        def _():
            fetched(2 * i + 2, probs_a, 0).start()

        fetched(2 * i + 1, probs_b, 1).wait()
        work(2 * i + 1, probs_b)

        @pl.when(2 * i + 3 < count)
        def _():
            fetched(2 * i + 3, probs_b, 1).start()

        return carry

    lax.fori_loop(0, count // 2, body, 0)
    scale = jnp.where(lane < VALUE, 1.0 / LOG2E, 1.0)
    rest = jnp.where(lane < MASK, jnp.transpose(sums[:, :HALF]) * scale, 0.0)
    own_out[...] = jnp.where(lane < KEY, own_out[...], rest)
    rest = jnp.where(
        (lane >= KEY) & (lane < MASK), jnp.transpose(sums[:, HALF:]) * scale, 0.0
    )
    other_out[...] = rest.astype(bf16)


def join_kernel(w_query, w_key, w_value, joined_out):
    blank = jnp.zeros((C, LANES - MASK), f32)
    parts = [w[...].astype(f32) for w in (w_query, w_key, w_value)]
    for head in range(HEADS):
        at = slice(head * HEAD, (head + 1) * HEAD)
        joined = jnp.concatenate([part[:, at] for part in parts] + [blank], axis=1)
        joined_out[:, head * LANES : (head + 1) * LANES] = joined.astype(bf16)


def widen_kernel(w_in, b_in, turned_out):
    wide = jnp.concatenate([w_in[...], bias_rows(b_in[...])], axis=0)
    turned_out[...] = jnp.transpose(wide)


def finish_kernel(
    place, rows, w_qkv, mixed, grad_first, slope, smooth, cond, w_out, latent_out, parts_out
):
    joined = jnp.concatenate(
        [rows[:, head].reshape(CELLS, LANES) for head in range(HEADS)], axis=1
    )
    unit, rate = moments(mixed[...])
    latent = grad_first[...] + norm_back(unit, rate, dot_nt(joined, w_qkv[...]))
    latent_out[...] = latent
    branch = latent.astype(bf16)
    inner = (dot_nt(branch, w_out[...]) * slope[...]).astype(bf16)
    inner_turned = jnp.transpose(inner)
    branch_turned = jnp.transpose(branch)
    here, there = place[1], 1 - place[1]

    def put(side, at, values):
        values = values.astype(bf16)
        for t in range(0, 3 * LANES, LANES):
            parts_out[side, at : at + C, :] = values[:, t : t + LANES]
            at += C

    lane = lane_of((C, LANES))
    ones = jnp.zeros((C, LANES), f32)
    kept = None
    for n in range(10):
        moment = dot(inner_turned, cond[n]) if n < 9 else dot(branch_turned, cond[4])
        one = pltpu.roll(moment[:, LANES:], 3 * n, 1)
        ones = jnp.where((lane >= 64 + 3 * n) & (lane < 67 + 3 * n), one, ones)
        if n % 2 == 0:
            kept = moment[:, :CIN]
            continue
        both = jnp.concatenate([kept, moment[:, :CIN]], axis=1)
        pair = n // 2
        put(here if pair < 3 else there, 3 * C * (pair % 3), both)
    values = dot(branch_turned, smooth[...])
    last = jnp.concatenate([values[:, 2 * LANES :], ones[:, 64:]], axis=1)
    put(there, 6 * C, jnp.concatenate([values[:, : 2 * LANES], last], axis=1))
    for side in range(2):
        parts_out[side, 9 * C :, :] = jnp.zeros((SUM_ROWS - 9 * C, LANES), bf16)


def weights_kernel(
    place, mine, theirs, w_turned, w_conv, win_out, bin_out, wconv_out, bconv_out, wout_out,
    bout_out, taps, sems,
):
    here = place[1]

    def tile(half, n):
        rows = slice(C * n, C * (n + 1))
        return jnp.where(here == half, mine[rows, :], theirs[rows, :]).astype(f32)

    ones = tile(1, 8)
    lane = lane_of((C, LANES))
    low = lane < 64

    def moment_of(n):
        pair = n // 2
        first, middle, last = [tile(pair // 3, 3 * (pair % 3) + t) for t in range(3)]
        if n % 2:
            middle, last = pltpu.roll(middle, 64, 1), pltpu.roll(last, 64, 1)
            first, middle = jnp.where(low, middle, last), last
        one = jnp.where(lane < 67, pltpu.roll(ones, LANES - 3 * n, 1) if n else ones, 0.0)
        return jnp.concatenate([first, jnp.where(low, middle, one)], axis=1).astype(bf16)

    grad_in = jnp.zeros((C, WIDE), f32)
    copies = []
    for n in range(9):
        moment = moment_of(n)
        taps[n] = dot_nt(w_turned[...], moment)
        copy = pltpu.make_async_copy(taps.at[n], wconv_out.at[n], sems.at[n])
        copy.start()
        copies.append(copy)
        grad_in += dot(w_conv[n], moment)
    last = jnp.concatenate([tile(1, 6), tile(1, 7), ones], axis=1)
    last = jnp.transpose(last)
    wout_out[...] = last[:C]
    bconv_out[...] = last[C + 12]
    bout_out[...] = last[C + 27]
    grad_in = jnp.transpose(grad_in + moment_of(9).astype(f32))
    win_out[...] = grad_in[:CIN]
    bin_out[...] = grad_in[CIN]
    for copy in copies:
        copy.wait()


def swap(array):
    return lax.ppermute(array, "c", [(0, 1), (1, 0)])


def across(blocks):
    return lax.all_to_all(blocks, ACROSS, 0, 0, tiled=True)


def per_device(
    latent, condition, text_states, valid_rows, text_lengths, w_in, b_in, w_conv, b_conv, w_out,
    b_out, w_query, w_key, w_value, w_attn_out, b_attn_out, w_cross_query, w_cross_key,
    w_cross_value, w_cross_out, b_cross_out, w_ff_in, b_ff_in, w_ff_out, b_ff_out, cotangent,
):
    core = lax.axis_index("c")
    place = jnp.stack([lax.axis_index("sp"), core, 2 * lax.axis_index("x") + core])
    place = place.astype(jnp.int32)

    down = [(i, i + 1) for i in range(15)]
    top = lax.ppermute(condition[:, ROWS - 1 :], "sp", down)
    bottom = lax.ppermute(condition[:, :1], "sp", [(b, a) for a, b in down])
    right_way = [(i, i + 1) for i in range(7)]

    def edge(col):
        tall = jnp.concatenate([top[:, :, col], condition[:, :, col], bottom[:, :, col]], axis=1)
        return tall.reshape(ITEMS * (ROWS + 2), CIN)

    left = lax.ppermute(edge(COLS - 1), ("x", "c"), right_way)
    right = lax.ppermute(edge(0), ("x", "c"), [(b, a) for a, b in right_way])
    top, first_bias = after(top, b_in)
    adapter_arrays = bring(
        [
            w_in, first_bias, w_conv.reshape(9, C, C), condition, latent.reshape(CELLS, C),
            b_conv, w_out, b_out, w_query, w_key, w_value,
        ],
        "load_adapter",
    )
    (w_in_here, b_in_here, taps_here, condition_here, latent_here, b_conv_here) = adapter_arrays[:6]
    (w_out_here, b_out_here, w_query_here, w_key_here, w_value_here) = adapter_arrays[6:]

    rows, mixed, smooth, slope, cond = call(
        adapter_kernel,
        (
            out(ITEMS, HEADS, PART, LANES),
            out(CELLS, C, dtype=f32),
            out(CELLS, C),
            out(CELLS, C, dtype=f32),
            out(9, CELLS, WIDE),
        ),
        (
            place, valid_rows, condition_here, top, bottom, left, right, latent_here, w_in_here,
            b_in_here, taps_here, b_conv_here, w_out_here, b_out_here, w_query_here, w_key_here,
            w_value_here,
        ),
        "adapter",
        scalars=2,
        scratch=[pltpu.VMEM((WIDE, C), bf16)],
        vmem=24,
        store=(1, 2, 3, 4),
        near=(0,),
        held=(2,) + tuple(range(7, 17)),
    )

    own = across(rows.reshape(CHIPS, PART, LANES)).reshape(HALF, LANES)
    other = swap(own)
    _, attn_weight = after(own, w_attn_out)
    w_cross_query_wide, w_cross_out_wide, w_attn_spread = call(
        form_kernel,
        (out(C, 2 * WIDE), out(2 * WIDE, C), out(HEADS * LANES, 768)),
        (w_cross_query, w_cross_out, attn_weight),
        "form",
        fetch=(2, 0, 1),
        store=(0, 1),
        near=(2,),
    )
    own, w_attn_spread = after(own, w_attn_spread)
    packed, full, probs = call(
        attend_kernel,
        (
            out(CHIPS, PART // 2, LANES),
            out(HALF, LANES, dtype=f32),
            out(HALF, 2 * HALF),
        ),
        (own, other),
        "attend",
        scratch=[
            pltpu.VMEM((2 * HALF, BLOCK), f32),
            pltpu.VMEM((2 * HALF, BLOCK), f32),
            pltpu.VMEM((2 * HALF, BLOCK), bf16),
            pltpu.VMEM((2 * HALF, BLOCK), bf16),
            pltpu.VMEM((BLOCK, 2 * HALF), bf16),
            pltpu.VMEM((BLOCK, 2 * HALF), bf16),
            pltpu.VMEM((LANES, 2 * HALF), bf16),
            pltpu.VMEM((LANES, HALF), bf16),
            pltpu.VMEM((LANES, HALF), f32),
            pltpu.SemaphoreType.DMA((2,)),
        ],
        vmem=32,
        store=(0, 1),
        far=(4,),
    )

    packed, text = after(packed, text_states)
    text_keys, text_values = call(
        text_kernel,
        (out(ITEMS, TEXT, 2 * WIDE), out(ITEMS, TEXT, 2 * WIDE)),
        (text.transpose(1, 0, 2).reshape(-1, text.shape[2]), w_cross_key.T, w_cross_value.T),
        "text",
        scratch=[pltpu.VMEM((2 * WIDE, text.shape[2]), bf16)] * 2,
        fetch=(1, 2, 0),
        store=(0, 1),
    )
    heads_in = across(packed).reshape(ITEMS, HEADS, PART // 2, LANES)
    result, grad_first, heads_out = call(
        middle_kernel,
        (out(CELLS, C), out(CELLS, C, dtype=f32), out(ITEMS, HEADS, PART // 2, LANES)),
        (
            text_lengths, heads_in, mixed, cotangent.reshape(CELLS, C), text_keys, text_values,
            w_attn_spread, b_attn_out, w_cross_query_wide, w_cross_out_wide, b_cross_out,
            w_ff_in, b_ff_in, w_ff_out.T, b_ff_out,
        ),
        "middle",
        scalars=1,
        scratch=[pltpu.VMEM((ITEMS, HEADS * PART, TEXT), f32)],
        vmem=32,
        fetch=(2, 7, 8, 4, 5, 9, 10, 3, 11, 12, 13, 14),
        store=(0, 1, 2),
        held=(6,),
    )

    heads_out, own_again = after(heads_out, own)
    keys_turned, query_turned = bring(
        [],
        "turn",
        turn_kernel,
        (out(LANES, 2 * HALF), out(LANES, HALF)),
        (own_again, other),
    )
    grads_in = across(heads_out.reshape(CHIPS, PART // 2, LANES))
    own_grads, other_grads = call(
        attend_back_kernel,
        (out(HALF, LANES, dtype=f32), out(HALF, LANES)),
        (keys_turned, query_turned, full, grads_in, probs),
        "attend_back",
        scratch=[
            pltpu.VMEM((HALF, LANES), bf16),
            pltpu.VMEM((LANES, 2 * HALF), bf16),
            pltpu.VMEM((LANES, 2 * HALF), f32),
            pltpu.VMEM((2 * HALF, WIDE_BLOCK), bf16),
            pltpu.VMEM((WIDE_BLOCK, 2 * HALF), bf16),
            pltpu.VMEM((WIDE_BLOCK, 2 * HALF), bf16),
            pltpu.SemaphoreType.DMA((2,)),
        ],
        vmem=36,
        near=(0, 1),
        held=(0, 1),
        fetch=(2,),
        far=(4,),
    )
    row_grads = (own_grads + swap(other_grads).astype(f32)).astype(bf16)

    row_grads, query_weight = after(row_grads, w_query)
    mixed_here, grad_here, w_out_here, slope_here, smooth_here, w_joined = bring(
        [mixed, grad_first, w_out, slope, smooth],
        "load_finish",
        join_kernel,
        (out(C, HEADS * LANES),),
        (query_weight, w_key, w_value),
    )
    row_grads = across(row_grads.reshape(CHIPS, PART, LANES))
    latent_grad, parts = call(
        finish_kernel,
        (out(CELLS, C, dtype=f32), out(2, SUM_ROWS, LANES)),
        (
            place, row_grads.reshape(ITEMS, HEADS, PART, LANES), w_joined, mixed_here, grad_here,
            slope_here, smooth_here, cond, w_out_here,
        ),
        "finish",
        scalars=1,
        store=(0,),
        fetch=(7,),
        held=(2, 3, 4, 5, 6, 8),
    )

    shares = (parts[0].astype(f32) + swap(parts[1]).astype(f32)).astype(bf16)
    shares, last_bias = after(shares, b_in)
    taps_last, w_turned = bring(
        [w_conv.reshape(9, C, C)],
        "load_weights",
        widen_kernel,
        (out(C, WIDE),),
        (w_in, last_bias),
    )
    shares = across(shares.reshape(CHIPS, SUM_ROWS // CHIPS, LANES))
    share = jnp.sum(shares.astype(f32), axis=0).astype(bf16)
    mine = across(jnp.broadcast_to(share[None], shares.shape)).reshape(SUM_ROWS, LANES)
    theirs = swap(mine)
    grad_w_in, grad_b_in, grad_w_conv, grad_b_conv, grad_w_out, grad_b_out = call(
        weights_kernel,
        (
            out(CIN, C, dtype=f32),
            out(C, dtype=f32),
            out(9, C, C, dtype=f32),
            out(C, dtype=f32),
            out(C, C, dtype=f32),
            out(C, dtype=f32),
        ),
        (place, mine, theirs, w_turned, taps_last),
        "weights",
        scalars=1,
        scratch=[
            pltpu.VMEM((9, C, C), f32),
            pltpu.SemaphoreType.DMA((9,)),
        ],
        vmem=24,
        store=(0, 4),
        far=(7,),
        held=(3, 4),
    )
    grid = (ITEMS, ROWS, COLS, C)
    return (
        result.reshape(grid),
        latent_grad.reshape(grid),
        grad_w_in,
        grad_b_in,
        grad_w_conv.reshape(3, 3, C, C),
        grad_b_conv,
        grad_w_out,
        grad_b_out,
    )


def solution(mesh):
    split = Mesh(mesh.devices.reshape(16, 4, 2), ("sp", "x", "c"))
    cells = P(None, "sp", ("x", "c"), None)
    in_specs = (cells, cells) + (P(),) * 23 + (cells,)
    out_specs = (cells, cells) + (P(),) * 6
    return jax.shard_map(
        per_device, mesh=split, in_specs=in_specs, out_specs=out_specs, check_vma=False
    )
```

```python
import jax
import jax.numpy as jnp
from jax import lax
from jax.experimental import pallas as pl
from jax.experimental.pallas import tpu as pltpu
from jax.sharding import Mesh
from jax.sharding import PartitionSpec as P

ITEMS, ROWS, COLS, C, CIN, HEADS, HEAD, FF = 8, 4, 8, 320, 192, 8, 40, 1280
CELLS = ITEMS * ROWS * COLS
PART = ROWS * COLS
CHIPS = 64
HALF = CHIPS * PART
TEXT = 80
LANES = 128
WIDE = 256
GROUP = 160
SCALE = HEAD**-0.5
LOG2E = 1.4426950408889634
EPS = 1e-5
MASKED = -1e30
KEY, VALUE, MASK = HEAD, 2 * HEAD, 3 * HEAD
ACROSS = ("sp", "x")
SUM_ROWS = 3072

bf16, f32 = jnp.bfloat16, jnp.float32
NT = (((1,), (1,)), ((), ()))


def dot(left, right):
    return jnp.dot(left, right, preferred_element_type=f32)


def dot_nt(left, right):
    return lax.dot_general(left, right, NT, preferred_element_type=f32)


def lane_of(shape):
    return lax.broadcasted_iota(jnp.int32, shape, len(shape) - 1)


def moments(values):
    center = values - jnp.mean(values, -1, keepdims=True)
    rate = lax.rsqrt(jnp.mean(center * center, -1, keepdims=True) + EPS)
    return center * rate, rate


def norm_back(unit, rate, grads):
    return rate * (
        grads
        - jnp.mean(grads, -1, keepdims=True)
        - unit * jnp.mean(grads * unit, -1, keepdims=True)
    )


class Fetched:
    def __init__(self, source, buffer, semaphore):
        self.copy = pltpu.make_async_copy(source, buffer, semaphore)
        self.buffer, self.shape, self.here = buffer, buffer.shape, False
        self.copy.start()

    def __getitem__(self, index):
        if not self.here:
            self.copy.wait()
            self.here = True
        return self.buffer[index]


class Stored:
    def __init__(self, target, buffer, semaphore):
        self.copy = pltpu.make_async_copy(buffer, target, semaphore)
        self.buffer, self.started = buffer, False

    def __setitem__(self, index, values):
        self.buffer[index] = values
        if index is Ellipsis:
            self.start()

    def start(self):
        if not self.started:
            self.copy.start()
            self.started = True


def call(kernel, outs, ins, name, scalars=0, scratch=(), vmem=16, fetch=(), store=(), far=(),
    near=(), held=(),
):
    fetch, store = list(fetch), list(store)
    far_in = [i for i in far if i < len(ins)]
    far_out = [i - len(ins) for i in far if i >= len(ins)]

    def body(*refs):
        refs = list(refs)
        given, refs = refs[: len(ins)], refs[len(ins) :]
        made, refs = refs[: len(outs)], refs[len(outs) :]
        own, refs = refs[: len(scratch)], refs[len(scratch) :]
        buffers, semaphores = refs[:-1], refs[-1] if refs else None
        for n, i in enumerate(fetch):
            given[i] = Fetched(given[i], buffers[n], semaphores.at[n])
        kept = []
        for n, i in enumerate(store, len(fetch)):
            made[i] = Stored(made[i], buffers[n], semaphores.at[n])
            kept.append(made[i])
        kernel(*given, *made, *own)
        for part in given:
            if isinstance(part, Fetched) and not part.here:
                part.copy.wait()
        for part in kept:
            part.start()
        for part in kept:
            part.copy.wait()

    def made_as(i, made):
        if i in store or i in far_out:
            return pltpu.HBM(made.shape, made.dtype)
        return pltpu.VMEM(made.shape, made.dtype) if i in near else made

    def in_spec(i):
        if i < scalars:
            return pl.BlockSpec(memory_space=pltpu.SMEM)
        space = pltpu.HBM if i in fetch or i in far_in else pltpu.VMEM
        return pl.BlockSpec(memory_space=space)

    def out_spec(i):
        space = pltpu.HBM if i in store or i in far_out else pltpu.VMEM
        return pl.BlockSpec(memory_space=space)

    extra = [pltpu.VMEM(ins[i].shape, ins[i].dtype) for i in fetch]
    extra += [pltpu.VMEM(outs[i].shape, outs[i].dtype) for i in store]
    if extra:
        extra.append(pltpu.SemaphoreType.DMA((len(extra),)))
    return pl.pallas_call(
        body,
        out_shape=tuple(made_as(i, made) for i, made in enumerate(outs)),
        in_specs=[in_spec(i) for i in range(len(ins))],
        out_specs=tuple(out_spec(i) for i in range(len(outs))),
        scratch_shapes=list(scratch) + extra,
        compiler_params=pltpu.CompilerParams(vmem_limit_bytes=vmem << 20),
        name=name,
    )(
        *(
            pltpu.with_memory_space_constraint(x, pltpu.HBM)
            if i in fetch or i in far_in
            else (pltpu.with_memory_space_constraint(x, pltpu.VMEM) if i in held else x)
            for i, x in enumerate(ins)
        )
    )


def bring(arrays, name, kernel=None, made=(), near=()):
    count, given = len(arrays), len(near)

    def body(*refs):
        sources, inputs = refs[:count], refs[count : count + given]
        targets = refs[count + given : -1]
        copies = [
            pltpu.make_async_copy(sources[n], targets[n], refs[-1].at[n]) for n in range(count)
        ]
        for copy in copies:
            copy.start()
        if kernel is not None:
            kernel(*inputs, *targets[count:])
        for copy in copies:
            copy.wait()

    shapes = [jax.ShapeDtypeStruct(x.shape, x.dtype) for x in arrays] + list(made)
    return pl.pallas_call(
        body,
        out_shape=tuple(pltpu.VMEM(x.shape, x.dtype) for x in shapes),
        in_specs=[pl.BlockSpec(memory_space=pltpu.HBM)] * count
        + [pl.BlockSpec(memory_space=pltpu.VMEM)] * given,
        out_specs=(pl.BlockSpec(memory_space=pltpu.VMEM),) * len(shapes),
        scratch_shapes=[pltpu.SemaphoreType.DMA((max(count, 1),))],
        compiler_params=pltpu.CompilerParams(vmem_limit_bytes=8 << 20),
        name=name,
    )(*(pltpu.with_memory_space_constraint(x, pltpu.HBM) for x in arrays), *near)


def after(value, *arrays):
    return lax.optimization_barrier((value,) + arrays)


def out(*shape, dtype=bf16):
    return jax.ShapeDtypeStruct(shape, dtype)


def bias_rows(bias):
    row = lax.broadcasted_iota(jnp.int32, (WIDE - CIN, C), 0)
    rest = jnp.broadcast_to(bias, (WIDE - CIN, C))
    rows = jnp.zeros((WIDE - CIN, C), f32)
    for n in range(3):
        piece = rest.astype(bf16).astype(f32)
        rows = jnp.where(row == n, piece, rows)
        rest = rest - piece
    return rows.astype(bf16)


def adapter_kernel(
    place, valid, center, top, bottom, left, right, latent, w_in, b_in, w_conv, b_conv, w_out,
    b_out, w_query, w_key, w_value, rows_out, mixed_out, smooth_out, slope_out, cond_out,
    w_wide,
):
    span = ITEMS * (ROWS + 2)
    w_wide[:CIN, :] = w_in[...]
    w_wide[CIN:, :] = bias_rows(b_in[...])

    def widen(values):
        blank = jnp.zeros(values.shape[:-1] + (WIDE - CIN,), f32)
        return jnp.concatenate([values.astype(f32), blank], axis=-1)

    block = jnp.concatenate([top[...], center[...], bottom[...]], axis=1)
    block = widen(block.reshape(span, COLS, CIN))
    shape = (ITEMS, ROWS + 2, COLS, WIDE)
    row = lax.broadcasted_iota(jnp.int32, shape, 1) + ROWS * place[0] - 1
    inside = (row >= 0) & (row < ROWS * 16)
    inside = jnp.where(inside, 1.0, 0.0).reshape(span, COLS, WIDE)
    lane = lane_of((span, COLS, WIDE))
    col = lax.broadcasted_iota(jnp.int32, (span, COLS, WIDE), 1)
    at = COLS * place[2]
    edges = []
    for n, side in enumerate((left, right)):
        there = (at > 0) if n == 0 else (at < COLS * 7)
        edges.append((widen(side[...]).reshape(span, 1, WIDE), jnp.where(there, inside, 0.0)))
    near = jnp.where(col == 0, edges[0][0], pltpu.roll(block, 1, 1))
    near_inside = jnp.where(col == 0, edges[0][1], inside)
    far = jnp.where(col == COLS - 1, edges[1][0], pltpu.roll(block, COLS - 1, 1))
    far_inside = jnp.where(col == COLS - 1, edges[1][1], inside)
    inner = jnp.zeros((CELLS, C), f32)
    start_here = None
    one = (lane >= CIN) & (lane < CIN + 3)
    moves = ((near, near_inside), (block, inside), (far, far_inside))
    for j, (moved, present) in enumerate(moves):
        moved = jnp.where(one, present, moved)
        start = dot(moved.reshape(span * COLS, WIDE).astype(bf16), w_wide[...])
        start = start.reshape(ITEMS, ROWS + 2, COLS, C)
        moved = moved.reshape(ITEMS, ROWS + 2, COLS, WIDE)
        for i in range(3):
            patch = start[:, i : i + ROWS].reshape(CELLS, C).astype(bf16)
            if i == 1 and j == 1:
                start_here = patch.astype(f32)
            inner += dot(patch, w_conv[3 * i + j])
            cond_out[3 * i + j] = moved[:, i : i + ROWS].reshape(CELLS, WIDE).astype(bf16)
    inner += b_conv[...]
    gate = jax.nn.sigmoid(inner)
    smooth = (inner * gate).astype(bf16)
    smooth_out[...] = smooth
    slope_out[...] = gate * (1.0 + inner * (1.0 - gate))
    mixed = latent[...].astype(f32) + (start_here + dot(smooth, w_out[...]) + b_out[...])
    mixed_out[...] = mixed
    normed = moments(mixed)[0].astype(bf16)
    projected = [dot(normed, w[...]) for w in (w_query, w_key, w_value)]
    projected[0] *= SCALE * LOG2E
    lane = lane_of((PART, LANES - MASK))
    row = lax.broadcasted_iota(jnp.int32, (PART, LANES - MASK), 0) // COLS + ROWS * place[0]
    extras = []
    for item in range(ITEMS):
        hidden = jnp.where(row >= valid[item], MASKED, 0.0)
        extras.append(jnp.where(lane == 0, hidden, 1.0))
    extras = jnp.concatenate(extras, axis=0)
    for head in range(HEADS):
        at = slice(head * HEAD, (head + 1) * HEAD)
        joined = jnp.concatenate([part[:, at] for part in projected] + [extras], axis=1)
        rows_out[:, head] = joined.astype(bf16).reshape(ITEMS, PART, LANES)


def text_kernel(
    text, w_key_turned, w_value_turned, keys_out, values_out, wide_key, wide_value
):
    count = text.shape[0]
    token = lax.broadcasted_iota(jnp.int32, (TEXT, count), 0)
    place = lane_of((TEXT, count))
    blank = jnp.zeros((WIDE - GROUP, text.shape[1]), bf16)
    for source, wide in ((w_key_turned, wide_key), (w_value_turned, wide_value)):
        for g in range(2):
            wide[g * WIDE : g * WIDE + GROUP, :] = source[g * GROUP : (g + 1) * GROUP, :]
            wide[g * WIDE + GROUP : (g + 1) * WIDE, :] = blank
    text[:16]

    def body(item, carry):
        pick = jnp.where(place == token * ITEMS + item, 1.0, 0.0).astype(bf16)
        states = dot(pick, text[...]).astype(bf16)
        keys_out.buffer[item] = dot_nt(states, wide_key[...]).astype(bf16)
        values_out.buffer[item] = dot_nt(states, wide_value[...]).astype(bf16)
        return carry

    lax.fori_loop(0, ITEMS, body, 0)
    keys_out.start()
    values_out.start()


def form_kernel(w_query, w_cross_out, w_attn, query_out, cross_out, spread_out):
    rows = w_query[...].astype(f32)
    blank = jnp.zeros((C, WIDE - GROUP), f32)
    rows = [rows[:, :GROUP], blank, rows[:, GROUP:], blank]
    query_out[...] = jnp.concatenate(rows, axis=1).astype(bf16)
    rows = w_cross_out[...]
    blank = jnp.zeros((WIDE - GROUP, C), bf16)
    cross_out[...] = jnp.concatenate([rows[:GROUP], blank, rows[GROUP:], blank], axis=0)
    rows = w_attn[...].astype(f32)
    gap = jnp.zeros((HEAD, 384 - C), f32)
    for head in range(HEADS):
        part = jnp.concatenate([rows[head * HEAD : (head + 1) * HEAD], gap], axis=1)
        blank = jnp.zeros_like(part)
        block = jnp.concatenate(
            [
                jnp.concatenate([part, blank], axis=1),
                jnp.concatenate([blank, part], axis=1),
                jnp.zeros((LANES - 2 * HEAD, 768), f32),
            ],
            axis=0,
        )
        spread_out[head * LANES : (head + 1) * LANES, :] = block.astype(bf16)


BLOCK = 256
STEP = 512


def attend_kernel(
    own, other, packed_out, full_out, probs_out, keys_out, query_out,
    scores_a, scores_b, probs_a, probs_b, turned_a, turned_b, output, sems,
):
    count = HALF // BLOCK
    keys_turned, query = keys_out.buffer, query_out.buffer
    keys_turned[:, :HALF] = jnp.transpose(own[...])
    keys_turned[:, HALF:] = jnp.transpose(other[...])
    keys_out.start()
    lane = lane_of((HALF, LANES))
    rows = pltpu.roll(own[...].astype(f32), KEY, 1)
    rows = jnp.where((lane >= KEY) & (lane < VALUE), rows, jnp.where(lane == MASK, 1.0, 0.0))
    query_out[...] = jnp.transpose(rows.astype(bf16))
    chunks = [(ref, at) for ref in (own, other) for at in range(0, HALF, STEP)]

    def columns(b):
        return pl.ds(pl.multiple_of(b * BLOCK, BLOCK), BLOCK)

    def score(queries, n, scores, peak):
        ref, at = chunks[n]
        part = dot(ref[at : at + STEP, :], queries)
        scores[n * STEP : (n + 1) * STEP, :] = part
        part = jnp.max(part.reshape(STEP // 8, 8, BLOCK), axis=0)
        return part if peak is None else jnp.maximum(peak, part)

    def sent(b, turned, n):
        return pltpu.make_async_copy(turned, probs_out.at[columns(b)], sems.at[n])

    def half(b, peak, following, scores, probs, turned):
        shift = jnp.max(peak, axis=0, keepdims=True)
        queries = query[:, columns(jnp.minimum(b + 1, count - 1))]
        ahead = None
        for n in range(len(chunks)):
            ahead = score(queries, n, following, ahead)
            keys = slice(n * STEP, (n + 1) * STEP)
            part = jnp.exp2(scores[keys, :] - shift).astype(bf16)
            probs[keys, :] = part
            turned[:, keys] = jnp.transpose(part)
        output[:, columns(b)] = dot(keys_turned[...], probs[...])
        return ahead

    peak = None
    for n in range(len(chunks)):
        peak = score(query[:, :BLOCK], n, scores_a, peak)

    def body(i, peak):
        @pl.when(i > 0)
        def _():
            sent(2 * i - 2, turned_a, 0).wait()

        peak = half(2 * i, peak, scores_b, scores_a, probs_a, turned_a)
        sent(2 * i, turned_a, 0).start()

        @pl.when(i > 0)
        def _():
            sent(2 * i - 1, turned_b, 1).wait()

        peak = half(2 * i + 1, peak, scores_a, scores_b, probs_b, turned_b)
        sent(2 * i + 1, turned_b, 1).start()
        return peak

    lax.fori_loop(0, count // 2, body, peak)
    total = output[...]
    inverse = 1.0 / total[MASK + 1 : MASK + 2, :]
    row = lax.broadcasted_iota(jnp.int32, (LANES, HALF), 0)
    total = jnp.transpose(jnp.where(row == 0, inverse, total * inverse))
    full_out[...] = total
    pairs = total.reshape(CHIPS, 2, PART // 2, LANES)
    lane = lane_of((HALF // 2, LANES))
    low = pltpu.roll(pairs[:, 0].reshape(HALF // 2, LANES), LANES - VALUE, 1)
    high = pltpu.roll(pairs[:, 1].reshape(HALF // 2, LANES), LANES - VALUE + HEAD, 1)
    packed = jnp.where(lane < HEAD, low, jnp.where(lane < 2 * HEAD, high, 0.0))
    packed_out[...] = packed.astype(bf16).reshape(CHIPS, PART // 2, LANES)
    sent(count - 2, turned_a, 0).wait()
    sent(count - 1, turned_b, 1).wait()


def middle_kernel(
    lengths, heads_in, mixed, cotangent, text_keys, text_values, w_attn, b_attn, w_cross_query,
    w_cross_out, b_cross, w_ff_in, b_ff_in, w_ff_turned, b_ff_out, result_out, grad_out, heads_out,
    probs_keep,
):
    half = CELLS // 2
    split = w_attn.shape[1] // 2
    packed = jnp.concatenate(
        [heads_in[:, head].reshape(half, LANES) for head in range(HEADS)], axis=1
    )
    both = dot(packed, w_attn[...])
    shape = (ITEMS, 1, PART // 2, C)
    attended = jnp.concatenate(
        [both[:, :C].reshape(shape), both[:, split : split + C].reshape(shape)], axis=1
    ).reshape(CELLS, C)
    first = mixed[...] + attended + b_attn[...]
    unit_two, rate_two = moments(first)
    cross_query = dot(unit_two.astype(bf16), w_cross_query[...]).astype(bf16)
    lane = lane_of((PART, WIDE))
    in_head = [(lane >= HEAD * h) & (lane < HEAD * (h + 1)) for h in range(HEADS // 2)]
    groups = [slice(0, WIDE), slice(WIDE, 2 * WIDE)]
    half_rows = HEADS * PART // 2

    def by_head(values, others):
        parts = []
        for lanes in groups:
            here = values[:, lanes]
            rows = [jnp.where(mask, here, jnp.zeros_like(here)) for mask in in_head]
            parts.append(dot_nt(jnp.concatenate(rows, axis=0), others[:, lanes]))
        return jnp.concatenate(parts, axis=0)

    def by_cell(weights, others):
        parts = []
        for g, lanes in enumerate(groups):
            rows = dot(weights[g * half_rows : (g + 1) * half_rows], others[:, lanes])
            total = jnp.zeros((PART, WIDE), f32)
            for h, mask in enumerate(in_head):
                total = jnp.where(mask, rows[h * PART : (h + 1) * PART], total)
            parts.append(total)
        return jnp.concatenate(parts, axis=1)

    token = lane_of((HEADS * PART, TEXT))
    outs = []
    for item in range(ITEMS):
        cells = slice(item * PART, (item + 1) * PART)
        scores = by_head(cross_query[cells], text_keys[item]) * SCALE
        scores = jnp.where(token < lengths[item], scores, MASKED)
        weights = jnp.exp(scores - jnp.max(scores, -1, keepdims=True))
        probs = weights / jnp.sum(weights, -1, keepdims=True)
        probs_keep[item] = probs
        outs.append(by_cell(probs.astype(bf16), text_values[item]))
    cross = jnp.concatenate(outs, axis=0).astype(bf16)
    second = first + dot(cross, w_cross_out[...]) + b_cross[...]
    unit_three, rate_three = moments(second)
    normed_three = unit_three.astype(bf16)
    upstream = cotangent[...]
    result = second + b_ff_out[...]
    grad_normed = jnp.zeros((CELLS, C), f32)
    step = 256
    for at in range(0, FF, step):
        values, gates = slice(at, at + step), slice(FF + at, FF + at + step)
        value = dot(normed_three, w_ff_in[:, values]) + b_ff_in[values]
        gate = dot(normed_three, w_ff_in[:, gates]) + b_ff_in[gates]
        normal = 0.5 + 0.5 * lax.erf(gate * (0.5**0.5))
        density = jnp.exp(gate * gate * -0.5) * 0.3989422804014327
        gelu = gate * normal
        result += dot_nt((value * gelu).astype(bf16), w_ff_turned[:, values])
        grad_act = dot(upstream, w_ff_turned[:, values])
        grad_value = (grad_act * gelu).astype(bf16)
        grad_gate = (grad_act * value * (normal + gate * density)).astype(bf16)
        grad_normed += dot_nt(grad_value, w_ff_in[:, values])
        grad_normed += dot_nt(grad_gate, w_ff_in[:, gates])
    result_out[...] = result.astype(bf16)
    grad_second = upstream.astype(f32) + norm_back(unit_three, rate_three, grad_normed)
    grad_cross = dot_nt(grad_second.astype(bf16), w_cross_out[...]).astype(bf16)
    outs = []
    for item in range(ITEMS):
        cells = slice(item * PART, (item + 1) * PART)
        grad_probs = by_head(grad_cross[cells], text_values[item])
        probs = probs_keep[item]
        weighted = jnp.sum(probs * grad_probs, -1, keepdims=True)
        grad_scores = (probs * (grad_probs - weighted)).astype(bf16)
        outs.append(by_cell(grad_scores, text_keys[item]))
    grad_query = (jnp.concatenate(outs, axis=0) * SCALE).astype(bf16)
    grad_first = grad_second + norm_back(
        unit_two, rate_two, dot_nt(grad_query, w_cross_query[...])
    )
    grad_out[...] = grad_first
    pairs = grad_first.reshape(ITEMS, 2, PART // 2, C)
    gap = jnp.zeros((half, split - C), f32)
    both = jnp.concatenate(
        [pairs[:, 0].reshape(half, C), gap, pairs[:, 1].reshape(half, C), gap], axis=1
    ).astype(bf16)
    packed = dot_nt(both, w_attn[...]).astype(bf16)
    for head in range(HEADS):
        piece = packed[:, head * LANES : (head + 1) * LANES]
        heads_out[:, head] = piece.reshape(ITEMS, PART // 2, LANES)


WIDE_BLOCK = 512
WIDE_STEP = 1024


def attend_back_kernel(
    keys_turned, query_turned, full, packed, probs_in, own_out, other_out,
    grads, left, sums, scores, probs_a, probs_b, sems,
):
    half, count = HALF // 2, HALF // WIDE_BLOCK

    def block(b):
        return pl.ds(pl.multiple_of(b * WIDE_BLOCK, WIDE_BLOCK), WIDE_BLOCK)

    def fetched(b, probs, n):
        return pltpu.make_async_copy(probs_in.at[block(b)], probs, sems.at[n])

    fetched(0, probs_a, 0).start()
    fetched(1, probs_b, 1).start()
    lane = lane_of((half, LANES))
    value_lane = (lane >= VALUE) & (lane < MASK)
    pairs = packed[...].reshape(half, LANES).astype(f32)
    low = jnp.where(value_lane, pltpu.roll(pairs, VALUE, 1), 0.0)
    high = jnp.where(value_lane, pltpu.roll(pairs, VALUE - HEAD, 1), 0.0)
    shape = (CHIPS, 1, PART // 2, LANES)
    upstream = jnp.concatenate([low.reshape(shape), high.reshape(shape)], axis=1)
    upstream = upstream.reshape(HALF, LANES)
    lane = lane_of((HALF, LANES))
    outputs = full[...]
    upstream *= jnp.sum(jnp.where(lane == 0, outputs, 0.0), axis=1, keepdims=True)
    weighted = jnp.sum(upstream * outputs, axis=1, keepdims=True)
    first = weighted.astype(bf16).astype(f32)
    upstream = jnp.where(lane == MASK + 4, -first, upstream)
    upstream = jnp.where(lane == MASK + 5, first - weighted, upstream).astype(bf16)
    grads[...] = upstream
    for b in range(count):
        rows, at = slice(b * WIDE_BLOCK, (b + 1) * WIDE_BLOCK), 2 * b * WIDE_BLOCK
        left[:, at : at + WIDE_BLOCK] = query_turned[:, rows]
        left[:, at + WIDE_BLOCK : at + 2 * WIDE_BLOCK] = jnp.transpose(upstream[rows])
    sums[...] = jnp.zeros_like(sums)

    def work(b, probs):
        rows = block(b)
        upstream = grads[rows, :]
        both = left[:, pl.ds(pl.multiple_of(2 * b * WIDE_BLOCK, 2 * WIDE_BLOCK), 2 * WIDE_BLOCK)]
        for at in range(0, 2 * HALF, WIDE_STEP):
            keys = slice(at, at + WIDE_STEP)
            part = probs[:, keys]
            grad = dot(upstream, keys_turned[:, keys])
            grad = (part.astype(f32) * grad).astype(bf16)
            sums[:, keys] += dot(both, jnp.concatenate([grad, part], axis=0))
            scores[keys, :] = jnp.transpose(grad)
        grad_query = jnp.transpose(dot(keys_turned[...], scores[...])) * SCALE
        own_out[rows, :] = pltpu.roll(grad_query, LANES - KEY, 1)

    def body(i, carry):
        fetched(2 * i, probs_a, 0).wait()
        work(2 * i, probs_a)

        @pl.when(2 * i + 2 < count)
        def _():
            fetched(2 * i + 2, probs_a, 0).start()

        fetched(2 * i + 1, probs_b, 1).wait()
        work(2 * i + 1, probs_b)

        @pl.when(2 * i + 3 < count)
        def _():
            fetched(2 * i + 3, probs_b, 1).start()

        return carry

    lax.fori_loop(0, count // 2, body, 0)
    scale = jnp.where(lane < VALUE, 1.0 / LOG2E, 1.0)
    rest = jnp.where(lane < MASK, jnp.transpose(sums[:, :HALF]) * scale, 0.0)
    own_out[...] = jnp.where(lane < KEY, own_out[...], rest)
    rest = jnp.where(
        (lane >= KEY) & (lane < MASK), jnp.transpose(sums[:, HALF:]) * scale, 0.0
    )
    other_out[...] = rest.astype(bf16)


def join_kernel(w_query, w_key, w_value, joined_out):
    blank = jnp.zeros((C, LANES - MASK), f32)
    parts = [w[...].astype(f32) for w in (w_query, w_key, w_value)]
    for head in range(HEADS):
        at = slice(head * HEAD, (head + 1) * HEAD)
        joined = jnp.concatenate([part[:, at] for part in parts] + [blank], axis=1)
        joined_out[:, head * LANES : (head + 1) * LANES] = joined.astype(bf16)


def widen_kernel(w_in, b_in, turned_out):
    wide = jnp.concatenate([w_in[...], bias_rows(b_in[...])], axis=0)
    turned_out[...] = jnp.transpose(wide)


def finish_kernel(
    place, rows, w_qkv, mixed, grad_first, slope, smooth, cond, w_out, latent_out, parts_out
):
    joined = jnp.concatenate(
        [rows[:, head].reshape(CELLS, LANES) for head in range(HEADS)], axis=1
    )
    unit, rate = moments(mixed[...])
    latent = grad_first[...] + norm_back(unit, rate, dot_nt(joined, w_qkv[...]))
    latent_out[...] = latent
    branch = latent.astype(bf16)
    inner = (dot_nt(branch, w_out[...]) * slope[...]).astype(bf16)
    inner_turned = jnp.transpose(inner)
    branch_turned = jnp.transpose(branch)
    here, there = place[1], 1 - place[1]

    def put(side, at, values):
        values = values.astype(bf16)
        for t in range(0, 3 * LANES, LANES):
            parts_out[side, at : at + C, :] = values[:, t : t + LANES]
            at += C

    lane = lane_of((C, LANES))
    ones = jnp.zeros((C, LANES), f32)
    kept = None
    for n in range(10):
        moment = dot(inner_turned, cond[n]) if n < 9 else dot(branch_turned, cond[4])
        one = pltpu.roll(moment[:, LANES:], 3 * n, 1)
        ones = jnp.where((lane >= 64 + 3 * n) & (lane < 67 + 3 * n), one, ones)
        if n % 2 == 0:
            kept = moment[:, :CIN]
            continue
        both = jnp.concatenate([kept, moment[:, :CIN]], axis=1)
        pair = n // 2
        put(here if pair < 3 else there, 3 * C * (pair % 3), both)
    values = dot(branch_turned, smooth[...])
    last = jnp.concatenate([values[:, 2 * LANES :], ones[:, 64:]], axis=1)
    put(there, 6 * C, jnp.concatenate([values[:, : 2 * LANES], last], axis=1))
    for side in range(2):
        parts_out[side, 9 * C :, :] = jnp.zeros((SUM_ROWS - 9 * C, LANES), bf16)


def weights_kernel(
    place, mine, theirs, w_turned, w_conv, win_out, bin_out, wconv_out, bconv_out, wout_out,
    bout_out, taps, sems,
):
    here = place[1]

    def tile(half, n):
        rows = slice(C * n, C * (n + 1))
        return jnp.where(here == half, mine[rows, :], theirs[rows, :]).astype(f32)

    ones = tile(1, 8)
    lane = lane_of((C, LANES))
    low = lane < 64

    def moment_of(n):
        pair = n // 2
        first, middle, last = [tile(pair // 3, 3 * (pair % 3) + t) for t in range(3)]
        if n % 2:
            middle, last = pltpu.roll(middle, 64, 1), pltpu.roll(last, 64, 1)
            first, middle = jnp.where(low, middle, last), last
        one = jnp.where(lane < 67, pltpu.roll(ones, LANES - 3 * n, 1) if n else ones, 0.0)
        return jnp.concatenate([first, jnp.where(low, middle, one)], axis=1).astype(bf16)

    grad_in = jnp.zeros((C, WIDE), f32)
    copies = []
    for n in range(9):
        moment = moment_of(n)
        taps[n] = dot_nt(w_turned[...], moment)
        copy = pltpu.make_async_copy(taps.at[n], wconv_out.at[n], sems.at[n])
        copy.start()
        copies.append(copy)
        grad_in += dot(w_conv[n], moment)
    last = jnp.concatenate([tile(1, 6), tile(1, 7), ones], axis=1)
    last = jnp.transpose(last)
    wout_out[...] = last[:C]
    bconv_out[...] = last[C + 12]
    bout_out[...] = last[C + 27]
    grad_in = jnp.transpose(grad_in + moment_of(9).astype(f32))
    win_out[...] = grad_in[:CIN]
    bin_out[...] = grad_in[CIN]
    for copy in copies:
        copy.wait()


def swap(array):
    return lax.ppermute(array, "c", [(0, 1), (1, 0)])


def across(blocks):
    return lax.all_to_all(blocks, ACROSS, 0, 0, tiled=True)


def per_device(
    latent, condition, text_states, valid_rows, text_lengths, w_in, b_in, w_conv, b_conv, w_out,
    b_out, w_query, w_key, w_value, w_attn_out, b_attn_out, w_cross_query, w_cross_key,
    w_cross_value, w_cross_out, b_cross_out, w_ff_in, b_ff_in, w_ff_out, b_ff_out, cotangent,
):
    core = lax.axis_index("c")
    place = jnp.stack([lax.axis_index("sp"), core, 2 * lax.axis_index("x") + core])
    place = place.astype(jnp.int32)

    down = [(i, i + 1) for i in range(15)]
    top = lax.ppermute(condition[:, ROWS - 1 :], "sp", down)
    bottom = lax.ppermute(condition[:, :1], "sp", [(b, a) for a, b in down])
    right_way = [(i, i + 1) for i in range(7)]

    def edge(col):
        tall = jnp.concatenate([top[:, :, col], condition[:, :, col], bottom[:, :, col]], axis=1)
        return tall.reshape(ITEMS * (ROWS + 2), CIN)

    left = lax.ppermute(edge(COLS - 1), ("x", "c"), right_way)
    right = lax.ppermute(edge(0), ("x", "c"), [(b, a) for a, b in right_way])
    top, first_bias = after(top, b_in)
    adapter_arrays = bring(
        [
            w_in, first_bias, w_conv.reshape(9, C, C), condition, latent.reshape(CELLS, C),
            b_conv, w_out, b_out, w_query, w_key, w_value,
        ],
        "load_adapter",
    )
    (w_in_here, b_in_here, taps_here, condition_here, latent_here, b_conv_here) = adapter_arrays[:6]
    (w_out_here, b_out_here, w_query_here, w_key_here, w_value_here) = adapter_arrays[6:]

    rows, mixed, smooth, slope, cond = call(
        adapter_kernel,
        (
            out(ITEMS, HEADS, PART, LANES),
            out(CELLS, C, dtype=f32),
            out(CELLS, C),
            out(CELLS, C, dtype=f32),
            out(9, CELLS, WIDE),
        ),
        (
            place, valid_rows, condition_here, top, bottom, left, right, latent_here, w_in_here,
            b_in_here, taps_here, b_conv_here, w_out_here, b_out_here, w_query_here, w_key_here,
            w_value_here,
        ),
        "adapter",
        scalars=2,
        scratch=[pltpu.VMEM((WIDE, C), bf16)],
        vmem=24,
        store=(0, 1, 2, 3, 4),
        held=(2,) + tuple(range(7, 17)),
    )

    rows, text = after(rows, text_states)
    text_keys, text_values = call(
        text_kernel,
        (out(ITEMS, TEXT, 2 * WIDE), out(ITEMS, TEXT, 2 * WIDE)),
        (text.transpose(1, 0, 2).reshape(-1, text.shape[2]), w_cross_key.T, w_cross_value.T),
        "text",
        scratch=[pltpu.VMEM((2 * WIDE, text.shape[2]), bf16)] * 2,
        fetch=(1, 2, 0),
        store=(0, 1),
    )
    own = across(rows.reshape(CHIPS, PART, LANES)).reshape(HALF, LANES)
    own, text_keys = after(own, text_keys)

    other = swap(own)
    _, attn_weight = after(own, w_attn_out)
    w_cross_query_wide, w_cross_out_wide, w_attn_spread = call(
        form_kernel,
        (out(C, 2 * WIDE), out(2 * WIDE, C), out(HEADS * LANES, 768)),
        (w_cross_query, w_cross_out, attn_weight),
        "form",
        fetch=(2, 0, 1),
        store=(0, 1),
        near=(2,),
    )
    own, w_attn_spread = after(own, w_attn_spread)
    packed, full, probs, keys_turned, query_turned = call(
        attend_kernel,
        (
            out(CHIPS, PART // 2, LANES),
            out(HALF, LANES, dtype=f32),
            out(HALF, 2 * HALF),
            out(LANES, 2 * HALF),
            out(LANES, HALF),
        ),
        (own, other),
        "attend",
        scratch=[
            pltpu.VMEM((2 * HALF, BLOCK), f32),
            pltpu.VMEM((2 * HALF, BLOCK), f32),
            pltpu.VMEM((2 * HALF, BLOCK), bf16),
            pltpu.VMEM((2 * HALF, BLOCK), bf16),
            pltpu.VMEM((BLOCK, 2 * HALF), bf16),
            pltpu.VMEM((BLOCK, 2 * HALF), bf16),
            pltpu.VMEM((LANES, HALF), f32),
            pltpu.SemaphoreType.DMA((2,)),
        ],
        vmem=32,
        store=(1, 3, 4),
        near=(0,),
        far=(4,),
    )

    heads_in = across(packed).reshape(ITEMS, HEADS, PART // 2, LANES)
    result, grad_first, heads_out = call(
        middle_kernel,
        (out(CELLS, C), out(CELLS, C, dtype=f32), out(ITEMS, HEADS, PART // 2, LANES)),
        (
            text_lengths, heads_in, mixed, cotangent.reshape(CELLS, C), text_keys, text_values,
            w_attn_spread, b_attn_out, w_cross_query_wide, w_cross_out_wide, b_cross_out,
            w_ff_in, b_ff_in, w_ff_out.T, b_ff_out,
        ),
        "middle",
        scalars=1,
        scratch=[pltpu.VMEM((ITEMS, HEADS * PART, TEXT), f32)],
        vmem=32,
        fetch=(2, 7, 8, 4, 5, 9, 10, 3, 11, 12, 13, 14),
        store=(0, 1),
        near=(2,),
        held=(6,),
    )

    grads_in = across(heads_out.reshape(CHIPS, PART // 2, LANES))
    own_grads, other_grads = call(
        attend_back_kernel,
        (out(HALF, LANES, dtype=f32), out(HALF, LANES)),
        (keys_turned, query_turned, full, grads_in, probs),
        "attend_back",
        scratch=[
            pltpu.VMEM((HALF, LANES), bf16),
            pltpu.VMEM((LANES, 2 * HALF), bf16),
            pltpu.VMEM((LANES, 2 * HALF), f32),
            pltpu.VMEM((2 * HALF, WIDE_BLOCK), bf16),
            pltpu.VMEM((WIDE_BLOCK, 2 * HALF), bf16),
            pltpu.VMEM((WIDE_BLOCK, 2 * HALF), bf16),
            pltpu.SemaphoreType.DMA((2,)),
        ],
        vmem=36,
        near=(0, 1),
        far=(4,),
    )

    _, query_weight = after(other_grads, w_query)
    (w_joined,) = call(
        join_kernel,
        (out(C, HEADS * LANES),),
        (query_weight, w_key, w_value),
        "join",
        fetch=(0, 1, 2),
        near=(0,),
    )
    own_grads, w_joined = after(own_grads, w_joined)
    row_grads = (own_grads + swap(other_grads).astype(f32)).astype(bf16)
    row_grads = across(row_grads.reshape(CHIPS, PART, LANES))
    latent_grad, parts = call(
        finish_kernel,
        (out(CELLS, C, dtype=f32), out(2, SUM_ROWS, LANES)),
        (
            place, row_grads.reshape(ITEMS, HEADS, PART, LANES), w_joined, mixed, grad_first,
            slope, smooth, cond, w_out,
        ),
        "finish",
        scalars=1,
        store=(0,),
    )

    shares = (parts[0].astype(f32) + swap(parts[1]).astype(f32)).astype(bf16)
    shares, last_bias = after(shares, b_in)
    taps_last, w_turned = bring(
        [w_conv.reshape(9, C, C)],
        "load_weights",
        widen_kernel,
        (out(C, WIDE),),
        (w_in, last_bias),
    )
    shares = across(shares.reshape(CHIPS, SUM_ROWS // CHIPS, LANES))
    share = jnp.sum(shares.astype(f32), axis=0).astype(bf16)
    mine = across(jnp.broadcast_to(share[None], shares.shape)).reshape(SUM_ROWS, LANES)
    theirs = swap(mine)
    grad_w_in, grad_b_in, grad_w_conv, grad_b_conv, grad_w_out, grad_b_out = call(
        weights_kernel,
        (
            out(CIN, C, dtype=f32),
            out(C, dtype=f32),
            out(9, C, C, dtype=f32),
            out(C, dtype=f32),
            out(C, C, dtype=f32),
            out(C, dtype=f32),
        ),
        (place, mine, theirs, w_turned, taps_last),
        "weights",
        scalars=1,
        scratch=[
            pltpu.VMEM((9, C, C), f32),
            pltpu.SemaphoreType.DMA((9,)),
        ],
        vmem=24,
        store=(0, 4),
        far=(7,),
        held=(3, 4),
    )
    grid = (ITEMS, ROWS, COLS, C)
    return (
        result.reshape(grid),
        latent_grad.reshape(grid),
        grad_w_in,
        grad_b_in,
        grad_w_conv.reshape(3, 3, C, C),
        grad_b_conv,
        grad_w_out,
        grad_b_out,
    )


def solution(mesh):
    split = Mesh(mesh.devices.reshape(16, 4, 2), ("sp", "x", "c"))
    cells = P(None, "sp", ("x", "c"), None)
    in_specs = (cells, cells) + (P(),) * 23 + (cells,)
    out_specs = (cells, cells) + (P(),) * 6
    return jax.shard_map(
        per_device, mesh=split, in_specs=in_specs, out_specs=out_specs, check_vma=False
    )
```

```python
import jax
import jax.numpy as jnp
from jax import lax
from jax.experimental import pallas as pl
from jax.experimental.pallas import tpu as pltpu
from jax.sharding import Mesh
from jax.sharding import PartitionSpec as P

STRIPS, ROWS, COLS, C, CIN, HEADS, HEAD, FF = 8, 4, 8, 320, 192, 8, 40, 1280
CELLS = STRIPS * ROWS * COLS
PART = ROWS * COLS
CHIPS = 64
HALF = CHIPS * PART
TEXT = 128
LANES = 128
WIDE = 256
GROUP = 160
SCALE = HEAD**-0.5
LOG2E = 1.4426950408889634
EPS = 1e-5
MASKED = -1e30
KEY, VALUE, MASK = HEAD, 2 * HEAD, 3 * HEAD
GROUP_OF_ITEM, CHIPS_ALL = ("b", "x"), ("a", "b", "x")
LATENT, COTANGENT = 256, 640
SUM_ROWS = 3072

bf16, f32 = jnp.bfloat16, jnp.float32
NT = (((1,), (1,)), ((), ()))


def dot(left, right):
    return jnp.dot(left, right, preferred_element_type=f32)


def dot_nt(left, right):
    return lax.dot_general(left, right, NT, preferred_element_type=f32)


def lane_of(shape):
    return lax.broadcasted_iota(jnp.int32, shape, len(shape) - 1)


def moments(values):
    center = values - jnp.mean(values, -1, keepdims=True)
    rate = lax.rsqrt(jnp.mean(center * center, -1, keepdims=True) + EPS)
    return center * rate, rate


def norm_back(unit, rate, grads):
    return rate * (
        grads
        - jnp.mean(grads, -1, keepdims=True)
        - unit * jnp.mean(grads * unit, -1, keepdims=True)
    )


class Fetched:
    def __init__(self, source, buffer, semaphore):
        self.copy = pltpu.make_async_copy(source, buffer, semaphore)
        self.buffer, self.shape, self.here = buffer, buffer.shape, False
        self.copy.start()

    def __getitem__(self, index):
        if not self.here:
            self.copy.wait()
            self.here = True
        return self.buffer[index]


class Stored:
    def __init__(self, target, buffer, semaphore):
        self.copy = pltpu.make_async_copy(buffer, target, semaphore)
        self.buffer, self.started = buffer, False

    def __setitem__(self, index, values):
        self.buffer[index] = values
        if index is Ellipsis:
            self.start()

    def start(self):
        if not self.started:
            self.copy.start()
            self.started = True


def call(kernel, outs, ins, name, scalars=0, scratch=(), vmem=16, fetch=(), store=(), far=(),
    near=(), held=(), cost=None,
):
    fetch, store = list(fetch), list(store)
    far_in = [i for i in far if i < len(ins)]
    far_out = [i - len(ins) for i in far if i >= len(ins)]

    def body(*refs):
        refs = list(refs)
        given, refs = refs[: len(ins)], refs[len(ins) :]
        made, refs = refs[: len(outs)], refs[len(outs) :]
        own, refs = refs[: len(scratch)], refs[len(scratch) :]
        buffers, semaphores = refs[:-1], refs[-1] if refs else None
        for n, i in enumerate(fetch):
            given[i] = Fetched(given[i], buffers[n], semaphores.at[n])
        kept = []
        for n, i in enumerate(store, len(fetch)):
            made[i] = Stored(made[i], buffers[n], semaphores.at[n])
            kept.append(made[i])
        kernel(*given, *made, *own)
        for part in given:
            if isinstance(part, Fetched) and not part.here:
                part.copy.wait()
        for part in kept:
            part.start()
        for part in kept:
            part.copy.wait()

    def made_as(i, made):
        if i in store or i in far_out:
            return pltpu.HBM(made.shape, made.dtype)
        return pltpu.VMEM(made.shape, made.dtype) if i in near else made

    def in_spec(i):
        if i < scalars:
            return pl.BlockSpec(memory_space=pltpu.SMEM)
        space = pltpu.HBM if i in fetch or i in far_in else pltpu.VMEM
        return pl.BlockSpec(memory_space=space)

    def out_spec(i):
        space = pltpu.HBM if i in store or i in far_out else pltpu.VMEM
        return pl.BlockSpec(memory_space=space)

    extra = [pltpu.VMEM(ins[i].shape, ins[i].dtype) for i in fetch]
    extra += [pltpu.VMEM(outs[i].shape, outs[i].dtype) for i in store]
    if extra:
        extra.append(pltpu.SemaphoreType.DMA((len(extra),)))
    return pl.pallas_call(
        body,
        out_shape=tuple(made_as(i, made) for i, made in enumerate(outs)),
        in_specs=[in_spec(i) for i in range(len(ins))],
        out_specs=tuple(out_spec(i) for i in range(len(outs))),
        scratch_shapes=list(scratch) + extra,
        compiler_params=pltpu.CompilerParams(vmem_limit_bytes=vmem << 20),
        cost_estimate=cost,
        name=name,
    )(
        *(
            pltpu.with_memory_space_constraint(x, pltpu.HBM)
            if i in fetch or i in far_in
            else (pltpu.with_memory_space_constraint(x, pltpu.VMEM) if i in held else x)
            for i, x in enumerate(ins)
        )
    )


def bring(arrays, name, kernel=None, made=(), near=()):
    count, given = len(arrays), len(near)

    def body(*refs):
        sources, inputs = refs[:count], refs[count : count + given]
        targets = refs[count + given : -1]
        copies = [
            pltpu.make_async_copy(sources[n], targets[n], refs[-1].at[n]) for n in range(count)
        ]
        for copy in copies:
            copy.start()
        if kernel is not None:
            kernel(*inputs, *targets[count:])
        for copy in copies:
            copy.wait()

    shapes = [jax.ShapeDtypeStruct(x.shape, x.dtype) for x in arrays] + list(made)
    return pl.pallas_call(
        body,
        out_shape=tuple(pltpu.VMEM(x.shape, x.dtype) for x in shapes),
        in_specs=[pl.BlockSpec(memory_space=pltpu.HBM)] * count
        + [pl.BlockSpec(memory_space=pltpu.VMEM)] * given,
        out_specs=(pl.BlockSpec(memory_space=pltpu.VMEM),) * len(shapes),
        scratch_shapes=[pltpu.SemaphoreType.DMA((max(count, 1),))],
        compiler_params=pltpu.CompilerParams(vmem_limit_bytes=8 << 20),
        name=name,
    )(*(pltpu.with_memory_space_constraint(x, pltpu.HBM) for x in arrays), *near)


def after(value, *arrays):
    return lax.optimization_barrier((value,) + arrays)


def out(*shape, dtype=bf16):
    return jax.ShapeDtypeStruct(shape, dtype)


def bias_rows(bias):
    row = lax.broadcasted_iota(jnp.int32, (WIDE - CIN, C), 0)
    rest = jnp.broadcast_to(bias, (WIDE - CIN, C))
    rows = jnp.zeros((WIDE - CIN, C), f32)
    for n in range(3):
        piece = rest.astype(bf16).astype(f32)
        rows = jnp.where(row == n, piece, rows)
        rest = rest - piece
    return rows.astype(bf16)


def adapter_kernel(
    place, valid, cells, beside, left, right, w_in, b_in, w_conv, b_conv, w_out,
    b_out, w_query, w_key, w_value, rows_out, mixed_out, smooth_out, slope_out, cond_out,
    w_wide,
):
    span = STRIPS * (ROWS + 2)
    w_wide[:CIN, :] = w_in[...]
    w_wide[CIN:, :] = bias_rows(b_in[...])
    upper = place[3] == 0

    def tall(own, first, last):
        blank = jnp.zeros_like(first[:1])
        above = jnp.where(upper, jnp.concatenate([blank, last[:-1]], axis=0), last)
        below = jnp.where(upper, first, jnp.concatenate([first[1:], blank], axis=0))
        return jnp.concatenate([above, own, below], axis=1)

    own = cells[:, :, :WIDE].astype(f32).reshape(STRIPS, ROWS, COLS, WIDE)
    other = beside[...].astype(f32)
    block = tall(own, other[:, :1], other[:, 1:]).reshape(span, COLS, WIDE)
    shape = (STRIPS, ROWS + 2, COLS, WIDE)
    row = 2 * ROWS * lax.broadcasted_iota(jnp.int32, shape, 0) + ROWS * place[3] - 1
    row += lax.broadcasted_iota(jnp.int32, shape, 1)
    inside = (row >= 0) & (row < ROWS * 16)
    inside = jnp.where(inside, 1.0, 0.0).reshape(span, COLS, WIDE)
    lane = lane_of((span, COLS, WIDE))
    col = lax.broadcasted_iota(jnp.int32, (span, COLS, WIDE), 1)
    at = COLS * place[2]
    edges = []
    for n, side in enumerate((left, right)):
        there = (at > 0) if n == 0 else (at < COLS * 7)
        side = side[...].astype(f32).reshape(span, 1, WIDE)
        side = side.reshape(STRIPS, ROWS + 2, 1, WIDE)
        side = tall(side[:, :ROWS], side[:, ROWS : ROWS + 1], side[:, ROWS + 1 :])
        edges.append((side.reshape(span, 1, WIDE), jnp.where(there, inside, 0.0)))
    near = jnp.where(col == 0, edges[0][0], pltpu.roll(block, 1, 1))
    near_inside = jnp.where(col == 0, edges[0][1], inside)
    far = jnp.where(col == COLS - 1, edges[1][0], pltpu.roll(block, COLS - 1, 1))
    far_inside = jnp.where(col == COLS - 1, edges[1][1], inside)
    inner = jnp.zeros((CELLS, C), f32)
    start_here = None
    one = (lane >= CIN) & (lane < CIN + 3)
    moves = ((near, near_inside), (block, inside), (far, far_inside))
    for j, (moved, present) in enumerate(moves):
        moved = jnp.where(one, present, moved)
        start = dot(moved.reshape(span * COLS, WIDE).astype(bf16), w_wide[...])
        start = start.reshape(STRIPS, ROWS + 2, COLS, C)
        moved = moved.reshape(STRIPS, ROWS + 2, COLS, WIDE)
        for i in range(3):
            patch = start[:, i : i + ROWS].reshape(CELLS, C).astype(bf16)
            if i == 1 and j == 1:
                start_here = patch.astype(f32)
            inner += dot(patch, w_conv[3 * i + j])
            cond_out[3 * i + j] = moved[:, i : i + ROWS].reshape(CELLS, WIDE).astype(bf16)
    inner += b_conv[...]
    gate = jax.nn.sigmoid(inner)
    smooth = (inner * gate).astype(bf16)
    smooth_out[...] = smooth
    slope_out[...] = gate * (1.0 + inner * (1.0 - gate))
    latent = cells[:, :, LATENT : LATENT + C].astype(f32).reshape(CELLS, C)
    mixed = latent + (start_here + dot(smooth, w_out[...]) + b_out[...])
    mixed_out[...] = mixed
    normed = moments(mixed)[0].astype(bf16)
    projected = [dot(normed, w[...]) for w in (w_query, w_key, w_value)]
    projected[0] *= SCALE * LOG2E
    shape = (STRIPS, ROWS, COLS, LANES - MASK)
    row = 2 * ROWS * lax.broadcasted_iota(jnp.int32, shape, 0) + ROWS * place[3]
    row += lax.broadcasted_iota(jnp.int32, shape, 1)
    hidden = jnp.where(row >= valid[place[0]], MASKED, 0.0)
    extras = jnp.where(lane_of(shape) == 0, hidden, 1.0).reshape(CELLS, LANES - MASK)
    for head in range(HEADS):
        at = slice(head * HEAD, (head + 1) * HEAD)
        joined = jnp.concatenate([part[:, at] for part in projected] + [extras], axis=1)
        rows_out[head] = joined.astype(bf16)


def text_kernel(
    text, w_key_turned, w_value_turned, keys_out, values_out, wide_key, wide_value
):
    blank = jnp.zeros((WIDE - GROUP, text.shape[1]), bf16)
    states = text[...]
    both = ((w_key_turned, wide_key, keys_out), (w_value_turned, wide_value, values_out))
    for source, wide, target in both:
        for g in range(2):
            wide[g * WIDE : g * WIDE + GROUP, :] = source[g * GROUP : (g + 1) * GROUP, :]
            wide[g * WIDE + GROUP : (g + 1) * WIDE, :] = blank
        target[...] = dot_nt(states, wide[...]).astype(bf16)


def form_kernel(w_query, w_cross_out, w_attn, query_out, cross_out, spread_out):
    rows = w_query[...].astype(f32)
    blank = jnp.zeros((C, WIDE - GROUP), f32)
    rows = [rows[:, :GROUP], blank, rows[:, GROUP:], blank]
    query_out[...] = jnp.concatenate(rows, axis=1).astype(bf16)
    rows = w_cross_out[...]
    blank = jnp.zeros((WIDE - GROUP, C), bf16)
    cross_out[...] = jnp.concatenate([rows[:GROUP], blank, rows[GROUP:], blank], axis=0)
    rows = w_attn[...].astype(f32)
    gap = jnp.zeros((HEAD, 384 - C), f32)
    for head in range(HEADS):
        part = jnp.concatenate([rows[head * HEAD : (head + 1) * HEAD], gap], axis=1)
        blank = jnp.zeros_like(part)
        block = jnp.concatenate(
            [
                jnp.concatenate([part, blank], axis=1),
                jnp.concatenate([blank, part], axis=1),
                jnp.zeros((LANES - 2 * HEAD, 768), f32),
            ],
            axis=0,
        )
        spread_out[head * LANES : (head + 1) * LANES, :] = block.astype(bf16)


BLOCK = 256
STEP = 512


def attend_kernel(
    own, other, packed_out, full_out, probs_out, keys_out, query_out,
    scores_a, scores_b, probs_a, probs_b, turned_a, turned_b, output, sems,
):
    count = HALF // BLOCK
    keys_turned, query = keys_out.buffer, query_out.buffer
    keys_turned[:, :HALF] = jnp.transpose(own[...])
    keys_turned[:, HALF:] = jnp.transpose(other[...])
    keys_out.start()
    lane = lane_of((HALF, LANES))
    rows = pltpu.roll(own[...].astype(f32), KEY, 1)
    rows = jnp.where((lane >= KEY) & (lane < VALUE), rows, jnp.where(lane == MASK, 1.0, 0.0))
    query_out[...] = jnp.transpose(rows.astype(bf16))
    chunks = [(ref, at) for ref in (own, other) for at in range(0, HALF, STEP)]

    def columns(b):
        return pl.ds(pl.multiple_of(b * BLOCK, BLOCK), BLOCK)

    def score(queries, n, scores, peak):
        ref, at = chunks[n]
        part = dot(ref[at : at + STEP, :], queries)
        scores[n * STEP : (n + 1) * STEP, :] = part
        part = jnp.max(part.reshape(STEP // 8, 8, BLOCK), axis=0)
        return part if peak is None else jnp.maximum(peak, part)

    def sent(b, turned, n):
        return pltpu.make_async_copy(turned, probs_out.at[columns(b)], sems.at[n])

    def half(b, peak, following, scores, probs, turned):
        shift = jnp.max(peak, axis=0, keepdims=True)
        queries = query[:, columns(jnp.minimum(b + 1, count - 1))]
        ahead = None
        for n in range(len(chunks)):
            ahead = score(queries, n, following, ahead)
            keys = slice(n * STEP, (n + 1) * STEP)
            part = jnp.exp2(scores[keys, :] - shift).astype(bf16)
            probs[keys, :] = part
            turned[:, keys] = jnp.transpose(part)
        output[:, columns(b)] = dot(keys_turned[...], probs[...])
        return ahead

    peak = None
    for n in range(len(chunks)):
        peak = score(query[:, :BLOCK], n, scores_a, peak)

    def body(i, peak):
        @pl.when(i > 0)
        def _():
            sent(2 * i - 2, turned_a, 0).wait()

        peak = half(2 * i, peak, scores_b, scores_a, probs_a, turned_a)
        sent(2 * i, turned_a, 0).start()

        @pl.when(i > 0)
        def _():
            sent(2 * i - 1, turned_b, 1).wait()

        peak = half(2 * i + 1, peak, scores_a, scores_b, probs_b, turned_b)
        sent(2 * i + 1, turned_b, 1).start()
        return peak

    lax.fori_loop(0, count // 2, body, peak)
    total = output[...]
    inverse = 1.0 / total[MASK + 1 : MASK + 2, :]
    row = lax.broadcasted_iota(jnp.int32, (LANES, HALF), 0)
    total = jnp.transpose(jnp.where(row == 0, inverse, total * inverse))
    full_out[...] = total
    pairs = total.reshape(CHIPS, 2, PART // 2, LANES)
    lane = lane_of((HALF // 2, LANES))
    low = pltpu.roll(pairs[:, 0].reshape(HALF // 2, LANES), LANES - VALUE, 1)
    high = pltpu.roll(pairs[:, 1].reshape(HALF // 2, LANES), LANES - VALUE + HEAD, 1)
    packed = jnp.where(lane < HEAD, low, jnp.where(lane < 2 * HEAD, high, 0.0))
    packed_out[...] = packed.astype(bf16).reshape(CHIPS, PART // 2, LANES)
    sent(count - 2, turned_a, 0).wait()
    sent(count - 1, turned_b, 1).wait()


def middle_kernel(
    place, lengths, heads_in, mixed, cells, text_keys, text_values, w_attn, b_attn,
    w_cross_query, w_cross_out, b_cross, w_ff_in, b_ff_in, w_ff_turned, b_ff_out, result_out,
    grad_out, heads_out, probs_keep,
):
    half = CELLS // 2
    split = w_attn.shape[1] // 2
    packed = jnp.concatenate([heads_in[head] for head in range(HEADS)], axis=1)
    both = dot(packed, w_attn[...])
    shape = (STRIPS, 1, PART // 2, C)
    attended = jnp.concatenate(
        [both[:, :C].reshape(shape), both[:, split : split + C].reshape(shape)], axis=1
    ).reshape(CELLS, C)
    first = mixed[...] + attended + b_attn[...]
    unit_two, rate_two = moments(first)
    cross_query = dot(unit_two.astype(bf16), w_cross_query[...]).astype(bf16)
    lane = lane_of((TEXT, WIDE))
    in_head = [(lane >= HEAD * h) & (lane < HEAD * (h + 1)) for h in range(HEADS // 2)]
    groups = [slice(0, WIDE), slice(WIDE, 2 * WIDE)]

    def by_head(text):
        kept = []
        for lanes in groups:
            here = text[:, lanes]
            kept.append(
                jnp.concatenate([jnp.where(m, here, jnp.zeros_like(here)) for m in in_head], 0)
            )
        return kept

    keys, values = by_head(text_keys), by_head(text_values)
    spans = [slice(g * HEADS // 2 * TEXT, (g + 1) * HEADS // 2 * TEXT) for g in range(2)]
    heads = [slice(h * TEXT, (h + 1) * TEXT) for h in range(HEADS)]
    token = lane_of((CELLS, TEXT)) < lengths[place[0]]
    scores = [dot_nt(cross_query[:, groups[g]], keys[g]) * SCALE for g in range(2)]
    scores = jnp.concatenate(scores, axis=1)
    for at in heads:
        part = jnp.where(token, scores[:, at], MASKED)
        weights = jnp.exp(part - jnp.max(part, -1, keepdims=True))
        probs_keep[:, at] = weights / jnp.sum(weights, -1, keepdims=True)
    cross = [dot(probs_keep[:, spans[g]].astype(bf16), values[g]) for g in range(2)]
    cross = jnp.concatenate(cross, axis=1).astype(bf16)
    second = first + dot(cross, w_cross_out[...]) + b_cross[...]
    unit_three, rate_three = moments(second)
    normed_three = unit_three.astype(bf16)
    upstream = cells[:, :, COTANGENT : COTANGENT + C].reshape(CELLS, C)
    result = second + b_ff_out[...]
    grad_normed = jnp.zeros((CELLS, C), f32)
    step = 256
    for at in range(0, FF, step):
        ups, gates = slice(at, at + step), slice(FF + at, FF + at + step)
        value = dot(normed_three, w_ff_in[:, ups]) + b_ff_in[ups]
        gate = dot(normed_three, w_ff_in[:, gates]) + b_ff_in[gates]
        normal = 0.5 + 0.5 * lax.erf(gate * (0.5**0.5))
        density = jnp.exp(gate * gate * -0.5) * 0.3989422804014327
        gelu = gate * normal
        result += dot_nt((value * gelu).astype(bf16), w_ff_turned[:, ups])
        grad_act = dot(upstream, w_ff_turned[:, ups])
        grad_value = (grad_act * gelu).astype(bf16)
        grad_gate = (grad_act * value * (normal + gate * density)).astype(bf16)
        grad_normed += dot_nt(grad_value, w_ff_in[:, ups])
        grad_normed += dot_nt(grad_gate, w_ff_in[:, gates])
    result_out[...] = result.astype(bf16)
    grad_second = upstream.astype(f32) + norm_back(unit_three, rate_three, grad_normed)
    grad_cross = dot_nt(grad_second.astype(bf16), w_cross_out[...]).astype(bf16)
    grad_probs = [dot_nt(grad_cross[:, groups[g]], values[g]) for g in range(2)]
    grad_probs = jnp.concatenate(grad_probs, axis=1)
    grad_scores = []
    for at in heads:
        probs, grads = probs_keep[:, at], grad_probs[:, at]
        weighted = jnp.sum(probs * grads, -1, keepdims=True)
        grad_scores.append((probs * (grads - weighted)).astype(bf16))
    grad_scores = jnp.concatenate(grad_scores, axis=1)
    grad_query = [dot(grad_scores[:, spans[g]], keys[g]) for g in range(2)]
    grad_query = (jnp.concatenate(grad_query, axis=1) * SCALE).astype(bf16)
    grad_first = grad_second + norm_back(
        unit_two, rate_two, dot_nt(grad_query, w_cross_query[...])
    )
    grad_out[...] = grad_first
    pairs = grad_first.reshape(STRIPS, 2, PART // 2, C)
    gap = jnp.zeros((half, split - C), f32)
    both = jnp.concatenate(
        [pairs[:, 0].reshape(half, C), gap, pairs[:, 1].reshape(half, C), gap], axis=1
    ).astype(bf16)
    packed = dot_nt(both, w_attn[...]).astype(bf16)
    for head in range(HEADS):
        heads_out[head] = packed[:, head * LANES : (head + 1) * LANES]


WIDE_BLOCK = 512
WIDE_STEP = 1024


def attend_back_kernel(
    keys_turned, query_turned, full, packed, probs_in, own_out, other_out,
    grads, left, sums, scores, probs_a, probs_b, sems,
):
    half, count = HALF // 2, HALF // WIDE_BLOCK

    def block(b):
        return pl.ds(pl.multiple_of(b * WIDE_BLOCK, WIDE_BLOCK), WIDE_BLOCK)

    def fetched(b, probs, n):
        return pltpu.make_async_copy(probs_in.at[block(b)], probs, sems.at[n])

    fetched(0, probs_a, 0).start()
    fetched(1, probs_b, 1).start()
    lane = lane_of((half, LANES))
    value_lane = (lane >= VALUE) & (lane < MASK)
    pairs = packed[...].reshape(half, LANES).astype(f32)
    low = jnp.where(value_lane, pltpu.roll(pairs, VALUE, 1), 0.0)
    high = jnp.where(value_lane, pltpu.roll(pairs, VALUE - HEAD, 1), 0.0)
    shape = (CHIPS, 1, PART // 2, LANES)
    upstream = jnp.concatenate([low.reshape(shape), high.reshape(shape)], axis=1)
    upstream = upstream.reshape(HALF, LANES)
    lane = lane_of((HALF, LANES))
    outputs = full[...]
    upstream *= jnp.sum(jnp.where(lane == 0, outputs, 0.0), axis=1, keepdims=True)
    weighted = jnp.sum(upstream * outputs, axis=1, keepdims=True)
    first = weighted.astype(bf16).astype(f32)
    upstream = jnp.where(lane == MASK + 4, -first, upstream)
    upstream = jnp.where(lane == MASK + 5, first - weighted, upstream).astype(bf16)
    grads[...] = upstream
    for b in range(count):
        rows, at = slice(b * WIDE_BLOCK, (b + 1) * WIDE_BLOCK), 2 * b * WIDE_BLOCK
        left[:, at : at + WIDE_BLOCK] = query_turned[:, rows]
        left[:, at + WIDE_BLOCK : at + 2 * WIDE_BLOCK] = jnp.transpose(upstream[rows])
    sums[...] = jnp.zeros_like(sums)

    def work(b, probs):
        rows = block(b)
        upstream = grads[rows, :]
        both = left[:, pl.ds(pl.multiple_of(2 * b * WIDE_BLOCK, 2 * WIDE_BLOCK), 2 * WIDE_BLOCK)]
        for at in range(0, 2 * HALF, WIDE_STEP):
            keys = slice(at, at + WIDE_STEP)
            part = probs[:, keys]
            grad = dot(upstream, keys_turned[:, keys])
            grad = (part.astype(f32) * grad).astype(bf16)
            sums[:, keys] += dot(both, jnp.concatenate([grad, part], axis=0))
            scores[keys, :] = jnp.transpose(grad)
        grad_query = jnp.transpose(dot(keys_turned[...], scores[...])) * SCALE
        own_out[rows, :] = pltpu.roll(grad_query, LANES - KEY, 1)

    def body(i, carry):
        fetched(2 * i, probs_a, 0).wait()
        work(2 * i, probs_a)

        @pl.when(2 * i + 2 < count)
        def _():
            fetched(2 * i + 2, probs_a, 0).start()

        fetched(2 * i + 1, probs_b, 1).wait()
        work(2 * i + 1, probs_b)

        @pl.when(2 * i + 3 < count)
        def _():
            fetched(2 * i + 3, probs_b, 1).start()

        return carry

    lax.fori_loop(0, count // 2, body, 0)
    scale = jnp.where(lane < VALUE, 1.0 / LOG2E, 1.0)
    rest = jnp.where(lane < MASK, jnp.transpose(sums[:, :HALF]) * scale, 0.0)
    own_out[...] = jnp.where(lane < KEY, own_out[...], rest)
    rest = jnp.where(
        (lane >= KEY) & (lane < MASK), jnp.transpose(sums[:, HALF:]) * scale, 0.0
    )
    other_out[...] = rest.astype(bf16)


def join_kernel(w_query, w_key, w_value, joined_out):
    blank = jnp.zeros((C, LANES - MASK), f32)
    parts = [w[...].astype(f32) for w in (w_query, w_key, w_value)]
    for head in range(HEADS):
        at = slice(head * HEAD, (head + 1) * HEAD)
        joined = jnp.concatenate([part[:, at] for part in parts] + [blank], axis=1)
        joined_out[:, head * LANES : (head + 1) * LANES] = joined.astype(bf16)


def widen_kernel(w_in, b_in, turned_out):
    wide = jnp.concatenate([w_in[...], bias_rows(b_in[...])], axis=0)
    turned_out[...] = jnp.transpose(wide)


def finish_kernel(
    place, rows, w_qkv, mixed, grad_first, slope, smooth, cond, w_out, result, back_out, parts_out
):
    joined = jnp.concatenate([rows[head] for head in range(HEADS)], axis=1)
    unit, rate = moments(mixed[...])
    latent = grad_first[...] + norm_back(unit, rate, dot_nt(joined, w_qkv[...]))
    branch = latent.astype(bf16)
    blank = jnp.zeros((CELLS, 384 - C), bf16)
    back = jnp.concatenate([result[...], blank, branch, blank], axis=1)
    back_out[...] = back.reshape(STRIPS, PART, 768)
    inner = (dot_nt(branch, w_out[...]) * slope[...]).astype(bf16)
    inner_turned = jnp.transpose(inner)
    branch_turned = jnp.transpose(branch)
    here, there = place[1], 1 - place[1]

    def put(side, at, values):
        values = values.astype(bf16)
        for t in range(0, 3 * LANES, LANES):
            parts_out[side, at : at + C, :] = values[:, t : t + LANES]
            at += C

    lane = lane_of((C, LANES))
    ones = jnp.zeros((C, LANES), f32)
    kept = None
    for n in range(10):
        moment = dot(inner_turned, cond[n]) if n < 9 else dot(branch_turned, cond[4])
        one = pltpu.roll(moment[:, LANES:], 3 * n, 1)
        ones = jnp.where((lane >= 64 + 3 * n) & (lane < 67 + 3 * n), one, ones)
        if n % 2 == 0:
            kept = moment[:, :CIN]
            continue
        both = jnp.concatenate([kept, moment[:, :CIN]], axis=1)
        pair = n // 2
        put(here if pair < 3 else there, 3 * C * (pair % 3), both)
    values = dot(branch_turned, smooth[...])
    last = jnp.concatenate([values[:, 2 * LANES :], ones[:, 64:]], axis=1)
    put(there, 6 * C, jnp.concatenate([values[:, : 2 * LANES], last], axis=1))
    for side in range(2):
        parts_out[side, 9 * C :, :] = jnp.zeros((SUM_ROWS - 9 * C, LANES), bf16)


def weights_kernel(
    place, mine, theirs, w_turned, w_conv, win_out, bin_out, wconv_out, bconv_out, wout_out,
    bout_out, taps, sems,
):
    here = place[1]

    def tile(half, n):
        rows = slice(C * n, C * (n + 1))
        return jnp.where(here == half, mine[rows, :], theirs[rows, :]).astype(f32)

    ones = tile(1, 8)
    lane = lane_of((C, LANES))
    low = lane < 64

    def moment_of(n):
        pair = n // 2
        first, middle, last = [tile(pair // 3, 3 * (pair % 3) + t) for t in range(3)]
        if n % 2:
            middle, last = pltpu.roll(middle, 64, 1), pltpu.roll(last, 64, 1)
            first, middle = jnp.where(low, middle, last), last
        one = jnp.where(lane < 67, pltpu.roll(ones, LANES - 3 * n, 1) if n else ones, 0.0)
        return jnp.concatenate([first, jnp.where(low, middle, one)], axis=1).astype(bf16)

    grad_in = jnp.zeros((C, WIDE), f32)
    copies = []
    for n in range(9):
        moment = moment_of(n)
        taps[n] = dot_nt(w_turned[...], moment)
        copy = pltpu.make_async_copy(taps.at[n], wconv_out.at[n], sems.at[n])
        copy.start()
        copies.append(copy)
        grad_in += dot(w_conv[n], moment)
    last = jnp.concatenate([tile(1, 6), tile(1, 7), ones], axis=1)
    last = jnp.transpose(last)
    wout_out[...] = last[:C]
    bconv_out[...] = last[C + 12]
    bout_out[...] = last[C + 27]
    grad_in = jnp.transpose(grad_in + moment_of(9).astype(f32))
    win_out[...] = grad_in[:CIN]
    bin_out[...] = grad_in[CIN]
    for copy in copies:
        copy.wait()


def swap(array):
    return lax.ppermute(array, "c", [(0, 1), (1, 0)])


def across(blocks, axes):
    return lax.all_to_all(blocks, axes, 0, 0, tiled=True)


def per_device(
    latent, condition, text_states, valid_rows, text_lengths, w_in, b_in, w_conv, b_conv, w_out,
    b_out, w_query, w_key, w_value, w_attn_out, b_attn_out, w_cross_query, w_cross_key,
    w_cross_value, w_cross_out, b_cross_out, w_ff_in, b_ff_in, w_ff_out, b_ff_out, cotangent,
):
    core, column = lax.axis_index("c"), 2 * lax.axis_index("x") + lax.axis_index("c")
    item, lower = lax.axis_index("a"), lax.axis_index("b")
    place = jnp.stack([item, core, column, lower]).astype(jnp.int32)

    wide = [
        jnp.pad(x.reshape(STRIPS, PART, -1), ((0, 0), (0, 0), (0, lanes - x.shape[-1])))
        for x, lanes in ((condition, 256), (latent, 384), (cotangent, 384))
    ]
    cells = across(jnp.concatenate(wide, axis=-1), "a")

    text = lax.dynamic_index_in_dim(text_states, item, 0, keepdims=False)
    text = jnp.pad(text, ((0, TEXT - text.shape[0]), (0, 0)))
    text_keys, text_values = call(
        text_kernel,
        (out(TEXT, 2 * WIDE), out(TEXT, 2 * WIDE)),
        (text, w_cross_key.T, w_cross_value.T),
        "text",
        scratch=[pltpu.VMEM((2 * WIDE, text.shape[1]), bf16)] * 2,
        fetch=(0, 1, 2),
        store=(0, 1),
        cost=pl.CostEstimate(flops=4 * 10**9, bytes_accessed=2 * 10**6, transcendentals=0),
    )
    (w_turned,) = call(
        widen_kernel, (out(C, WIDE),), (w_in, b_in), "widen", fetch=(0, 1), store=(0,)
    )
    cells, text_keys, w_turned = after(cells, text_keys, w_turned)

    here = cells[:, :, :WIDE].reshape(STRIPS, ROWS, COLS, WIDE)
    ends = jnp.concatenate([here[:, :1], here[:, ROWS - 1 :]], axis=1)
    beside = lax.ppermute(ends, "b", [(0, 1), (1, 0)])
    right_way = [(i, i + 1) for i in range(7)]

    def edge(col):
        rows = jnp.concatenate([here[:, :, col], beside[:, :, col]], axis=1)
        return rows.reshape(STRIPS * (ROWS + 2), WIDE)

    left = lax.ppermute(edge(COLS - 1), ("x", "c"), right_way)
    right = lax.ppermute(edge(0), ("x", "c"), [(b, a) for a, b in right_way])
    beside, first_bias = after(beside, b_in)
    (
        w_in_here, b_in_here, taps_here, b_conv_here, w_out_here, b_out_here, w_query_here,
        w_key_here, w_value_here,
    ) = bring(
        [
            w_in, first_bias, w_conv.reshape(9, C, C), b_conv, w_out, b_out, w_query, w_key,
            w_value,
        ],
        "load_adapter",
    )
    rows, mixed, smooth, slope, cond = call(
        adapter_kernel,
        (
            out(HEADS, CELLS, LANES),
            out(CELLS, C, dtype=f32),
            out(CELLS, C),
            out(CELLS, C, dtype=f32),
            out(9, CELLS, WIDE),
        ),
        (
            place, valid_rows, cells, beside, left, right, w_in_here, b_in_here, taps_here,
            b_conv_here, w_out_here, b_out_here, w_query_here, w_key_here, w_value_here,
        ),
        "adapter",
        scalars=2,
        scratch=[pltpu.VMEM((WIDE, C), bf16)],
        vmem=24,
        store=(1, 2, 3, 4),
        near=(0,),
        held=tuple(range(6, 15)),
    )

    own = across(rows, GROUP_OF_ITEM).reshape(HALF, LANES)

    other = swap(own)
    _, attn_weight = after(own, w_attn_out)
    w_cross_query_wide, w_cross_out_wide, w_attn_spread = call(
        form_kernel,
        (out(C, 2 * WIDE), out(2 * WIDE, C), out(HEADS * LANES, 768)),
        (w_cross_query, w_cross_out, attn_weight),
        "form",
        fetch=(2, 0, 1),
        store=(0, 1),
        near=(2,),
    )
    own, w_attn_spread = after(own, w_attn_spread)
    packed, full, probs, keys_turned, query_turned = call(
        attend_kernel,
        (
            out(CHIPS, PART // 2, LANES),
            out(HALF, LANES, dtype=f32),
            out(HALF, 2 * HALF),
            out(LANES, 2 * HALF),
            out(LANES, HALF),
        ),
        (own, other),
        "attend",
        scratch=[
            pltpu.VMEM((2 * HALF, BLOCK), f32),
            pltpu.VMEM((2 * HALF, BLOCK), f32),
            pltpu.VMEM((2 * HALF, BLOCK), bf16),
            pltpu.VMEM((2 * HALF, BLOCK), bf16),
            pltpu.VMEM((BLOCK, 2 * HALF), bf16),
            pltpu.VMEM((BLOCK, 2 * HALF), bf16),
            pltpu.VMEM((LANES, HALF), f32),
            pltpu.SemaphoreType.DMA((2,)),
        ],
        vmem=32,
        store=(1, 3, 4),
        near=(0,),
        far=(4,),
    )

    heads_in = across(packed.reshape(HEADS, CELLS // 2, LANES), GROUP_OF_ITEM)
    result, grad_first, heads_out = call(
        middle_kernel,
        (out(CELLS, C), out(CELLS, C, dtype=f32), out(HEADS, CELLS // 2, LANES)),
        (
            place, text_lengths, heads_in, mixed, cells, text_keys, text_values,
            w_attn_spread, b_attn_out, w_cross_query_wide, w_cross_out_wide, b_cross_out,
            w_ff_in, b_ff_in, w_ff_out.T, b_ff_out,
        ),
        "middle",
        scalars=2,
        scratch=[pltpu.VMEM((CELLS, HEADS * TEXT), f32)],
        vmem=32,
        fetch=(3, 8, 9, 5, 6, 10, 11, 12, 13, 14, 15),
        store=(0, 1),
        near=(2,),
        held=(7,),
    )

    grads_in = across(heads_out, GROUP_OF_ITEM).reshape(CHIPS, PART // 2, LANES)
    own_grads, other_grads = call(
        attend_back_kernel,
        (out(HALF, LANES, dtype=f32), out(HALF, LANES)),
        (keys_turned, query_turned, full, grads_in, probs),
        "attend_back",
        scratch=[
            pltpu.VMEM((HALF, LANES), bf16),
            pltpu.VMEM((LANES, 2 * HALF), bf16),
            pltpu.VMEM((LANES, 2 * HALF), f32),
            pltpu.VMEM((2 * HALF, WIDE_BLOCK), bf16),
            pltpu.VMEM((WIDE_BLOCK, 2 * HALF), bf16),
            pltpu.VMEM((WIDE_BLOCK, 2 * HALF), bf16),
            pltpu.SemaphoreType.DMA((2,)),
        ],
        vmem=36,
        near=(0, 1),
        far=(4,),
    )

    _, query_weight = after(other_grads, w_query)
    (w_joined,) = call(
        join_kernel,
        (out(C, HEADS * LANES),),
        (query_weight, w_key, w_value),
        "join",
        fetch=(0, 1, 2),
        near=(0,),
    )
    own_grads, w_joined = after(own_grads, w_joined)
    row_grads = (own_grads + swap(other_grads).astype(f32)).astype(bf16)
    row_grads = across(row_grads.reshape(HEADS, CELLS, LANES), GROUP_OF_ITEM)
    back, parts = call(
        finish_kernel,
        (out(STRIPS, PART, 768), out(2, SUM_ROWS, LANES)),
        (
            place, row_grads, w_joined, mixed, grad_first, slope, smooth, cond, w_out, result,
        ),
        "finish",
        scalars=1,
        store=(0,),
    )

    shares = (parts[0].astype(f32) + swap(parts[1]).astype(f32)).astype(bf16)
    shares = across(shares.reshape(CHIPS, SUM_ROWS // CHIPS, LANES), CHIPS_ALL)
    share = jnp.sum(shares.astype(f32), axis=0).astype(bf16)
    mine = across(jnp.broadcast_to(share[None], shares.shape), CHIPS_ALL)
    mine = mine.reshape(SUM_ROWS, LANES)

    mine, back = after(mine, back)
    back = across(back, "a")
    theirs = swap(mine)
    grad_w_in, grad_b_in, grad_w_conv, grad_b_conv, grad_w_out, grad_b_out = call(
        weights_kernel,
        (
            out(CIN, C, dtype=f32),
            out(C, dtype=f32),
            out(9, C, C, dtype=f32),
            out(C, dtype=f32),
            out(C, C, dtype=f32),
            out(C, dtype=f32),
        ),
        (place, mine, theirs, w_turned, w_conv.reshape(9, C, C)),
        "weights",
        scalars=1,
        scratch=[
            pltpu.VMEM((9, C, C), f32),
            pltpu.SemaphoreType.DMA((9,)),
        ],
        vmem=24,
        fetch=(3, 4),
        store=(0, 4),
        far=(7,),
        cost=pl.CostEstimate(flops=6 * 10**9, bytes_accessed=2 * 10**7, transcendentals=0),
    )
    back, grad_b_in = after(back, grad_b_in)
    grid = (STRIPS, ROWS, COLS, C)
    return (
        back[:, :, :C].reshape(grid),
        back[:, :, 384 : 384 + C].reshape(grid).astype(f32),
        grad_w_in,
        grad_b_in,
        grad_w_conv.reshape(3, 3, C, C),
        grad_b_conv,
        grad_w_out,
        grad_b_out,
    )


def solution(mesh):
    split = Mesh(mesh.devices.reshape(8, 2, 4, 2), ("a", "b", "x", "c"))
    cells = P(None, ("a", "b"), ("x", "c"), None)
    in_specs = (cells, cells) + (P(),) * 23 + (cells,)
    out_specs = (cells, cells) + (P(),) * 6
    return jax.shard_map(
        per_device, mesh=split, in_specs=in_specs, out_specs=out_specs, check_vma=False
    )
```

```python
import jax
import jax.numpy as jnp
from jax import lax
from jax.experimental import pallas as pl
from jax.experimental.pallas import tpu as pltpu
from jax.sharding import Mesh
from jax.sharding import PartitionSpec as P

STRIPS, ROWS, COLS, C, CIN, HEADS, HEAD, FF = 8, 4, 8, 320, 192, 8, 40, 1280
CELLS = STRIPS * ROWS * COLS
PART = ROWS * COLS
CHIPS = 64
HALF = CHIPS * PART
TEXT = 128
LANES = 128
WIDE = 256
GROUP = 160
SCALE = HEAD**-0.5
LOG2E = 1.4426950408889634
EPS = 1e-5
MASKED = -1e30
KEY, VALUE, MASK = HEAD, 2 * HEAD, 3 * HEAD
GROUP_OF_ITEM, CHIPS_ALL = ("b", "x"), ("a", "b", "x")
LATENT, COTANGENT = 256, 640
SUM_ROWS = 3072
SHARE = SUM_ROWS // CHIPS

bf16, f32 = jnp.bfloat16, jnp.float32
NT = (((1,), (1,)), ((), ()))


def dot(left, right):
    return jnp.dot(left, right, preferred_element_type=f32)


def dot_nt(left, right):
    return lax.dot_general(left, right, NT, preferred_element_type=f32)


def lane_of(shape):
    return lax.broadcasted_iota(jnp.int32, shape, len(shape) - 1)


def moments(values):
    center = values - jnp.mean(values, -1, keepdims=True)
    rate = lax.rsqrt(jnp.mean(center * center, -1, keepdims=True) + EPS)
    return center * rate, rate


def norm_back(unit, rate, grads):
    return rate * (
        grads
        - jnp.mean(grads, -1, keepdims=True)
        - unit * jnp.mean(grads * unit, -1, keepdims=True)
    )


class Fetched:
    def __init__(self, source, buffer, semaphore):
        self.copy = pltpu.make_async_copy(source, buffer, semaphore)
        self.buffer, self.shape, self.here = buffer, buffer.shape, False
        self.copy.start()

    def __getitem__(self, index):
        if not self.here:
            self.copy.wait()
            self.here = True
        return self.buffer[index]


class Stored:
    def __init__(self, target, buffer, semaphore):
        self.copy = pltpu.make_async_copy(buffer, target, semaphore)
        self.buffer, self.started = buffer, False

    def __setitem__(self, index, values):
        self.buffer[index] = values
        if index is Ellipsis:
            self.start()

    def start(self):
        if not self.started:
            self.copy.start()
            self.started = True


def call(kernel, outs, ins, name, scalars=0, scratch=(), vmem=16, fetch=(), store=(), far=(),
    near=(), held=(), cost=None,
):
    fetch, store = list(fetch), list(store)
    far_in = [i for i in far if i < len(ins)]
    far_out = [i - len(ins) for i in far if i >= len(ins)]

    def body(*refs):
        refs = list(refs)
        given, refs = refs[: len(ins)], refs[len(ins) :]
        made, refs = refs[: len(outs)], refs[len(outs) :]
        own, refs = refs[: len(scratch)], refs[len(scratch) :]
        buffers, semaphores = refs[:-1], refs[-1] if refs else None
        for n, i in enumerate(fetch):
            given[i] = Fetched(given[i], buffers[n], semaphores.at[n])
        kept = []
        for n, i in enumerate(store, len(fetch)):
            made[i] = Stored(made[i], buffers[n], semaphores.at[n])
            kept.append(made[i])
        kernel(*given, *made, *own)
        for part in given:
            if isinstance(part, Fetched) and not part.here:
                part.copy.wait()
        for part in kept:
            part.start()
        for part in kept:
            part.copy.wait()

    def made_as(i, made):
        if i in store or i in far_out:
            return pltpu.HBM(made.shape, made.dtype)
        return pltpu.VMEM(made.shape, made.dtype) if i in near else made

    def in_spec(i):
        if i < scalars:
            return pl.BlockSpec(memory_space=pltpu.SMEM)
        space = pltpu.HBM if i in fetch or i in far_in else pltpu.VMEM
        return pl.BlockSpec(memory_space=space)

    def out_spec(i):
        space = pltpu.HBM if i in store or i in far_out else pltpu.VMEM
        return pl.BlockSpec(memory_space=space)

    extra = [pltpu.VMEM(ins[i].shape, ins[i].dtype) for i in fetch]
    extra += [pltpu.VMEM(outs[i].shape, outs[i].dtype) for i in store]
    if extra:
        extra.append(pltpu.SemaphoreType.DMA((len(extra),)))
    return pl.pallas_call(
        body,
        out_shape=tuple(made_as(i, made) for i, made in enumerate(outs)),
        in_specs=[in_spec(i) for i in range(len(ins))],
        out_specs=tuple(out_spec(i) for i in range(len(outs))),
        scratch_shapes=list(scratch) + extra,
        compiler_params=pltpu.CompilerParams(vmem_limit_bytes=vmem << 20),
        cost_estimate=cost,
        name=name,
    )(
        *(
            pltpu.with_memory_space_constraint(x, pltpu.HBM)
            if i in fetch or i in far_in
            else (pltpu.with_memory_space_constraint(x, pltpu.VMEM) if i in held else x)
            for i, x in enumerate(ins)
        )
    )


def bring(arrays, name, kernel=None, made=(), near=()):
    count, given = len(arrays), len(near)

    def body(*refs):
        sources, inputs = refs[:count], refs[count : count + given]
        targets = refs[count + given : -1]
        copies = [
            pltpu.make_async_copy(sources[n], targets[n], refs[-1].at[n]) for n in range(count)
        ]
        for copy in copies:
            copy.start()
        if kernel is not None:
            kernel(*inputs, *targets[count:])
        for copy in copies:
            copy.wait()

    shapes = [jax.ShapeDtypeStruct(x.shape, x.dtype) for x in arrays] + list(made)
    return pl.pallas_call(
        body,
        out_shape=tuple(pltpu.VMEM(x.shape, x.dtype) for x in shapes),
        in_specs=[pl.BlockSpec(memory_space=pltpu.HBM)] * count
        + [pl.BlockSpec(memory_space=pltpu.VMEM)] * given,
        out_specs=(pl.BlockSpec(memory_space=pltpu.VMEM),) * len(shapes),
        scratch_shapes=[pltpu.SemaphoreType.DMA((max(count, 1),))],
        compiler_params=pltpu.CompilerParams(vmem_limit_bytes=8 << 20),
        name=name,
    )(*(pltpu.with_memory_space_constraint(x, pltpu.HBM) for x in arrays), *near)


def after(value, *arrays):
    return lax.optimization_barrier((value,) + arrays)


def out(*shape, dtype=bf16):
    return jax.ShapeDtypeStruct(shape, dtype)


def bias_rows(bias):
    row = lax.broadcasted_iota(jnp.int32, (WIDE - CIN, C), 0)
    rest = jnp.broadcast_to(bias, (WIDE - CIN, C))
    rows = jnp.zeros((WIDE - CIN, C), f32)
    for n in range(3):
        piece = rest.astype(bf16).astype(f32)
        rows = jnp.where(row == n, piece, rows)
        rest = rest - piece
    return rows.astype(bf16)


def adapter_kernel(
    place, valid, cells, beside, left, right, w_in, b_in, w_conv, b_conv, w_out,
    b_out, w_query, w_key, w_value, rows_out, mixed_out, smooth_out, slope_out, cond_out,
    w_wide,
):
    span = STRIPS * (ROWS + 2)
    w_wide[:CIN, :] = w_in[...]
    w_wide[CIN:, :] = bias_rows(b_in[...])
    upper = place[3] == 0

    def tall(own, first, last):
        blank = jnp.zeros_like(first[:1])
        above = jnp.where(upper, jnp.concatenate([blank, last[:-1]], axis=0), last)
        below = jnp.where(upper, first, jnp.concatenate([first[1:], blank], axis=0))
        return jnp.concatenate([above, own, below], axis=1)

    own = cells[:, :, :WIDE].astype(f32).reshape(STRIPS, ROWS, COLS, WIDE)
    other = beside[...].astype(f32)
    block = tall(own, other[:, :1], other[:, 1:]).reshape(span, COLS, WIDE)
    shape = (STRIPS, ROWS + 2, COLS, WIDE)
    row = 2 * ROWS * lax.broadcasted_iota(jnp.int32, shape, 0) + ROWS * place[3] - 1
    row += lax.broadcasted_iota(jnp.int32, shape, 1)
    inside = (row >= 0) & (row < ROWS * 16)
    inside = jnp.where(inside, 1.0, 0.0).reshape(span, COLS, WIDE)
    lane = lane_of((span, COLS, WIDE))
    col = lax.broadcasted_iota(jnp.int32, (span, COLS, WIDE), 1)
    at = COLS * place[2]
    edges = []
    for n, side in enumerate((left, right)):
        there = (at > 0) if n == 0 else (at < COLS * 7)
        side = side[...].astype(f32).reshape(span, 1, WIDE)
        side = side.reshape(STRIPS, ROWS + 2, 1, WIDE)
        side = tall(side[:, :ROWS], side[:, ROWS : ROWS + 1], side[:, ROWS + 1 :])
        edges.append((side.reshape(span, 1, WIDE), jnp.where(there, inside, 0.0)))
    near = jnp.where(col == 0, edges[0][0], pltpu.roll(block, 1, 1))
    near_inside = jnp.where(col == 0, edges[0][1], inside)
    far = jnp.where(col == COLS - 1, edges[1][0], pltpu.roll(block, COLS - 1, 1))
    far_inside = jnp.where(col == COLS - 1, edges[1][1], inside)
    inner = jnp.zeros((CELLS, C), f32)
    start_here = None
    one = (lane >= CIN) & (lane < CIN + 3)
    moves = ((near, near_inside), (block, inside), (far, far_inside))
    for j, (moved, present) in enumerate(moves):
        moved = jnp.where(one, present, moved)
        start = dot(moved.reshape(span * COLS, WIDE).astype(bf16), w_wide[...])
        start = start.reshape(STRIPS, ROWS + 2, COLS, C)
        moved = moved.reshape(STRIPS, ROWS + 2, COLS, WIDE)
        for i in range(3):
            patch = start[:, i : i + ROWS].reshape(CELLS, C).astype(bf16)
            if i == 1 and j == 1:
                start_here = patch.astype(f32)
            inner += dot(patch, w_conv[3 * i + j])
            cond_out[3 * i + j] = moved[:, i : i + ROWS].reshape(CELLS, WIDE).astype(bf16)
    inner += b_conv[...]
    gate = jax.nn.sigmoid(inner)
    smooth = (inner * gate).astype(bf16)
    smooth_out[...] = smooth
    slope_out[...] = gate * (1.0 + inner * (1.0 - gate))
    latent = cells[:, :, LATENT : LATENT + C].astype(f32).reshape(CELLS, C)
    mixed = latent + (start_here + dot(smooth, w_out[...]) + b_out[...])
    mixed_out[...] = mixed
    normed = moments(mixed)[0].astype(bf16)
    projected = [dot(normed, w[...]) for w in (w_query, w_key, w_value)]
    projected[0] *= SCALE * LOG2E
    shape = (STRIPS, ROWS, COLS, LANES - MASK)
    row = 2 * ROWS * lax.broadcasted_iota(jnp.int32, shape, 0) + ROWS * place[3]
    row += lax.broadcasted_iota(jnp.int32, shape, 1)
    hidden = jnp.where(row >= valid[place[0]], MASKED, 0.0)
    extras = jnp.where(lane_of(shape) == 0, hidden, 1.0).reshape(CELLS, LANES - MASK)
    for head in range(HEADS):
        at = slice(head * HEAD, (head + 1) * HEAD)
        joined = jnp.concatenate([part[:, at] for part in projected] + [extras], axis=1)
        rows_out[head] = joined.astype(bf16)


def text_kernel(
    text, w_key_turned, w_value_turned, keys_out, values_out, wide_key, wide_value
):
    blank = jnp.zeros((WIDE - GROUP, text.shape[1]), bf16)
    states = text[...]
    both = ((w_key_turned, wide_key, keys_out), (w_value_turned, wide_value, values_out))
    for source, wide, target in both:
        for g in range(2):
            wide[g * WIDE : g * WIDE + GROUP, :] = source[g * GROUP : (g + 1) * GROUP, :]
            wide[g * WIDE + GROUP : (g + 1) * WIDE, :] = blank
        target[...] = dot_nt(states, wide[...]).astype(bf16)


def form_kernel(w_query, w_cross_out, w_attn, query_out, cross_out, spread_out):
    rows = w_query[...].astype(f32)
    blank = jnp.zeros((C, WIDE - GROUP), f32)
    rows = [rows[:, :GROUP], blank, rows[:, GROUP:], blank]
    query_out[...] = jnp.concatenate(rows, axis=1).astype(bf16)
    rows = w_cross_out[...]
    blank = jnp.zeros((WIDE - GROUP, C), bf16)
    cross_out[...] = jnp.concatenate([rows[:GROUP], blank, rows[GROUP:], blank], axis=0)
    rows = w_attn[...].astype(f32)
    gap = jnp.zeros((HEAD, 384 - C), f32)
    for head in range(HEADS):
        part = jnp.concatenate([rows[head * HEAD : (head + 1) * HEAD], gap], axis=1)
        blank = jnp.zeros_like(part)
        block = jnp.concatenate(
            [
                jnp.concatenate([part, blank], axis=1),
                jnp.concatenate([blank, part], axis=1),
                jnp.zeros((LANES - 2 * HEAD, 768), f32),
            ],
            axis=0,
        )
        spread_out[head * LANES : (head + 1) * LANES, :] = block.astype(bf16)


BLOCK = 256
STEP = 512


def attend_kernel(
    own, other, packed_out, full_out, probs_out, keys_out, query_out,
    scores_a, scores_b, probs_a, probs_b, turned_a, turned_b, output, sems,
):
    count = HALF // BLOCK
    keys_turned, query = keys_out.buffer, query_out.buffer
    keys_turned[:, :HALF] = jnp.transpose(own[...])
    keys_turned[:, HALF:] = jnp.transpose(other[...])
    keys_out.start()
    lane = lane_of((HALF, LANES))
    rows = pltpu.roll(own[...].astype(f32), KEY, 1)
    rows = jnp.where((lane >= KEY) & (lane < VALUE), rows, jnp.where(lane == MASK, 1.0, 0.0))
    query_out[...] = jnp.transpose(rows.astype(bf16))
    chunks = [(ref, at) for ref in (own, other) for at in range(0, HALF, STEP)]

    def columns(b):
        return pl.ds(pl.multiple_of(b * BLOCK, BLOCK), BLOCK)

    def score(queries, n, scores, peak):
        ref, at = chunks[n]
        part = dot(ref[at : at + STEP, :], queries)
        scores[n * STEP : (n + 1) * STEP, :] = part
        part = jnp.max(part.reshape(STEP // 8, 8, BLOCK), axis=0)
        return part if peak is None else jnp.maximum(peak, part)

    def sent(b, turned, n):
        return pltpu.make_async_copy(turned, probs_out.at[columns(b)], sems.at[n])

    def half(b, peak, following, scores, probs, turned):
        shift = jnp.max(peak, axis=0, keepdims=True)
        queries = query[:, columns(jnp.minimum(b + 1, count - 1))]
        ahead = None
        for n in range(len(chunks)):
            ahead = score(queries, n, following, ahead)
            keys = slice(n * STEP, (n + 1) * STEP)
            part = jnp.exp2(scores[keys, :] - shift).astype(bf16)
            probs[keys, :] = part
            turned[:, keys] = jnp.transpose(part)
        output[:, columns(b)] = dot(keys_turned[...], probs[...])
        return ahead

    peak = None
    for n in range(len(chunks)):
        peak = score(query[:, :BLOCK], n, scores_a, peak)

    def body(i, peak):
        @pl.when(i > 0)
        def _():
            sent(2 * i - 2, turned_a, 0).wait()

        peak = half(2 * i, peak, scores_b, scores_a, probs_a, turned_a)
        sent(2 * i, turned_a, 0).start()

        @pl.when(i > 0)
        def _():
            sent(2 * i - 1, turned_b, 1).wait()

        peak = half(2 * i + 1, peak, scores_a, scores_b, probs_b, turned_b)
        sent(2 * i + 1, turned_b, 1).start()
        return peak

    lax.fori_loop(0, count // 2, body, peak)
    total = output[...]
    inverse = 1.0 / total[MASK + 1 : MASK + 2, :]
    row = lax.broadcasted_iota(jnp.int32, (LANES, HALF), 0)
    total = jnp.transpose(jnp.where(row == 0, inverse, total * inverse))
    full_out[...] = total
    pairs = total.reshape(CHIPS, 2, PART // 2, LANES)
    lane = lane_of((HALF // 2, LANES))
    low = pltpu.roll(pairs[:, 0].reshape(HALF // 2, LANES), LANES - VALUE, 1)
    high = pltpu.roll(pairs[:, 1].reshape(HALF // 2, LANES), LANES - VALUE + HEAD, 1)
    packed = jnp.where(lane < HEAD, low, jnp.where(lane < 2 * HEAD, high, 0.0))
    packed_out[...] = packed.astype(bf16).reshape(CHIPS, PART // 2, LANES)
    sent(count - 2, turned_a, 0).wait()
    sent(count - 1, turned_b, 1).wait()


def middle_kernel(
    place, lengths, heads_in, mixed, cells, text_keys, text_values, w_attn, b_attn,
    w_cross_query, w_cross_out, b_cross, w_ff_in, b_ff_in, w_ff_turned, b_ff_out, result_out,
    grad_out, heads_out, probs_keep,
):
    half = CELLS // 2
    split = w_attn.shape[1] // 2
    packed = jnp.concatenate([heads_in[head] for head in range(HEADS)], axis=1)
    both = dot(packed, w_attn[...])
    shape = (STRIPS, 1, PART // 2, C)
    attended = jnp.concatenate(
        [both[:, :C].reshape(shape), both[:, split : split + C].reshape(shape)], axis=1
    ).reshape(CELLS, C)
    first = mixed[...] + attended + b_attn[...]
    unit_two, rate_two = moments(first)
    cross_query = dot(unit_two.astype(bf16), w_cross_query[...]).astype(bf16)
    lane = lane_of((TEXT, WIDE))
    in_head = [(lane >= HEAD * h) & (lane < HEAD * (h + 1)) for h in range(HEADS // 2)]
    groups = [slice(0, WIDE), slice(WIDE, 2 * WIDE)]

    def by_head(text):
        kept = []
        for lanes in groups:
            here = text[:, lanes]
            kept.append(
                jnp.concatenate([jnp.where(m, here, jnp.zeros_like(here)) for m in in_head], 0)
            )
        return kept

    keys, values = by_head(text_keys), by_head(text_values)
    spans = [slice(g * HEADS // 2 * TEXT, (g + 1) * HEADS // 2 * TEXT) for g in range(2)]
    heads = [slice(h * TEXT, (h + 1) * TEXT) for h in range(HEADS)]
    token = lane_of((CELLS, TEXT)) < lengths[place[0]]
    scores = [dot_nt(cross_query[:, groups[g]], keys[g]) * SCALE for g in range(2)]
    scores = jnp.concatenate(scores, axis=1)
    for at in heads:
        part = jnp.where(token, scores[:, at], MASKED)
        weights = jnp.exp(part - jnp.max(part, -1, keepdims=True))
        probs_keep[:, at] = weights / jnp.sum(weights, -1, keepdims=True)
    cross = [dot(probs_keep[:, spans[g]].astype(bf16), values[g]) for g in range(2)]
    cross = jnp.concatenate(cross, axis=1).astype(bf16)
    second = first + dot(cross, w_cross_out[...]) + b_cross[...]
    unit_three, rate_three = moments(second)
    normed_three = unit_three.astype(bf16)
    upstream = cells[:, :, COTANGENT : COTANGENT + C].reshape(CELLS, C)
    result = second + b_ff_out[...]
    grad_normed = jnp.zeros((CELLS, C), f32)
    step = 256
    for at in range(0, FF, step):
        ups, gates = slice(at, at + step), slice(FF + at, FF + at + step)
        value = dot(normed_three, w_ff_in[:, ups]) + b_ff_in[ups]
        gate = dot(normed_three, w_ff_in[:, gates]) + b_ff_in[gates]
        normal = 0.5 + 0.5 * lax.erf(gate * (0.5**0.5))
        density = jnp.exp(gate * gate * -0.5) * 0.3989422804014327
        gelu = gate * normal
        result += dot_nt((value * gelu).astype(bf16), w_ff_turned[:, ups])
        grad_act = dot(upstream, w_ff_turned[:, ups])
        grad_value = (grad_act * gelu).astype(bf16)
        grad_gate = (grad_act * value * (normal + gate * density)).astype(bf16)
        grad_normed += dot_nt(grad_value, w_ff_in[:, ups])
        grad_normed += dot_nt(grad_gate, w_ff_in[:, gates])
    result_out[...] = result.astype(bf16)
    grad_second = upstream.astype(f32) + norm_back(unit_three, rate_three, grad_normed)
    grad_cross = dot_nt(grad_second.astype(bf16), w_cross_out[...]).astype(bf16)
    grad_probs = [dot_nt(grad_cross[:, groups[g]], values[g]) for g in range(2)]
    grad_probs = jnp.concatenate(grad_probs, axis=1)
    grad_scores = []
    for at in heads:
        probs, grads = probs_keep[:, at], grad_probs[:, at]
        weighted = jnp.sum(probs * grads, -1, keepdims=True)
        grad_scores.append((probs * (grads - weighted)).astype(bf16))
    grad_scores = jnp.concatenate(grad_scores, axis=1)
    grad_query = [dot(grad_scores[:, spans[g]], keys[g]) for g in range(2)]
    grad_query = (jnp.concatenate(grad_query, axis=1) * SCALE).astype(bf16)
    grad_first = grad_second + norm_back(
        unit_two, rate_two, dot_nt(grad_query, w_cross_query[...])
    )
    grad_out[...] = grad_first
    pairs = grad_first.reshape(STRIPS, 2, PART // 2, C)
    gap = jnp.zeros((half, split - C), f32)
    both = jnp.concatenate(
        [pairs[:, 0].reshape(half, C), gap, pairs[:, 1].reshape(half, C), gap], axis=1
    ).astype(bf16)
    packed = dot_nt(both, w_attn[...]).astype(bf16)
    for head in range(HEADS):
        heads_out[head] = packed[:, head * LANES : (head + 1) * LANES]


WIDE_BLOCK = 512
WIDE_STEP = 1024


def attend_back_kernel(
    keys_turned, query_turned, full, packed, probs_in, own_out, other_out,
    grads, left, sums, scores, probs_a, probs_b, sems,
):
    half, count = HALF // 2, HALF // WIDE_BLOCK

    def block(b):
        return pl.ds(pl.multiple_of(b * WIDE_BLOCK, WIDE_BLOCK), WIDE_BLOCK)

    def fetched(b, probs, n):
        return pltpu.make_async_copy(probs_in.at[block(b)], probs, sems.at[n])

    fetched(0, probs_a, 0).start()
    fetched(1, probs_b, 1).start()
    lane = lane_of((half, LANES))
    value_lane = (lane >= VALUE) & (lane < MASK)
    pairs = packed[...].reshape(half, LANES).astype(f32)
    low = jnp.where(value_lane, pltpu.roll(pairs, VALUE, 1), 0.0)
    high = jnp.where(value_lane, pltpu.roll(pairs, VALUE - HEAD, 1), 0.0)
    shape = (CHIPS, 1, PART // 2, LANES)
    upstream = jnp.concatenate([low.reshape(shape), high.reshape(shape)], axis=1)
    upstream = upstream.reshape(HALF, LANES)
    lane = lane_of((HALF, LANES))
    outputs = full[...]
    upstream *= jnp.sum(jnp.where(lane == 0, outputs, 0.0), axis=1, keepdims=True)
    weighted = jnp.sum(upstream * outputs, axis=1, keepdims=True)
    first = weighted.astype(bf16).astype(f32)
    upstream = jnp.where(lane == MASK + 4, -first, upstream)
    upstream = jnp.where(lane == MASK + 5, first - weighted, upstream).astype(bf16)
    grads[...] = upstream
    for b in range(count):
        rows, at = slice(b * WIDE_BLOCK, (b + 1) * WIDE_BLOCK), 2 * b * WIDE_BLOCK
        left[:, at : at + WIDE_BLOCK] = query_turned[:, rows]
        left[:, at + WIDE_BLOCK : at + 2 * WIDE_BLOCK] = jnp.transpose(upstream[rows])
    sums[...] = jnp.zeros_like(sums)

    def work(b, probs):
        rows = block(b)
        upstream = grads[rows, :]
        both = left[:, pl.ds(pl.multiple_of(2 * b * WIDE_BLOCK, 2 * WIDE_BLOCK), 2 * WIDE_BLOCK)]
        for at in range(0, 2 * HALF, WIDE_STEP):
            keys = slice(at, at + WIDE_STEP)
            part = probs[:, keys]
            grad = dot(upstream, keys_turned[:, keys])
            grad = (part.astype(f32) * grad).astype(bf16)
            sums[:, keys] += dot(both, jnp.concatenate([grad, part], axis=0))
            scores[keys, :] = jnp.transpose(grad)
        grad_query = jnp.transpose(dot(keys_turned[...], scores[...])) * SCALE
        own_out[rows, :] = pltpu.roll(grad_query, LANES - KEY, 1)

    def body(i, carry):
        fetched(2 * i, probs_a, 0).wait()
        work(2 * i, probs_a)

        @pl.when(2 * i + 2 < count)
        def _():
            fetched(2 * i + 2, probs_a, 0).start()

        fetched(2 * i + 1, probs_b, 1).wait()
        work(2 * i + 1, probs_b)

        @pl.when(2 * i + 3 < count)
        def _():
            fetched(2 * i + 3, probs_b, 1).start()

        return carry

    lax.fori_loop(0, count // 2, body, 0)
    scale = jnp.where(lane < VALUE, 1.0 / LOG2E, 1.0)
    rest = jnp.where(lane < MASK, jnp.transpose(sums[:, :HALF]) * scale, 0.0)
    own_out[...] = jnp.where(lane < KEY, own_out[...], rest)
    rest = jnp.where(
        (lane >= KEY) & (lane < MASK), jnp.transpose(sums[:, HALF:]) * scale, 0.0
    )
    other_out[...] = rest.astype(bf16)


def join_kernel(w_query, w_key, w_value, joined_out):
    blank = jnp.zeros((C, LANES - MASK), f32)
    parts = [w[...].astype(f32) for w in (w_query, w_key, w_value)]
    for head in range(HEADS):
        at = slice(head * HEAD, (head + 1) * HEAD)
        joined = jnp.concatenate([part[:, at] for part in parts] + [blank], axis=1)
        joined_out[:, head * LANES : (head + 1) * LANES] = joined.astype(bf16)


def unpack_kernel(parcel, result_out, latent_out):
    for item in range(STRIPS):
        tiles = [
            parcel[item, SHARE + PART * t : SHARE + PART * (t + 1), :] for t in range(6)
        ]
        result_out[item] = jnp.concatenate(tiles[:3], axis=1)[:, :C]
        latent_out[item] = jnp.concatenate(tiles[3:], axis=1)[:, :C].astype(f32)


def widen_kernel(w_in, b_in, turned_out):
    wide = jnp.concatenate([w_in[...], bias_rows(b_in[...])], axis=0)
    turned_out[...] = jnp.transpose(wide)


def finish_kernel(
    place, rows, w_qkv, mixed, grad_first, slope, smooth, cond, w_out, result, back_out, parts_out
):
    joined = jnp.concatenate([rows[head] for head in range(HEADS)], axis=1)
    unit, rate = moments(mixed[...])
    latent = grad_first[...] + norm_back(unit, rate, dot_nt(joined, w_qkv[...]))
    branch = latent.astype(bf16)
    blank = jnp.zeros((CELLS, 384 - C), bf16)
    back = jnp.concatenate([result[...], blank, branch, blank], axis=1)
    for t in range(6):
        back_out[:, t] = back[:, t * LANES : (t + 1) * LANES].reshape(STRIPS, PART, LANES)
    inner = (dot_nt(branch, w_out[...]) * slope[...]).astype(bf16)
    inner_turned = jnp.transpose(inner)
    branch_turned = jnp.transpose(branch)
    here, there = place[1], 1 - place[1]

    def put(side, at, values):
        values = values.astype(bf16)
        for t in range(0, 3 * LANES, LANES):
            parts_out[side, at : at + C, :] = values[:, t : t + LANES]
            at += C

    lane = lane_of((C, LANES))
    ones = jnp.zeros((C, LANES), f32)
    kept = None
    for n in range(10):
        moment = dot(inner_turned, cond[n]) if n < 9 else dot(branch_turned, cond[4])
        one = pltpu.roll(moment[:, LANES:], 3 * n, 1)
        ones = jnp.where((lane >= 64 + 3 * n) & (lane < 67 + 3 * n), one, ones)
        if n % 2 == 0:
            kept = moment[:, :CIN]
            continue
        both = jnp.concatenate([kept, moment[:, :CIN]], axis=1)
        pair = n // 2
        put(here if pair < 3 else there, 3 * C * (pair % 3), both)
    values = dot(branch_turned, smooth[...])
    last = jnp.concatenate([values[:, 2 * LANES :], ones[:, 64:]], axis=1)
    put(there, 6 * C, jnp.concatenate([values[:, : 2 * LANES], last], axis=1))
    for side in range(2):
        parts_out[side, 9 * C :, :] = jnp.zeros((SUM_ROWS - 9 * C, LANES), bf16)


def weights_kernel(
    place, mine, theirs, w_turned, w_conv, win_out, bin_out, wconv_out, bconv_out, wout_out,
    bout_out, taps, sems,
):
    here = place[1]

    def tile(half, n):
        rows = slice(C * n, C * (n + 1))
        return jnp.where(here == half, mine[rows, :], theirs[rows, :]).astype(f32)

    ones = tile(1, 8)
    lane = lane_of((C, LANES))
    low = lane < 64

    def moment_of(n):
        pair = n // 2
        first, middle, last = [tile(pair // 3, 3 * (pair % 3) + t) for t in range(3)]
        if n % 2:
            middle, last = pltpu.roll(middle, 64, 1), pltpu.roll(last, 64, 1)
            first, middle = jnp.where(low, middle, last), last
        one = jnp.where(lane < 67, pltpu.roll(ones, LANES - 3 * n, 1) if n else ones, 0.0)
        return jnp.concatenate([first, jnp.where(low, middle, one)], axis=1).astype(bf16)

    grad_in = jnp.zeros((C, WIDE), f32)
    copies = []
    for n in range(9):
        moment = moment_of(n)
        taps[n] = dot_nt(w_turned[...], moment)
        copy = pltpu.make_async_copy(taps.at[n], wconv_out.at[n], sems.at[n])
        copy.start()
        copies.append(copy)
        grad_in += dot(w_conv[n], moment)
    last = jnp.concatenate([tile(1, 6), tile(1, 7), ones], axis=1)
    last = jnp.transpose(last)
    wout_out[...] = last[:C]
    bconv_out[...] = last[C + 12]
    bout_out[...] = last[C + 27]
    grad_in = jnp.transpose(grad_in + moment_of(9).astype(f32))
    win_out[...] = grad_in[:CIN]
    bin_out[...] = grad_in[CIN]
    for copy in copies:
        copy.wait()


def swap(array):
    return lax.ppermute(array, "c", [(0, 1), (1, 0)])


def across(blocks, axes):
    return lax.all_to_all(blocks, axes, 0, 0, tiled=True)


def per_device(
    latent, condition, text_states, valid_rows, text_lengths, w_in, b_in, w_conv, b_conv, w_out,
    b_out, w_query, w_key, w_value, w_attn_out, b_attn_out, w_cross_query, w_cross_key,
    w_cross_value, w_cross_out, b_cross_out, w_ff_in, b_ff_in, w_ff_out, b_ff_out, cotangent,
):
    core, column = lax.axis_index("c"), 2 * lax.axis_index("x") + lax.axis_index("c")
    item, lower = lax.axis_index("a"), lax.axis_index("b")
    place = jnp.stack([item, core, column, lower]).astype(jnp.int32)

    wide = [
        jnp.pad(x.reshape(STRIPS, PART, -1), ((0, 0), (0, 0), (0, lanes - x.shape[-1])))
        for x, lanes in ((condition, 256), (latent, 384), (cotangent, 384))
    ]
    cells = across(jnp.concatenate(wide, axis=-1), "a")

    text = lax.dynamic_index_in_dim(text_states, item, 0, keepdims=False)
    text = jnp.pad(text, ((0, TEXT - text.shape[0]), (0, 0)))
    text_keys, text_values = call(
        text_kernel,
        (out(TEXT, 2 * WIDE), out(TEXT, 2 * WIDE)),
        (text, w_cross_key.T, w_cross_value.T),
        "text",
        scratch=[pltpu.VMEM((2 * WIDE, text.shape[1]), bf16)] * 2,
        fetch=(0, 1, 2),
        store=(0, 1),
        cost=pl.CostEstimate(flops=4 * 10**9, bytes_accessed=2 * 10**6, transcendentals=0),
    )
    (w_turned,) = call(
        widen_kernel, (out(C, WIDE),), (w_in, b_in), "widen", fetch=(0, 1), store=(0,)
    )
    cells, text_keys, w_turned = after(cells, text_keys, w_turned)

    here = cells[:, :, :WIDE].reshape(STRIPS, ROWS, COLS, WIDE)
    ends = jnp.concatenate([here[:, :1], here[:, ROWS - 1 :]], axis=1)
    beside = lax.ppermute(ends, "b", [(0, 1), (1, 0)])
    right_way = [(i, i + 1) for i in range(7)]

    def edge(col):
        rows = jnp.concatenate([here[:, :, col], beside[:, :, col]], axis=1)
        return rows.reshape(STRIPS * (ROWS + 2), WIDE)

    left = lax.ppermute(edge(COLS - 1), ("x", "c"), right_way)
    right = lax.ppermute(edge(0), ("x", "c"), [(b, a) for a, b in right_way])
    beside, first_bias = after(beside, b_in)
    (
        w_in_here, b_in_here, taps_here, b_conv_here, w_out_here, b_out_here, w_query_here,
        w_key_here, w_value_here,
    ) = bring(
        [
            w_in, first_bias, w_conv.reshape(9, C, C), b_conv, w_out, b_out, w_query, w_key,
            w_value,
        ],
        "load_adapter",
    )
    rows, mixed, smooth, slope, cond = call(
        adapter_kernel,
        (
            out(HEADS, CELLS, LANES),
            out(CELLS, C, dtype=f32),
            out(CELLS, C),
            out(CELLS, C, dtype=f32),
            out(9, CELLS, WIDE),
        ),
        (
            place, valid_rows, cells, beside, left, right, w_in_here, b_in_here, taps_here,
            b_conv_here, w_out_here, b_out_here, w_query_here, w_key_here, w_value_here,
        ),
        "adapter",
        scalars=2,
        scratch=[pltpu.VMEM((WIDE, C), bf16)],
        vmem=24,
        store=(1, 2, 3, 4),
        near=(0,),
        held=tuple(range(6, 15)),
    )

    own = across(rows, GROUP_OF_ITEM).reshape(HALF, LANES)

    other = swap(own)
    _, attn_weight = after(own, w_attn_out)
    w_cross_query_wide, w_cross_out_wide, w_attn_spread = call(
        form_kernel,
        (out(C, 2 * WIDE), out(2 * WIDE, C), out(HEADS * LANES, 768)),
        (w_cross_query, w_cross_out, attn_weight),
        "form",
        fetch=(2, 0, 1),
        store=(0, 1),
        near=(2,),
    )
    own, w_attn_spread = after(own, w_attn_spread)
    packed, full, probs, keys_turned, query_turned = call(
        attend_kernel,
        (
            out(CHIPS, PART // 2, LANES),
            out(HALF, LANES, dtype=f32),
            out(HALF, 2 * HALF),
            out(LANES, 2 * HALF),
            out(LANES, HALF),
        ),
        (own, other),
        "attend",
        scratch=[
            pltpu.VMEM((2 * HALF, BLOCK), f32),
            pltpu.VMEM((2 * HALF, BLOCK), f32),
            pltpu.VMEM((2 * HALF, BLOCK), bf16),
            pltpu.VMEM((2 * HALF, BLOCK), bf16),
            pltpu.VMEM((BLOCK, 2 * HALF), bf16),
            pltpu.VMEM((BLOCK, 2 * HALF), bf16),
            pltpu.VMEM((LANES, HALF), f32),
            pltpu.SemaphoreType.DMA((2,)),
        ],
        vmem=32,
        store=(1, 3, 4),
        near=(0,),
        far=(4,),
    )

    heads_in = across(packed.reshape(HEADS, CELLS // 2, LANES), GROUP_OF_ITEM)
    result, grad_first, heads_out = call(
        middle_kernel,
        (out(CELLS, C), out(CELLS, C, dtype=f32), out(HEADS, CELLS // 2, LANES)),
        (
            place, text_lengths, heads_in, mixed, cells, text_keys, text_values,
            w_attn_spread, b_attn_out, w_cross_query_wide, w_cross_out_wide, b_cross_out,
            w_ff_in, b_ff_in, w_ff_out.T, b_ff_out,
        ),
        "middle",
        scalars=2,
        scratch=[pltpu.VMEM((CELLS, HEADS * TEXT), f32)],
        vmem=32,
        fetch=(3, 8, 9, 5, 6, 10, 11, 12, 13, 14, 15),
        store=(0, 1),
        near=(2,),
        held=(7,),
    )

    grads_in = across(heads_out, GROUP_OF_ITEM).reshape(CHIPS, PART // 2, LANES)
    own_grads, other_grads = call(
        attend_back_kernel,
        (out(HALF, LANES, dtype=f32), out(HALF, LANES)),
        (keys_turned, query_turned, full, grads_in, probs),
        "attend_back",
        scratch=[
            pltpu.VMEM((HALF, LANES), bf16),
            pltpu.VMEM((LANES, 2 * HALF), bf16),
            pltpu.VMEM((LANES, 2 * HALF), f32),
            pltpu.VMEM((2 * HALF, WIDE_BLOCK), bf16),
            pltpu.VMEM((WIDE_BLOCK, 2 * HALF), bf16),
            pltpu.VMEM((WIDE_BLOCK, 2 * HALF), bf16),
            pltpu.SemaphoreType.DMA((2,)),
        ],
        vmem=36,
        near=(0, 1),
        far=(4,),
    )

    _, query_weight = after(other_grads, w_query)
    (w_joined,) = call(
        join_kernel,
        (out(C, HEADS * LANES),),
        (query_weight, w_key, w_value),
        "join",
        fetch=(0, 1, 2),
        near=(0,),
    )
    own_grads, w_joined = after(own_grads, w_joined)
    row_grads = (own_grads + swap(other_grads).astype(f32)).astype(bf16)
    row_grads = across(row_grads.reshape(HEADS, CELLS, LANES), GROUP_OF_ITEM)
    back, parts = call(
        finish_kernel,
        (out(STRIPS, 6, PART, LANES), out(2, SUM_ROWS, LANES)),
        (
            place, row_grads, w_joined, mixed, grad_first, slope, smooth, cond, w_out, result,
        ),
        "finish",
        scalars=1,
        store=(0,),
    )

    shares = (parts[0].astype(f32) + swap(parts[1]).astype(f32)).astype(bf16)
    shares = shares.reshape(8, 8, SHARE, LANES).transpose(1, 0, 2, 3)
    shares = across(shares.reshape(CHIPS, SHARE, LANES), CHIPS_ALL)
    share = jnp.sum(shares.astype(f32), axis=0).astype(bf16)

    sums = jnp.broadcast_to(share[None], (STRIPS, SHARE, LANES))
    parcel = jnp.concatenate([sums, back.reshape(STRIPS, 6 * PART, LANES)], axis=1)
    parcel = across(parcel, "a")
    sums = parcel[:, :SHARE].reshape(1, STRIPS * SHARE, LANES)
    sums = jnp.broadcast_to(sums, (HEADS,) + sums.shape[1:])
    mine = across(sums, GROUP_OF_ITEM).reshape(SUM_ROWS, LANES)
    mine, parcel = after(mine, parcel)
    theirs = swap(mine)
    result, latent_grad = call(
        unpack_kernel,
        (out(STRIPS, PART, C), out(STRIPS, PART, C, dtype=f32)),
        (parcel,),
        "unpack",
        store=(0, 1),
    )
    grad_w_in, grad_b_in, grad_w_conv, grad_b_conv, grad_w_out, grad_b_out = call(
        weights_kernel,
        (
            out(CIN, C, dtype=f32),
            out(C, dtype=f32),
            out(9, C, C, dtype=f32),
            out(C, dtype=f32),
            out(C, C, dtype=f32),
            out(C, dtype=f32),
        ),
        (place, mine, theirs, w_turned, w_conv.reshape(9, C, C)),
        "weights",
        scalars=1,
        scratch=[
            pltpu.VMEM((9, C, C), f32),
            pltpu.SemaphoreType.DMA((9,)),
        ],
        vmem=24,
        fetch=(3, 4),
        store=(0, 4),
        far=(7,),
        cost=pl.CostEstimate(flops=6 * 10**9, bytes_accessed=2 * 10**7, transcendentals=0),
    )
    grid = (STRIPS, ROWS, COLS, C)
    return (
        result.reshape(grid),
        latent_grad.reshape(grid),
        grad_w_in,
        grad_b_in,
        grad_w_conv.reshape(3, 3, C, C),
        grad_b_conv,
        grad_w_out,
        grad_b_out,
    )


def solution(mesh):
    split = Mesh(mesh.devices.reshape(8, 2, 4, 2), ("a", "b", "x", "c"))
    cells = P(None, ("a", "b"), ("x", "c"), None)
    in_specs = (cells, cells) + (P(),) * 23 + (cells,)
    out_specs = (cells, cells) + (P(),) * 6
    return jax.shard_map(
        per_device, mesh=split, in_specs=in_specs, out_specs=out_specs, check_vma=False
    )
```

```python
import jax
import jax.numpy as jnp
from jax import lax
from jax.experimental import pallas as pl
from jax.experimental.pallas import tpu as pltpu
from jax.sharding import Mesh
from jax.sharding import PartitionSpec as P

STRIPS, ROWS, COLS, C, CIN, HEADS, HEAD, FF = 8, 4, 8, 320, 192, 8, 40, 1280
CELLS = STRIPS * ROWS * COLS
PART = ROWS * COLS
CHIPS = 64
HALF = CHIPS * PART
TEXT = 128
LANES = 128
WIDE = 256
GROUP = 160
SCALE = HEAD**-0.5
LOG2E = 1.4426950408889634
EPS = 1e-5
MASKED = -1e30
KEY, VALUE, MASK = HEAD, 2 * HEAD, 3 * HEAD
GROUP_OF_ITEM, CHIPS_ALL = ("b", "x"), ("a", "b", "x")
LATENT, COTANGENT = 256, 640
SUM_ROWS = 3072
SHARE = SUM_ROWS // CHIPS

bf16, f32 = jnp.bfloat16, jnp.float32
NT = (((1,), (1,)), ((), ()))


def dot(left, right):
    return jnp.dot(left, right, preferred_element_type=f32)


def dot_nt(left, right):
    return lax.dot_general(left, right, NT, preferred_element_type=f32)


def lane_of(shape):
    return lax.broadcasted_iota(jnp.int32, shape, len(shape) - 1)


def moments(values):
    center = values - jnp.mean(values, -1, keepdims=True)
    rate = lax.rsqrt(jnp.mean(center * center, -1, keepdims=True) + EPS)
    return center * rate, rate


def norm_back(unit, rate, grads):
    return rate * (
        grads
        - jnp.mean(grads, -1, keepdims=True)
        - unit * jnp.mean(grads * unit, -1, keepdims=True)
    )


class Fetched:
    def __init__(self, source, buffer, semaphore):
        self.copy = pltpu.make_async_copy(source, buffer, semaphore)
        self.buffer, self.shape, self.here = buffer, buffer.shape, False
        self.copy.start()

    def __getitem__(self, index):
        if not self.here:
            self.copy.wait()
            self.here = True
        return self.buffer[index]


class Stored:
    def __init__(self, target, buffer, semaphore):
        self.copy = pltpu.make_async_copy(buffer, target, semaphore)
        self.buffer, self.started = buffer, False

    def __setitem__(self, index, values):
        self.buffer[index] = values
        if index is Ellipsis:
            self.start()

    def start(self):
        if not self.started:
            self.copy.start()
            self.started = True


def call(kernel, outs, ins, name, scalars=0, scratch=(), vmem=16, fetch=(), store=(), far=(),
    near=(), held=(), cost=None,
):
    fetch, store = list(fetch), list(store)
    far_in = [i for i in far if i < len(ins)]
    far_out = [i - len(ins) for i in far if i >= len(ins)]

    def body(*refs):
        refs = list(refs)
        given, refs = refs[: len(ins)], refs[len(ins) :]
        made, refs = refs[: len(outs)], refs[len(outs) :]
        own, refs = refs[: len(scratch)], refs[len(scratch) :]
        buffers, semaphores = refs[:-1], refs[-1] if refs else None
        for n, i in enumerate(fetch):
            given[i] = Fetched(given[i], buffers[n], semaphores.at[n])
        kept = []
        for n, i in enumerate(store, len(fetch)):
            made[i] = Stored(made[i], buffers[n], semaphores.at[n])
            kept.append(made[i])
        kernel(*given, *made, *own)
        for part in given:
            if isinstance(part, Fetched) and not part.here:
                part.copy.wait()
        for part in kept:
            part.start()
        for part in kept:
            part.copy.wait()

    def made_as(i, made):
        if i in store or i in far_out:
            return pltpu.HBM(made.shape, made.dtype)
        return pltpu.VMEM(made.shape, made.dtype) if i in near else made

    def in_spec(i):
        if i < scalars:
            return pl.BlockSpec(memory_space=pltpu.SMEM)
        space = pltpu.HBM if i in fetch or i in far_in else pltpu.VMEM
        return pl.BlockSpec(memory_space=space)

    def out_spec(i):
        space = pltpu.HBM if i in store or i in far_out else pltpu.VMEM
        return pl.BlockSpec(memory_space=space)

    extra = [pltpu.VMEM(ins[i].shape, ins[i].dtype) for i in fetch]
    extra += [pltpu.VMEM(outs[i].shape, outs[i].dtype) for i in store]
    if extra:
        extra.append(pltpu.SemaphoreType.DMA((len(extra),)))
    return pl.pallas_call(
        body,
        out_shape=tuple(made_as(i, made) for i, made in enumerate(outs)),
        in_specs=[in_spec(i) for i in range(len(ins))],
        out_specs=tuple(out_spec(i) for i in range(len(outs))),
        scratch_shapes=list(scratch) + extra,
        compiler_params=pltpu.CompilerParams(vmem_limit_bytes=vmem << 20),
        cost_estimate=cost,
        name=name,
    )(
        *(
            pltpu.with_memory_space_constraint(x, pltpu.HBM)
            if i in fetch or i in far_in
            else (pltpu.with_memory_space_constraint(x, pltpu.VMEM) if i in held else x)
            for i, x in enumerate(ins)
        )
    )


def bring(arrays, name, kernel=None, made=(), near=()):
    count, given = len(arrays), len(near)

    def body(*refs):
        sources, inputs = refs[:count], refs[count : count + given]
        targets = refs[count + given : -1]
        copies = [
            pltpu.make_async_copy(sources[n], targets[n], refs[-1].at[n]) for n in range(count)
        ]
        for copy in copies:
            copy.start()
        if kernel is not None:
            kernel(*inputs, *targets[count:])
        for copy in copies:
            copy.wait()

    shapes = [jax.ShapeDtypeStruct(x.shape, x.dtype) for x in arrays] + list(made)
    return pl.pallas_call(
        body,
        out_shape=tuple(pltpu.VMEM(x.shape, x.dtype) for x in shapes),
        in_specs=[pl.BlockSpec(memory_space=pltpu.HBM)] * count
        + [pl.BlockSpec(memory_space=pltpu.VMEM)] * given,
        out_specs=(pl.BlockSpec(memory_space=pltpu.VMEM),) * len(shapes),
        scratch_shapes=[pltpu.SemaphoreType.DMA((max(count, 1),))],
        compiler_params=pltpu.CompilerParams(vmem_limit_bytes=8 << 20),
        name=name,
    )(*(pltpu.with_memory_space_constraint(x, pltpu.HBM) for x in arrays), *near)


def after(value, *arrays):
    return lax.optimization_barrier((value,) + arrays)


def out(*shape, dtype=bf16):
    return jax.ShapeDtypeStruct(shape, dtype)


def bias_rows(bias):
    row = lax.broadcasted_iota(jnp.int32, (WIDE - CIN, C), 0)
    rest = jnp.broadcast_to(bias, (WIDE - CIN, C))
    rows = jnp.zeros((WIDE - CIN, C), f32)
    for n in range(3):
        piece = rest.astype(bf16).astype(f32)
        rows = jnp.where(row == n, piece, rows)
        rest = rest - piece
    return rows.astype(bf16)


def adapter_kernel(
    place, valid, cells, beside, left, right, w_in, b_in, w_conv, b_conv, w_out,
    b_out, w_query, w_key, w_value, rows_out, mixed_out, smooth_out, slope_out, cond_out,
    w_wide,
):
    span = STRIPS * (ROWS + 2)
    w_wide[:CIN, :] = w_in[...]
    w_wide[CIN:, :] = bias_rows(b_in[...])
    upper = place[3] == 0

    def tall(own, first, last):
        blank = jnp.zeros_like(first[:1])
        above = jnp.where(upper, jnp.concatenate([blank, last[:-1]], axis=0), last)
        below = jnp.where(upper, first, jnp.concatenate([first[1:], blank], axis=0))
        return jnp.concatenate([above, own, below], axis=1)

    own = cells[:, :, :WIDE].astype(f32).reshape(STRIPS, ROWS, COLS, WIDE)
    other = beside[...].astype(f32)
    block = tall(own, other[:, :1], other[:, 1:]).reshape(span, COLS, WIDE)
    shape = (STRIPS, ROWS + 2, COLS, WIDE)
    row = 2 * ROWS * lax.broadcasted_iota(jnp.int32, shape, 0) + ROWS * place[3] - 1
    row += lax.broadcasted_iota(jnp.int32, shape, 1)
    inside = (row >= 0) & (row < ROWS * 16)
    inside = jnp.where(inside, 1.0, 0.0).reshape(span, COLS, WIDE)
    lane = lane_of((span, COLS, WIDE))
    col = lax.broadcasted_iota(jnp.int32, (span, COLS, WIDE), 1)
    at = COLS * place[2]
    edges = []
    for n, side in enumerate((left, right)):
        there = (at > 0) if n == 0 else (at < COLS * 7)
        side = side[...].astype(f32).reshape(span, 1, WIDE)
        side = side.reshape(STRIPS, ROWS + 2, 1, WIDE)
        side = tall(side[:, :ROWS], side[:, ROWS : ROWS + 1], side[:, ROWS + 1 :])
        edges.append((side.reshape(span, 1, WIDE), jnp.where(there, inside, 0.0)))
    near = jnp.where(col == 0, edges[0][0], pltpu.roll(block, 1, 1))
    near_inside = jnp.where(col == 0, edges[0][1], inside)
    far = jnp.where(col == COLS - 1, edges[1][0], pltpu.roll(block, COLS - 1, 1))
    far_inside = jnp.where(col == COLS - 1, edges[1][1], inside)
    inner = jnp.zeros((CELLS, C), f32)
    start_here = None
    one = (lane >= CIN) & (lane < CIN + 3)
    moves = ((near, near_inside), (block, inside), (far, far_inside))
    for j, (moved, present) in enumerate(moves):
        moved = jnp.where(one, present, moved)
        start = dot(moved.reshape(span * COLS, WIDE).astype(bf16), w_wide[...])
        start = start.reshape(STRIPS, ROWS + 2, COLS, C)
        moved = moved.reshape(STRIPS, ROWS + 2, COLS, WIDE)
        for i in range(3):
            patch = start[:, i : i + ROWS].reshape(CELLS, C).astype(bf16)
            if i == 1 and j == 1:
                start_here = patch.astype(f32)
            inner += dot(patch, w_conv[3 * i + j])
            cond_out[3 * i + j] = moved[:, i : i + ROWS].reshape(CELLS, WIDE).astype(bf16)
    inner += b_conv[...]
    gate = jax.nn.sigmoid(inner)
    smooth = (inner * gate).astype(bf16)
    smooth_out[...] = smooth
    slope_out[...] = gate * (1.0 + inner * (1.0 - gate))
    latent = cells[:, :, LATENT : LATENT + C].astype(f32).reshape(CELLS, C)
    mixed = latent + (start_here + dot(smooth, w_out[...]) + b_out[...])
    mixed_out[...] = mixed
    normed = moments(mixed)[0].astype(bf16)
    projected = [dot(normed, w[...]) for w in (w_query, w_key, w_value)]
    projected[0] *= SCALE * LOG2E
    shape = (STRIPS, ROWS, COLS, LANES - MASK)
    row = 2 * ROWS * lax.broadcasted_iota(jnp.int32, shape, 0) + ROWS * place[3]
    row += lax.broadcasted_iota(jnp.int32, shape, 1)
    hidden = jnp.where(row >= valid[place[0]], MASKED, 0.0)
    extras = jnp.where(lane_of(shape) == 0, hidden, 1.0).reshape(CELLS, LANES - MASK)
    for head in range(HEADS):
        at = slice(head * HEAD, (head + 1) * HEAD)
        joined = jnp.concatenate([part[:, at] for part in projected] + [extras], axis=1)
        rows_out[head] = joined.astype(bf16)


def text_kernel(
    text, w_key_turned, w_value_turned, keys_out, values_out, wide_key, wide_value
):
    blank = jnp.zeros((WIDE - GROUP, text.shape[1]), bf16)
    states = text[...]
    both = ((w_key_turned, wide_key, keys_out), (w_value_turned, wide_value, values_out))
    for source, wide, target in both:
        for g in range(2):
            wide[g * WIDE : g * WIDE + GROUP, :] = source[g * GROUP : (g + 1) * GROUP, :]
            wide[g * WIDE + GROUP : (g + 1) * WIDE, :] = blank
        target[...] = dot_nt(states, wide[...]).astype(bf16)


def form_kernel(w_query, w_cross_out, w_attn, query_out, cross_out, spread_out):
    rows = w_query[...].astype(f32)
    blank = jnp.zeros((C, WIDE - GROUP), f32)
    rows = [rows[:, :GROUP], blank, rows[:, GROUP:], blank]
    query_out[...] = jnp.concatenate(rows, axis=1).astype(bf16)
    rows = w_cross_out[...]
    blank = jnp.zeros((WIDE - GROUP, C), bf16)
    cross_out[...] = jnp.concatenate([rows[:GROUP], blank, rows[GROUP:], blank], axis=0)
    rows = w_attn[...].astype(f32)
    gap = jnp.zeros((HEAD, 384 - C), f32)
    for head in range(HEADS):
        part = jnp.concatenate([rows[head * HEAD : (head + 1) * HEAD], gap], axis=1)
        blank = jnp.zeros_like(part)
        block = jnp.concatenate(
            [
                jnp.concatenate([part, blank], axis=1),
                jnp.concatenate([blank, part], axis=1),
                jnp.zeros((LANES - 2 * HEAD, 768), f32),
            ],
            axis=0,
        )
        spread_out[head * LANES : (head + 1) * LANES, :] = block.astype(bf16)


BLOCK = 256
STEP = 512


def attend_kernel(
    own, other, packed_out, full_out, probs_out, keys_out, query_out,
    scores_a, scores_b, probs_a, probs_b, turned_a, turned_b, output, sems,
):
    count = HALF // BLOCK
    keys_turned, query = keys_out.buffer, query_out.buffer
    keys_turned[:, :HALF] = jnp.transpose(own[...])
    keys_turned[:, HALF:] = jnp.transpose(other[...])
    keys_out.start()
    lane = lane_of((HALF, LANES))
    rows = pltpu.roll(own[...].astype(f32), KEY, 1)
    rows = jnp.where((lane >= KEY) & (lane < VALUE), rows, jnp.where(lane == MASK, 1.0, 0.0))
    query_out[...] = jnp.transpose(rows.astype(bf16))
    chunks = [(ref, at) for ref in (own, other) for at in range(0, HALF, STEP)]

    def columns(b):
        return pl.ds(pl.multiple_of(b * BLOCK, BLOCK), BLOCK)

    def score(queries, n, scores, peak):
        ref, at = chunks[n]
        part = dot(ref[at : at + STEP, :], queries)
        scores[n * STEP : (n + 1) * STEP, :] = part
        part = jnp.max(part.reshape(STEP // 8, 8, BLOCK), axis=0)
        return part if peak is None else jnp.maximum(peak, part)

    def sent(b, turned, n):
        return pltpu.make_async_copy(turned, probs_out.at[columns(b)], sems.at[n])

    def half(b, peak, following, scores, probs, turned):
        shift = jnp.max(peak, axis=0, keepdims=True)
        queries = query[:, columns(jnp.minimum(b + 1, count - 1))]
        ahead = None
        for n in range(len(chunks)):
            ahead = score(queries, n, following, ahead)
            keys = slice(n * STEP, (n + 1) * STEP)
            part = jnp.exp2(scores[keys, :] - shift).astype(bf16)
            probs[keys, :] = part
            turned[:, keys] = jnp.transpose(part)
        output[:, columns(b)] = dot(keys_turned[...], probs[...])
        return ahead

    peak = None
    for n in range(len(chunks)):
        peak = score(query[:, :BLOCK], n, scores_a, peak)

    def body(i, peak):
        @pl.when(i > 0)
        def _():
            sent(2 * i - 2, turned_a, 0).wait()

        peak = half(2 * i, peak, scores_b, scores_a, probs_a, turned_a)
        sent(2 * i, turned_a, 0).start()

        @pl.when(i > 0)
        def _():
            sent(2 * i - 1, turned_b, 1).wait()

        peak = half(2 * i + 1, peak, scores_a, scores_b, probs_b, turned_b)
        sent(2 * i + 1, turned_b, 1).start()
        return peak

    lax.fori_loop(0, count // 2, body, peak)
    total = output[...]
    inverse = 1.0 / total[MASK + 1 : MASK + 2, :]
    row = lax.broadcasted_iota(jnp.int32, (LANES, HALF), 0)
    total = jnp.transpose(jnp.where(row == 0, inverse, total * inverse))
    full_out[...] = total
    pairs = total.reshape(CHIPS, 2, PART // 2, LANES)
    lane = lane_of((HALF // 2, LANES))
    low = pltpu.roll(pairs[:, 0].reshape(HALF // 2, LANES), LANES - VALUE, 1)
    high = pltpu.roll(pairs[:, 1].reshape(HALF // 2, LANES), LANES - VALUE + HEAD, 1)
    packed = jnp.where(lane < HEAD, low, jnp.where(lane < 2 * HEAD, high, 0.0))
    packed_out[...] = packed.astype(bf16).reshape(CHIPS, PART // 2, LANES)
    sent(count - 2, turned_a, 0).wait()
    sent(count - 1, turned_b, 1).wait()


def middle_kernel(
    place, lengths, heads_in, mixed, cells, text_keys, text_values, w_attn, b_attn,
    w_cross_query, w_cross_out, b_cross, w_ff_in, b_ff_in, w_ff_turned, b_ff_out, result_out,
    grad_out, heads_out, probs_keep,
):
    half = CELLS // 2
    split = w_attn.shape[1] // 2
    packed = jnp.concatenate([heads_in[head] for head in range(HEADS)], axis=1)
    both = dot(packed, w_attn[...])
    shape = (STRIPS, 1, PART // 2, C)
    attended = jnp.concatenate(
        [both[:, :C].reshape(shape), both[:, split : split + C].reshape(shape)], axis=1
    ).reshape(CELLS, C)
    first = mixed[...] + attended + b_attn[...]
    unit_two, rate_two = moments(first)
    cross_query = dot(unit_two.astype(bf16), w_cross_query[...]).astype(bf16)
    lane = lane_of((TEXT, WIDE))
    in_head = [(lane >= HEAD * h) & (lane < HEAD * (h + 1)) for h in range(HEADS // 2)]
    groups = [slice(0, WIDE), slice(WIDE, 2 * WIDE)]

    def by_head(text):
        kept = []
        for lanes in groups:
            here = text[:, lanes]
            kept.append(
                jnp.concatenate([jnp.where(m, here, jnp.zeros_like(here)) for m in in_head], 0)
            )
        return kept

    keys, values = by_head(text_keys), by_head(text_values)
    spans = [slice(g * HEADS // 2 * TEXT, (g + 1) * HEADS // 2 * TEXT) for g in range(2)]
    heads = [slice(h * TEXT, (h + 1) * TEXT) for h in range(HEADS)]
    token = lane_of((CELLS, TEXT)) < lengths[place[0]]
    scores = [dot_nt(cross_query[:, groups[g]], keys[g]) * SCALE for g in range(2)]
    scores = jnp.concatenate(scores, axis=1)
    for at in heads:
        part = jnp.where(token, scores[:, at], MASKED)
        weights = jnp.exp(part - jnp.max(part, -1, keepdims=True))
        probs_keep[:, at] = weights / jnp.sum(weights, -1, keepdims=True)
    cross = [dot(probs_keep[:, spans[g]].astype(bf16), values[g]) for g in range(2)]
    cross = jnp.concatenate(cross, axis=1).astype(bf16)
    second = first + dot(cross, w_cross_out[...]) + b_cross[...]
    unit_three, rate_three = moments(second)
    normed_three = unit_three.astype(bf16)
    upstream = cells[:, :, COTANGENT : COTANGENT + C].reshape(CELLS, C)
    result = second + b_ff_out[...]
    grad_normed = jnp.zeros((CELLS, C), f32)
    step = 256
    for at in range(0, FF, step):
        ups, gates = slice(at, at + step), slice(FF + at, FF + at + step)
        value = dot(normed_three, w_ff_in[:, ups]) + b_ff_in[ups]
        gate = dot(normed_three, w_ff_in[:, gates]) + b_ff_in[gates]
        normal = 0.5 + 0.5 * lax.erf(gate * (0.5**0.5))
        density = jnp.exp(gate * gate * -0.5) * 0.3989422804014327
        gelu = gate * normal
        result += dot_nt((value * gelu).astype(bf16), w_ff_turned[:, ups])
        grad_act = dot(upstream, w_ff_turned[:, ups])
        grad_value = (grad_act * gelu).astype(bf16)
        grad_gate = (grad_act * value * (normal + gate * density)).astype(bf16)
        grad_normed += dot_nt(grad_value, w_ff_in[:, ups])
        grad_normed += dot_nt(grad_gate, w_ff_in[:, gates])
    result_out[...] = result.astype(bf16)
    grad_second = upstream.astype(f32) + norm_back(unit_three, rate_three, grad_normed)
    grad_cross = dot_nt(grad_second.astype(bf16), w_cross_out[...]).astype(bf16)
    grad_probs = [dot_nt(grad_cross[:, groups[g]], values[g]) for g in range(2)]
    grad_probs = jnp.concatenate(grad_probs, axis=1)
    grad_scores = []
    for at in heads:
        probs, grads = probs_keep[:, at], grad_probs[:, at]
        weighted = jnp.sum(probs * grads, -1, keepdims=True)
        grad_scores.append((probs * (grads - weighted)).astype(bf16))
    grad_scores = jnp.concatenate(grad_scores, axis=1)
    grad_query = [dot(grad_scores[:, spans[g]], keys[g]) for g in range(2)]
    grad_query = (jnp.concatenate(grad_query, axis=1) * SCALE).astype(bf16)
    grad_first = grad_second + norm_back(
        unit_two, rate_two, dot_nt(grad_query, w_cross_query[...])
    )
    grad_out[...] = grad_first
    pairs = grad_first.reshape(STRIPS, 2, PART // 2, C)
    gap = jnp.zeros((half, split - C), f32)
    both = jnp.concatenate(
        [pairs[:, 0].reshape(half, C), gap, pairs[:, 1].reshape(half, C), gap], axis=1
    ).astype(bf16)
    packed = dot_nt(both, w_attn[...]).astype(bf16)
    for head in range(HEADS):
        heads_out[head] = packed[:, head * LANES : (head + 1) * LANES]


WIDE_BLOCK = 512
WIDE_STEP = 1024


def attend_back_kernel(
    keys_turned, query_turned, full, packed, probs_in, own_out, other_out,
    grads, left, sums, scores, probs_a, probs_b, sems,
):
    half, count = HALF // 2, HALF // WIDE_BLOCK

    def block(b):
        return pl.ds(pl.multiple_of(b * WIDE_BLOCK, WIDE_BLOCK), WIDE_BLOCK)

    def fetched(b, probs, n):
        return pltpu.make_async_copy(probs_in.at[block(b)], probs, sems.at[n])

    fetched(0, probs_a, 0).start()
    fetched(1, probs_b, 1).start()
    lane = lane_of((half, LANES))
    value_lane = (lane >= VALUE) & (lane < MASK)
    pairs = packed[...].reshape(half, LANES).astype(f32)
    low = jnp.where(value_lane, pltpu.roll(pairs, VALUE, 1), 0.0)
    high = jnp.where(value_lane, pltpu.roll(pairs, VALUE - HEAD, 1), 0.0)
    shape = (CHIPS, 1, PART // 2, LANES)
    upstream = jnp.concatenate([low.reshape(shape), high.reshape(shape)], axis=1)
    upstream = upstream.reshape(HALF, LANES)
    lane = lane_of((HALF, LANES))
    outputs = full[...]
    upstream *= jnp.sum(jnp.where(lane == 0, outputs, 0.0), axis=1, keepdims=True)
    weighted = jnp.sum(upstream * outputs, axis=1, keepdims=True)
    first = weighted.astype(bf16).astype(f32)
    upstream = jnp.where(lane == MASK + 4, -first, upstream)
    upstream = jnp.where(lane == MASK + 5, first - weighted, upstream).astype(bf16)
    grads[...] = upstream
    for b in range(count):
        rows, at = slice(b * WIDE_BLOCK, (b + 1) * WIDE_BLOCK), 2 * b * WIDE_BLOCK
        left[:, at : at + WIDE_BLOCK] = query_turned[:, rows]
        left[:, at + WIDE_BLOCK : at + 2 * WIDE_BLOCK] = jnp.transpose(upstream[rows])
    sums[...] = jnp.zeros_like(sums)

    def work(b, probs):
        rows = block(b)
        upstream = grads[rows, :]
        both = left[:, pl.ds(pl.multiple_of(2 * b * WIDE_BLOCK, 2 * WIDE_BLOCK), 2 * WIDE_BLOCK)]
        for at in range(0, 2 * HALF, WIDE_STEP):
            keys = slice(at, at + WIDE_STEP)
            part = probs[:, keys]
            grad = dot(upstream, keys_turned[:, keys])
            grad = (part.astype(f32) * grad).astype(bf16)
            sums[:, keys] += dot(both, jnp.concatenate([grad, part], axis=0))
            scores[keys, :] = jnp.transpose(grad)
        grad_query = jnp.transpose(dot(keys_turned[...], scores[...])) * SCALE
        own_out[rows, :] = pltpu.roll(grad_query, LANES - KEY, 1)

    def body(i, carry):
        fetched(2 * i, probs_a, 0).wait()
        work(2 * i, probs_a)

        @pl.when(2 * i + 2 < count)
        def _():
            fetched(2 * i + 2, probs_a, 0).start()

        fetched(2 * i + 1, probs_b, 1).wait()
        work(2 * i + 1, probs_b)

        @pl.when(2 * i + 3 < count)
        def _():
            fetched(2 * i + 3, probs_b, 1).start()

        return carry

    lax.fori_loop(0, count // 2, body, 0)
    scale = jnp.where(lane < VALUE, 1.0 / LOG2E, 1.0)
    rest = jnp.where(lane < MASK, jnp.transpose(sums[:, :HALF]) * scale, 0.0)
    own_out[...] = jnp.where(lane < KEY, own_out[...], rest)
    rest = jnp.where(
        (lane >= KEY) & (lane < MASK), jnp.transpose(sums[:, HALF:]) * scale, 0.0
    )
    other_out[...] = rest.astype(bf16)


def join_kernel(w_query, w_key, w_value, joined_out):
    blank = jnp.zeros((C, LANES - MASK), f32)
    parts = [w[...].astype(f32) for w in (w_query, w_key, w_value)]
    for head in range(HEADS):
        at = slice(head * HEAD, (head + 1) * HEAD)
        joined = jnp.concatenate([part[:, at] for part in parts] + [blank], axis=1)
        joined_out[:, head * LANES : (head + 1) * LANES] = joined.astype(bf16)


def unpack_kernel(parcel, result_out, latent_out):
    for item in range(STRIPS):
        tiles = [
            parcel[item, SHARE + PART * t : SHARE + PART * (t + 1), :] for t in range(6)
        ]
        result_out[item] = jnp.concatenate(tiles[:3], axis=1)[:, :C]
        latent_out[item] = jnp.concatenate(tiles[3:], axis=1)[:, :C].astype(f32)


def widen_kernel(w_in, b_in, turned_out):
    wide = jnp.concatenate([w_in[...], bias_rows(b_in[...])], axis=0)
    turned_out[...] = jnp.transpose(wide)


def finish_kernel(
    place, rows, w_qkv, mixed, grad_first, slope, smooth, cond, w_out, result, back_out, parts_out
):
    joined = jnp.concatenate([rows[head] for head in range(HEADS)], axis=1)
    unit, rate = moments(mixed[...])
    latent = grad_first[...] + norm_back(unit, rate, dot_nt(joined, w_qkv[...]))
    branch = latent.astype(bf16)
    blank = jnp.zeros((CELLS, 384 - C), bf16)
    back = jnp.concatenate([result[...], blank, branch, blank], axis=1)
    for t in range(6):
        back_out[:, t] = back[:, t * LANES : (t + 1) * LANES].reshape(STRIPS, PART, LANES)
    inner = (dot_nt(branch, w_out[...]) * slope[...]).astype(bf16)
    inner_turned = jnp.transpose(inner)
    branch_turned = jnp.transpose(branch)
    here, there = place[1], 1 - place[1]

    def put(side, at, values):
        values = values.astype(bf16)
        for t in range(0, 3 * LANES, LANES):
            parts_out[side, at : at + C, :] = values[:, t : t + LANES]
            at += C

    lane = lane_of((C, LANES))
    ones = jnp.zeros((C, LANES), f32)
    kept = None
    for n in range(10):
        moment = dot(inner_turned, cond[n]) if n < 9 else dot(branch_turned, cond[4])
        one = pltpu.roll(moment[:, LANES:], 3 * n, 1)
        ones = jnp.where((lane >= 64 + 3 * n) & (lane < 67 + 3 * n), one, ones)
        if n % 2 == 0:
            kept = moment[:, :CIN]
            continue
        both = jnp.concatenate([kept, moment[:, :CIN]], axis=1)
        pair = n // 2
        put(here if pair < 3 else there, 3 * C * (pair % 3), both)
    values = dot(branch_turned, smooth[...])
    last = jnp.concatenate([values[:, 2 * LANES :], ones[:, 64:]], axis=1)
    put(there, 6 * C, jnp.concatenate([values[:, : 2 * LANES], last], axis=1))
    for side in range(2):
        parts_out[side, 9 * C :, :] = jnp.zeros((SUM_ROWS - 9 * C, LANES), bf16)


def weights_kernel(
    place, mine, theirs, w_turned, w_conv, win_out, bin_out, wconv_out, bconv_out, wout_out,
    bout_out, taps, sems,
):
    here = place[1]

    def tile(half, n):
        rows = slice(C * n, C * (n + 1))
        return jnp.where(here == half, mine[rows, :], theirs[rows, :]).astype(f32)

    ones = tile(1, 8)
    lane = lane_of((C, LANES))
    low = lane < 64

    def moment_of(n):
        pair = n // 2
        first, middle, last = [tile(pair // 3, 3 * (pair % 3) + t) for t in range(3)]
        if n % 2:
            middle, last = pltpu.roll(middle, 64, 1), pltpu.roll(last, 64, 1)
            first, middle = jnp.where(low, middle, last), last
        one = jnp.where(lane < 67, pltpu.roll(ones, LANES - 3 * n, 1) if n else ones, 0.0)
        return jnp.concatenate([first, jnp.where(low, middle, one)], axis=1).astype(bf16)

    grad_in = jnp.zeros((C, WIDE), f32)
    copies = []
    for n in range(9):
        moment = moment_of(n)
        taps[n] = dot_nt(w_turned[...], moment)
        copy = pltpu.make_async_copy(taps.at[n], wconv_out.at[n], sems.at[n])
        copy.start()
        copies.append(copy)
        grad_in += dot(w_conv[n], moment)
    last = jnp.concatenate([tile(1, 6), tile(1, 7), ones], axis=1)
    last = jnp.transpose(last)
    wout_out[...] = last[:C]
    bconv_out[...] = last[C + 12]
    bout_out[...] = last[C + 27]
    grad_in = jnp.transpose(grad_in + moment_of(9).astype(f32))
    win_out[...] = grad_in[:CIN]
    bin_out[...] = grad_in[CIN]
    for copy in copies:
        copy.wait()


def swap(array):
    return lax.ppermute(array, "c", [(0, 1), (1, 0)])


def across(blocks, axes):
    return lax.all_to_all(blocks, axes, 0, 0, tiled=True)


def per_device(
    latent, condition, text_states, valid_rows, text_lengths, w_in, b_in, w_conv, b_conv, w_out,
    b_out, w_query, w_key, w_value, w_attn_out, b_attn_out, w_cross_query, w_cross_key,
    w_cross_value, w_cross_out, b_cross_out, w_ff_in, b_ff_in, w_ff_out, b_ff_out, cotangent,
):
    core, column = lax.axis_index("c"), 2 * lax.axis_index("x") + lax.axis_index("c")
    item, lower = lax.axis_index("a"), lax.axis_index("b")
    place = jnp.stack([item, core, column, lower]).astype(jnp.int32)

    wide = [
        jnp.pad(x.reshape(STRIPS, PART, -1), ((0, 0), (0, 0), (0, lanes - x.shape[-1])))
        for x, lanes in ((condition, 256), (latent, 384), (cotangent, 384))
    ]
    cells = across(jnp.concatenate(wide, axis=-1), "a")

    text = lax.dynamic_index_in_dim(text_states, item, 0, keepdims=False)
    text = jnp.pad(text, ((0, TEXT - text.shape[0]), (0, 0)))
    text_keys, text_values = call(
        text_kernel,
        (out(TEXT, 2 * WIDE), out(TEXT, 2 * WIDE)),
        (text, w_cross_key.T, w_cross_value.T),
        "text",
        scratch=[pltpu.VMEM((2 * WIDE, text.shape[1]), bf16)] * 2,
        fetch=(0, 1, 2),
        store=(0, 1),
        cost=pl.CostEstimate(flops=4 * 10**9, bytes_accessed=2 * 10**6, transcendentals=0),
    )
    (w_turned,) = call(
        widen_kernel, (out(C, WIDE),), (w_in, b_in), "widen", fetch=(0, 1), store=(0,)
    )
    cells, text_keys, w_turned = after(cells, text_keys, w_turned)

    here = cells[:, :, :WIDE].reshape(STRIPS, ROWS, COLS, WIDE)
    ends = jnp.concatenate([here[:, :1], here[:, ROWS - 1 :]], axis=1)
    beside = lax.ppermute(ends, "b", [(0, 1), (1, 0)])
    right_way = [(i, i + 1) for i in range(7)]

    def edge(col):
        rows = jnp.concatenate([here[:, :, col], beside[:, :, col]], axis=1)
        return rows.reshape(STRIPS * (ROWS + 2), WIDE)

    left = lax.ppermute(edge(COLS - 1), ("x", "c"), right_way)
    right = lax.ppermute(edge(0), ("x", "c"), [(b, a) for a, b in right_way])
    beside, first_bias = after(beside, b_in)
    (
        w_in_here, b_in_here, taps_here, b_conv_here, w_out_here, b_out_here, w_query_here,
        w_key_here, w_value_here,
    ) = bring(
        [
            w_in, first_bias, w_conv.reshape(9, C, C), b_conv, w_out, b_out, w_query, w_key,
            w_value,
        ],
        "load_adapter",
    )
    rows, mixed, smooth, slope, cond = call(
        adapter_kernel,
        (
            out(HEADS, CELLS, LANES),
            out(CELLS, C, dtype=f32),
            out(CELLS, C),
            out(CELLS, C, dtype=f32),
            out(9, CELLS, WIDE),
        ),
        (
            place, valid_rows, cells, beside, left, right, w_in_here, b_in_here, taps_here,
            b_conv_here, w_out_here, b_out_here, w_query_here, w_key_here, w_value_here,
        ),
        "adapter",
        scalars=2,
        scratch=[pltpu.VMEM((WIDE, C), bf16)],
        vmem=24,
        store=(1, 2, 3, 4),
        near=(0,),
        held=tuple(range(6, 15)),
    )

    own = across(rows, GROUP_OF_ITEM).reshape(HALF, LANES)

    other = swap(own)
    _, attn_weight = after(own, w_attn_out)
    w_cross_query_wide, w_cross_out_wide, w_attn_spread = call(
        form_kernel,
        (out(C, 2 * WIDE), out(2 * WIDE, C), out(HEADS * LANES, 768)),
        (w_cross_query, w_cross_out, attn_weight),
        "form",
        fetch=(2, 0, 1),
        store=(0, 1),
        near=(2,),
    )
    own, w_attn_spread = after(own, w_attn_spread)
    packed, full, probs, keys_turned, query_turned = call(
        attend_kernel,
        (
            out(CHIPS, PART // 2, LANES),
            out(HALF, LANES, dtype=f32),
            out(HALF, 2 * HALF),
            out(LANES, 2 * HALF),
            out(LANES, HALF),
        ),
        (own, other),
        "attend",
        scratch=[
            pltpu.VMEM((2 * HALF, BLOCK), f32),
            pltpu.VMEM((2 * HALF, BLOCK), f32),
            pltpu.VMEM((2 * HALF, BLOCK), bf16),
            pltpu.VMEM((2 * HALF, BLOCK), bf16),
            pltpu.VMEM((BLOCK, 2 * HALF), bf16),
            pltpu.VMEM((BLOCK, 2 * HALF), bf16),
            pltpu.VMEM((LANES, HALF), f32),
            pltpu.SemaphoreType.DMA((2,)),
        ],
        vmem=32,
        store=(1, 3, 4),
        near=(0,),
        far=(4,),
    )

    heads_in = across(packed.reshape(HEADS, CELLS // 2, LANES), GROUP_OF_ITEM)
    result, grad_first, heads_out = call(
        middle_kernel,
        (out(CELLS, C), out(CELLS, C, dtype=f32), out(HEADS, CELLS // 2, LANES)),
        (
            place, text_lengths, heads_in, mixed, cells, text_keys, text_values,
            w_attn_spread, b_attn_out, w_cross_query_wide, w_cross_out_wide, b_cross_out,
            w_ff_in, b_ff_in, w_ff_out.T, b_ff_out,
        ),
        "middle",
        scalars=2,
        scratch=[pltpu.VMEM((CELLS, HEADS * TEXT), f32)],
        vmem=32,
        fetch=(3, 8, 9, 5, 6, 10, 11, 12, 13, 14, 15),
        store=(0, 1),
        near=(2,),
        held=(7,),
    )

    grads_in = across(heads_out, GROUP_OF_ITEM).reshape(CHIPS, PART // 2, LANES)
    own_grads, other_grads = call(
        attend_back_kernel,
        (out(HALF, LANES, dtype=f32), out(HALF, LANES)),
        (keys_turned, query_turned, full, grads_in, probs),
        "attend_back",
        scratch=[
            pltpu.VMEM((HALF, LANES), bf16),
            pltpu.VMEM((LANES, 2 * HALF), bf16),
            pltpu.VMEM((LANES, 2 * HALF), f32),
            pltpu.VMEM((2 * HALF, WIDE_BLOCK), bf16),
            pltpu.VMEM((WIDE_BLOCK, 2 * HALF), bf16),
            pltpu.VMEM((WIDE_BLOCK, 2 * HALF), bf16),
            pltpu.SemaphoreType.DMA((2,)),
        ],
        vmem=36,
        near=(0, 1),
        far=(4,),
    )

    _, query_weight = after(other_grads, w_query)
    (w_joined,) = call(
        join_kernel,
        (out(C, HEADS * LANES),),
        (query_weight, w_key, w_value),
        "join",
        fetch=(0, 1, 2),
        near=(0,),
    )
    own_grads, w_joined = after(own_grads, w_joined)
    row_grads = (own_grads + swap(other_grads).astype(f32)).astype(bf16)
    row_grads = across(row_grads.reshape(HEADS, CELLS, LANES), GROUP_OF_ITEM)
    back, parts = call(
        finish_kernel,
        (out(STRIPS, 6, PART, LANES), out(2, SUM_ROWS, LANES)),
        (
            place, row_grads, w_joined, mixed, grad_first, slope, smooth, cond, w_out, result,
        ),
        "finish",
        scalars=1,
        store=(0,),
    )

    shares = (parts[0].astype(f32) + swap(parts[1]).astype(f32)).astype(bf16)
    shares = shares.reshape(8, 8, SHARE, LANES).transpose(1, 0, 2, 3)
    shares = across(shares.reshape(CHIPS, SHARE, LANES), CHIPS_ALL)
    share = jnp.sum(shares.astype(f32), axis=0).astype(bf16)

    sums = jnp.broadcast_to(share[None], (STRIPS, SHARE, LANES))
    parcel = jnp.concatenate([sums, back.reshape(STRIPS, 6 * PART, LANES)], axis=1)
    parcel = across(parcel, "a")
    sums = parcel[:, :SHARE].reshape(1, STRIPS * SHARE, LANES)
    sums = jnp.broadcast_to(sums, (HEADS,) + sums.shape[1:])
    mine = across(sums, GROUP_OF_ITEM).reshape(SUM_ROWS, LANES)
    mine, parcel, w_turned = after(mine, parcel, w_turned)
    theirs = swap(mine)
    taps_here, w_turned_here = bring([w_conv.reshape(9, C, C), w_turned], "load_weights")
    result, latent_grad = call(
        unpack_kernel,
        (out(STRIPS, PART, C), out(STRIPS, PART, C, dtype=f32)),
        (parcel,),
        "unpack",
        store=(0, 1),
    )
    grad_w_in, grad_b_in, grad_w_conv, grad_b_conv, grad_w_out, grad_b_out = call(
        weights_kernel,
        (
            out(CIN, C, dtype=f32),
            out(C, dtype=f32),
            out(9, C, C, dtype=f32),
            out(C, dtype=f32),
            out(C, C, dtype=f32),
            out(C, dtype=f32),
        ),
        (place, mine, theirs, w_turned_here, taps_here),
        "weights",
        scalars=1,
        scratch=[
            pltpu.VMEM((9, C, C), f32),
            pltpu.SemaphoreType.DMA((9,)),
        ],
        vmem=24,
        store=(0, 4),
        far=(7,),
        held=(3, 4),
        cost=pl.CostEstimate(flops=6 * 10**9, bytes_accessed=2 * 10**7, transcendentals=0),
    )
    grid = (STRIPS, ROWS, COLS, C)
    return (
        result.reshape(grid),
        latent_grad.reshape(grid),
        grad_w_in,
        grad_b_in,
        grad_w_conv.reshape(3, 3, C, C),
        grad_b_conv,
        grad_w_out,
        grad_b_out,
    )


def solution(mesh):
    split = Mesh(mesh.devices.reshape(8, 2, 4, 2), ("a", "b", "x", "c"))
    cells = P(None, ("a", "b"), ("x", "c"), None)
    in_specs = (cells, cells) + (P(),) * 23 + (cells,)
    out_specs = (cells, cells) + (P(),) * 6
    return jax.shard_map(
        per_device, mesh=split, in_specs=in_specs, out_specs=out_specs, check_vma=False
    )
```

```python
import jax
import jax.numpy as jnp
from jax import lax
from jax.experimental import pallas as pl
from jax.experimental.pallas import tpu as pltpu
from jax.sharding import Mesh
from jax.sharding import PartitionSpec as P

STRIPS, ROWS, COLS, C, CIN, HEADS, HEAD, FF = 8, 4, 8, 320, 192, 8, 40, 1280
CELLS = STRIPS * ROWS * COLS
PART = ROWS * COLS
CHIPS = 64
HALF = CHIPS * PART
TEXT = 128
LANES = 128
WIDE = 256
GROUP = 160
SCALE = HEAD**-0.5
LOG2E = 1.4426950408889634
EPS = 1e-5
MASKED = -1e30
KEY, VALUE, MASK = HEAD, 2 * HEAD, 3 * HEAD
GROUP_OF_ITEM, CHIPS_ALL = ("b", "x"), ("a", "b", "x")
LATENT, COTANGENT = 256, 640
SUM_ROWS = 3072
SHARE = SUM_ROWS // CHIPS

bf16, f32 = jnp.bfloat16, jnp.float32
NT = (((1,), (1,)), ((), ()))


def dot(left, right):
    return jnp.dot(left, right, preferred_element_type=f32)


def dot_nt(left, right):
    return lax.dot_general(left, right, NT, preferred_element_type=f32)


def lane_of(shape):
    return lax.broadcasted_iota(jnp.int32, shape, len(shape) - 1)


def moments(values):
    center = values - jnp.mean(values, -1, keepdims=True)
    rate = lax.rsqrt(jnp.mean(center * center, -1, keepdims=True) + EPS)
    return center * rate, rate


def norm_back(unit, rate, grads):
    return rate * (
        grads
        - jnp.mean(grads, -1, keepdims=True)
        - unit * jnp.mean(grads * unit, -1, keepdims=True)
    )


class Fetched:
    def __init__(self, source, buffer, semaphore):
        self.copy = pltpu.make_async_copy(source, buffer, semaphore)
        self.buffer, self.shape, self.here = buffer, buffer.shape, False
        self.copy.start()

    def __getitem__(self, index):
        if not self.here:
            self.copy.wait()
            self.here = True
        return self.buffer[index]


class Stored:
    def __init__(self, target, buffer, semaphore):
        self.copy = pltpu.make_async_copy(buffer, target, semaphore)
        self.buffer, self.started = buffer, False

    def __setitem__(self, index, values):
        self.buffer[index] = values
        if index is Ellipsis:
            self.start()

    def start(self):
        if not self.started:
            self.copy.start()
            self.started = True


def call(kernel, outs, ins, name, scalars=0, scratch=(), vmem=16, fetch=(), store=(), far=(),
    near=(), held=(), cost=None,
):
    fetch, store = list(fetch), list(store)
    far_in = [i for i in far if i < len(ins)]
    far_out = [i - len(ins) for i in far if i >= len(ins)]

    def body(*refs):
        refs = list(refs)
        given, refs = refs[: len(ins)], refs[len(ins) :]
        made, refs = refs[: len(outs)], refs[len(outs) :]
        own, refs = refs[: len(scratch)], refs[len(scratch) :]
        buffers, semaphores = refs[:-1], refs[-1] if refs else None
        for n, i in enumerate(fetch):
            given[i] = Fetched(given[i], buffers[n], semaphores.at[n])
        kept = []
        for n, i in enumerate(store, len(fetch)):
            made[i] = Stored(made[i], buffers[n], semaphores.at[n])
            kept.append(made[i])
        kernel(*given, *made, *own)
        for part in given:
            if isinstance(part, Fetched) and not part.here:
                part.copy.wait()
        for part in kept:
            part.start()
        for part in kept:
            part.copy.wait()

    def made_as(i, made):
        if i in store or i in far_out:
            return pltpu.HBM(made.shape, made.dtype)
        return pltpu.VMEM(made.shape, made.dtype) if i in near else made

    def in_spec(i):
        if i < scalars:
            return pl.BlockSpec(memory_space=pltpu.SMEM)
        space = pltpu.HBM if i in fetch or i in far_in else pltpu.VMEM
        return pl.BlockSpec(memory_space=space)

    def out_spec(i):
        space = pltpu.HBM if i in store or i in far_out else pltpu.VMEM
        return pl.BlockSpec(memory_space=space)

    extra = [pltpu.VMEM(ins[i].shape, ins[i].dtype) for i in fetch]
    extra += [pltpu.VMEM(outs[i].shape, outs[i].dtype) for i in store]
    if extra:
        extra.append(pltpu.SemaphoreType.DMA((len(extra),)))
    return pl.pallas_call(
        body,
        out_shape=tuple(made_as(i, made) for i, made in enumerate(outs)),
        in_specs=[in_spec(i) for i in range(len(ins))],
        out_specs=tuple(out_spec(i) for i in range(len(outs))),
        scratch_shapes=list(scratch) + extra,
        compiler_params=pltpu.CompilerParams(vmem_limit_bytes=vmem << 20),
        cost_estimate=cost,
        name=name,
    )(
        *(
            pltpu.with_memory_space_constraint(x, pltpu.HBM)
            if i in fetch or i in far_in
            else (pltpu.with_memory_space_constraint(x, pltpu.VMEM) if i in held else x)
            for i, x in enumerate(ins)
        )
    )


def bring(arrays, name, kernel=None, made=(), near=()):
    count, given = len(arrays), len(near)

    def body(*refs):
        sources, inputs = refs[:count], refs[count : count + given]
        targets = refs[count + given : -1]
        copies = [
            pltpu.make_async_copy(sources[n], targets[n], refs[-1].at[n]) for n in range(count)
        ]
        for copy in copies:
            copy.start()
        if kernel is not None:
            kernel(*inputs, *targets[count:])
        for copy in copies:
            copy.wait()

    shapes = [jax.ShapeDtypeStruct(x.shape, x.dtype) for x in arrays] + list(made)
    return pl.pallas_call(
        body,
        out_shape=tuple(pltpu.VMEM(x.shape, x.dtype) for x in shapes),
        in_specs=[pl.BlockSpec(memory_space=pltpu.HBM)] * count
        + [pl.BlockSpec(memory_space=pltpu.VMEM)] * given,
        out_specs=(pl.BlockSpec(memory_space=pltpu.VMEM),) * len(shapes),
        scratch_shapes=[pltpu.SemaphoreType.DMA((max(count, 1),))],
        compiler_params=pltpu.CompilerParams(vmem_limit_bytes=8 << 20),
        name=name,
    )(*(pltpu.with_memory_space_constraint(x, pltpu.HBM) for x in arrays), *near)


def after(value, *arrays):
    return lax.optimization_barrier((value,) + arrays)


def out(*shape, dtype=bf16):
    return jax.ShapeDtypeStruct(shape, dtype)


def bias_rows(bias):
    row = lax.broadcasted_iota(jnp.int32, (WIDE - CIN, C), 0)
    rest = jnp.broadcast_to(bias, (WIDE - CIN, C))
    rows = jnp.zeros((WIDE - CIN, C), f32)
    for n in range(3):
        piece = rest.astype(bf16).astype(f32)
        rows = jnp.where(row == n, piece, rows)
        rest = rest - piece
    return rows.astype(bf16)


def adapter_kernel(
    place, valid, cells, beside, left, right, w_in, b_in, w_conv, b_conv, w_out,
    b_out, w_query, w_key, w_value, rows_out, mixed_out, smooth_out, slope_out, cond_out,
    w_wide,
):
    span = STRIPS * (ROWS + 2)
    w_wide[:CIN, :] = w_in[...]
    w_wide[CIN:, :] = bias_rows(b_in[...])
    upper = place[3] == 0

    def tall(own, first, last):
        blank = jnp.zeros_like(first[:1])
        above = jnp.where(upper, jnp.concatenate([blank, last[:-1]], axis=0), last)
        below = jnp.where(upper, first, jnp.concatenate([first[1:], blank], axis=0))
        return jnp.concatenate([above, own, below], axis=1)

    own = cells[:, :, :WIDE].astype(f32).reshape(STRIPS, ROWS, COLS, WIDE)
    other = beside[...].astype(f32)
    block = tall(own, other[:, :1], other[:, 1:]).reshape(span, COLS, WIDE)
    shape = (STRIPS, ROWS + 2, COLS, WIDE)
    row = 2 * ROWS * lax.broadcasted_iota(jnp.int32, shape, 0) + ROWS * place[3] - 1
    row += lax.broadcasted_iota(jnp.int32, shape, 1)
    inside = (row >= 0) & (row < ROWS * 16)
    inside = jnp.where(inside, 1.0, 0.0).reshape(span, COLS, WIDE)
    lane = lane_of((span, COLS, WIDE))
    col = lax.broadcasted_iota(jnp.int32, (span, COLS, WIDE), 1)
    at = COLS * place[2]
    edges = []
    for n, side in enumerate((left, right)):
        there = (at > 0) if n == 0 else (at < COLS * 7)
        side = side[...].astype(f32).reshape(span, 1, WIDE)
        side = side.reshape(STRIPS, ROWS + 2, 1, WIDE)
        side = tall(side[:, :ROWS], side[:, ROWS : ROWS + 1], side[:, ROWS + 1 :])
        edges.append((side.reshape(span, 1, WIDE), jnp.where(there, inside, 0.0)))
    near = jnp.where(col == 0, edges[0][0], pltpu.roll(block, 1, 1))
    near_inside = jnp.where(col == 0, edges[0][1], inside)
    far = jnp.where(col == COLS - 1, edges[1][0], pltpu.roll(block, COLS - 1, 1))
    far_inside = jnp.where(col == COLS - 1, edges[1][1], inside)
    inner = jnp.zeros((CELLS, C), f32)
    start_here = None
    one = (lane >= CIN) & (lane < CIN + 3)
    moves = ((near, near_inside), (block, inside), (far, far_inside))
    for j, (moved, present) in enumerate(moves):
        moved = jnp.where(one, present, moved)
        start = dot(moved.reshape(span * COLS, WIDE).astype(bf16), w_wide[...])
        start = start.reshape(STRIPS, ROWS + 2, COLS, C)
        moved = moved.reshape(STRIPS, ROWS + 2, COLS, WIDE)
        for i in range(3):
            patch = start[:, i : i + ROWS].reshape(CELLS, C).astype(bf16)
            if i == 1 and j == 1:
                start_here = patch.astype(f32)
            inner += dot(patch, w_conv[3 * i + j])
            cond_out[3 * i + j] = moved[:, i : i + ROWS].reshape(CELLS, WIDE).astype(bf16)
    cond_out.start()
    inner += b_conv[...]
    gate = jax.nn.sigmoid(inner)
    smooth = (inner * gate).astype(bf16)
    smooth_out[...] = smooth
    slope_out[...] = gate * (1.0 + inner * (1.0 - gate))
    latent = cells[:, :, LATENT : LATENT + C].astype(f32).reshape(CELLS, C)
    mixed = latent + (start_here + dot(smooth, w_out[...]) + b_out[...])
    mixed_out[...] = mixed
    normed = moments(mixed)[0].astype(bf16)
    projected = [dot(normed, w[...]) for w in (w_query, w_key, w_value)]
    projected[0] *= SCALE * LOG2E
    shape = (STRIPS, ROWS, COLS, LANES - MASK)
    row = 2 * ROWS * lax.broadcasted_iota(jnp.int32, shape, 0) + ROWS * place[3]
    row += lax.broadcasted_iota(jnp.int32, shape, 1)
    hidden = jnp.where(row >= valid[place[0]], MASKED, 0.0)
    extras = jnp.where(lane_of(shape) == 0, hidden, 1.0).reshape(CELLS, LANES - MASK)
    for head in range(HEADS):
        at = slice(head * HEAD, (head + 1) * HEAD)
        joined = jnp.concatenate([part[:, at] for part in projected] + [extras], axis=1)
        rows_out[head] = joined.astype(bf16)


def text_kernel(
    text, w_key_turned, w_value_turned, keys_out, values_out, wide_key, wide_value
):
    blank = jnp.zeros((WIDE - GROUP, text.shape[1]), bf16)
    states = text[...]
    both = ((w_key_turned, wide_key, keys_out), (w_value_turned, wide_value, values_out))
    for source, wide, target in both:
        for g in range(2):
            wide[g * WIDE : g * WIDE + GROUP, :] = source[g * GROUP : (g + 1) * GROUP, :]
            wide[g * WIDE + GROUP : (g + 1) * WIDE, :] = blank
        target[...] = dot_nt(states, wide[...]).astype(bf16)


def form_kernel(w_query, w_cross_out, w_attn, query_out, cross_out, spread_out):
    rows = w_query[...].astype(f32)
    blank = jnp.zeros((C, WIDE - GROUP), f32)
    rows = [rows[:, :GROUP], blank, rows[:, GROUP:], blank]
    query_out[...] = jnp.concatenate(rows, axis=1).astype(bf16)
    rows = w_cross_out[...]
    blank = jnp.zeros((WIDE - GROUP, C), bf16)
    cross_out[...] = jnp.concatenate([rows[:GROUP], blank, rows[GROUP:], blank], axis=0)
    rows = w_attn[...].astype(f32)
    gap = jnp.zeros((HEAD, 384 - C), f32)
    for head in range(HEADS):
        part = jnp.concatenate([rows[head * HEAD : (head + 1) * HEAD], gap], axis=1)
        blank = jnp.zeros_like(part)
        block = jnp.concatenate(
            [
                jnp.concatenate([part, blank], axis=1),
                jnp.concatenate([blank, part], axis=1),
                jnp.zeros((LANES - 2 * HEAD, 768), f32),
            ],
            axis=0,
        )
        spread_out[head * LANES : (head + 1) * LANES, :] = block.astype(bf16)


BLOCK = 256
STEP = 512


def attend_kernel(
    own, other, packed_out, full_out, probs_out, keys_out, query_out,
    scores_a, scores_b, probs_a, probs_b, turned_a, turned_b, output, sems,
):
    count = HALF // BLOCK
    keys_turned, query = keys_out.buffer, query_out.buffer
    keys_turned[:, :HALF] = jnp.transpose(own[...])
    keys_turned[:, HALF:] = jnp.transpose(other[...])
    keys_out.start()
    lane = lane_of((HALF, LANES))
    rows = pltpu.roll(own[...].astype(f32), KEY, 1)
    rows = jnp.where((lane >= KEY) & (lane < VALUE), rows, jnp.where(lane == MASK, 1.0, 0.0))
    query_out[...] = jnp.transpose(rows.astype(bf16))
    chunks = [(ref, at) for ref in (own, other) for at in range(0, HALF, STEP)]

    def columns(b):
        return pl.ds(pl.multiple_of(b * BLOCK, BLOCK), BLOCK)

    def score(queries, n, scores, peak):
        ref, at = chunks[n]
        part = dot(ref[at : at + STEP, :], queries)
        scores[n * STEP : (n + 1) * STEP, :] = part
        part = jnp.max(part.reshape(STEP // 8, 8, BLOCK), axis=0)
        return part if peak is None else jnp.maximum(peak, part)

    def sent(b, turned, n):
        return pltpu.make_async_copy(turned, probs_out.at[columns(b)], sems.at[n])

    def half(b, peak, following, scores, probs, turned):
        shift = jnp.max(peak, axis=0, keepdims=True)
        queries = query[:, columns(jnp.minimum(b + 1, count - 1))]
        ahead = None
        for n in range(len(chunks)):
            ahead = score(queries, n, following, ahead)
            keys = slice(n * STEP, (n + 1) * STEP)
            part = jnp.exp2(scores[keys, :] - shift).astype(bf16)
            probs[keys, :] = part
            turned[:, keys] = jnp.transpose(part)
        output[:, columns(b)] = dot(keys_turned[...], probs[...])
        return ahead

    peak = None
    for n in range(len(chunks)):
        peak = score(query[:, :BLOCK], n, scores_a, peak)

    def body(i, peak):
        @pl.when(i > 0)
        def _():
            sent(2 * i - 2, turned_a, 0).wait()

        peak = half(2 * i, peak, scores_b, scores_a, probs_a, turned_a)
        sent(2 * i, turned_a, 0).start()

        @pl.when(i > 0)
        def _():
            sent(2 * i - 1, turned_b, 1).wait()

        peak = half(2 * i + 1, peak, scores_a, scores_b, probs_b, turned_b)
        sent(2 * i + 1, turned_b, 1).start()
        return peak

    lax.fori_loop(0, count // 2, body, peak)
    total = output[...]
    inverse = 1.0 / total[MASK + 1 : MASK + 2, :]
    row = lax.broadcasted_iota(jnp.int32, (LANES, HALF), 0)
    total = jnp.transpose(jnp.where(row == 0, inverse, total * inverse))
    full_out[...] = total
    pairs = total.reshape(CHIPS, 2, PART // 2, LANES)
    lane = lane_of((HALF // 2, LANES))
    low = pltpu.roll(pairs[:, 0].reshape(HALF // 2, LANES), LANES - VALUE, 1)
    high = pltpu.roll(pairs[:, 1].reshape(HALF // 2, LANES), LANES - VALUE + HEAD, 1)
    packed = jnp.where(lane < HEAD, low, jnp.where(lane < 2 * HEAD, high, 0.0))
    packed_out[...] = packed.astype(bf16).reshape(CHIPS, PART // 2, LANES)
    sent(count - 2, turned_a, 0).wait()
    sent(count - 1, turned_b, 1).wait()


def middle_kernel(
    place, lengths, heads_in, mixed, cells, text_keys, text_values, w_attn, b_attn,
    w_cross_query, w_cross_out, b_cross, w_ff_in, b_ff_in, w_ff_turned, b_ff_out, result_out,
    grad_out, heads_out, probs_keep,
):
    half = CELLS // 2
    split = w_attn.shape[1] // 2
    packed = jnp.concatenate([heads_in[head] for head in range(HEADS)], axis=1)
    both = dot(packed, w_attn[...])
    shape = (STRIPS, 1, PART // 2, C)
    attended = jnp.concatenate(
        [both[:, :C].reshape(shape), both[:, split : split + C].reshape(shape)], axis=1
    ).reshape(CELLS, C)
    first = mixed[...] + attended + b_attn[...]
    unit_two, rate_two = moments(first)
    cross_query = dot(unit_two.astype(bf16), w_cross_query[...]).astype(bf16)
    lane = lane_of((TEXT, WIDE))
    in_head = [(lane >= HEAD * h) & (lane < HEAD * (h + 1)) for h in range(HEADS // 2)]
    groups = [slice(0, WIDE), slice(WIDE, 2 * WIDE)]

    def by_head(text):
        kept = []
        for lanes in groups:
            here = text[:, lanes]
            kept.append(
                jnp.concatenate([jnp.where(m, here, jnp.zeros_like(here)) for m in in_head], 0)
            )
        return kept

    keys, values = by_head(text_keys), by_head(text_values)
    spans = [slice(g * HEADS // 2 * TEXT, (g + 1) * HEADS // 2 * TEXT) for g in range(2)]
    heads = [slice(h * TEXT, (h + 1) * TEXT) for h in range(HEADS)]
    token = lane_of((CELLS, TEXT)) < lengths[place[0]]
    scores = [dot_nt(cross_query[:, groups[g]], keys[g]) * SCALE for g in range(2)]
    scores = jnp.concatenate(scores, axis=1)
    for at in heads:
        part = jnp.where(token, scores[:, at], MASKED)
        weights = jnp.exp(part - jnp.max(part, -1, keepdims=True))
        probs_keep[:, at] = weights / jnp.sum(weights, -1, keepdims=True)
    cross = [dot(probs_keep[:, spans[g]].astype(bf16), values[g]) for g in range(2)]
    cross = jnp.concatenate(cross, axis=1).astype(bf16)
    second = first + dot(cross, w_cross_out[...]) + b_cross[...]
    unit_three, rate_three = moments(second)
    normed_three = unit_three.astype(bf16)
    upstream = cells[:, :, COTANGENT : COTANGENT + C].reshape(CELLS, C)
    result = second + b_ff_out[...]
    grad_normed = jnp.zeros((CELLS, C), f32)
    step = 256
    for at in range(0, FF, step):
        ups, gates = slice(at, at + step), slice(FF + at, FF + at + step)
        value = dot(normed_three, w_ff_in[:, ups]) + b_ff_in[ups]
        gate = dot(normed_three, w_ff_in[:, gates]) + b_ff_in[gates]
        normal = 0.5 + 0.5 * lax.erf(gate * (0.5**0.5))
        density = jnp.exp(gate * gate * -0.5) * 0.3989422804014327
        gelu = gate * normal
        result += dot_nt((value * gelu).astype(bf16), w_ff_turned[:, ups])
        grad_act = dot(upstream, w_ff_turned[:, ups])
        grad_value = (grad_act * gelu).astype(bf16)
        grad_gate = (grad_act * value * (normal + gate * density)).astype(bf16)
        grad_normed += dot_nt(grad_value, w_ff_in[:, ups])
        grad_normed += dot_nt(grad_gate, w_ff_in[:, gates])
    result_out[...] = result.astype(bf16)
    grad_second = upstream.astype(f32) + norm_back(unit_three, rate_three, grad_normed)
    grad_cross = dot_nt(grad_second.astype(bf16), w_cross_out[...]).astype(bf16)
    grad_probs = [dot_nt(grad_cross[:, groups[g]], values[g]) for g in range(2)]
    grad_probs = jnp.concatenate(grad_probs, axis=1)
    grad_scores = []
    for at in heads:
        probs, grads = probs_keep[:, at], grad_probs[:, at]
        weighted = jnp.sum(probs * grads, -1, keepdims=True)
        grad_scores.append((probs * (grads - weighted)).astype(bf16))
    grad_scores = jnp.concatenate(grad_scores, axis=1)
    grad_query = [dot(grad_scores[:, spans[g]], keys[g]) for g in range(2)]
    grad_query = (jnp.concatenate(grad_query, axis=1) * SCALE).astype(bf16)
    grad_first = grad_second + norm_back(
        unit_two, rate_two, dot_nt(grad_query, w_cross_query[...])
    )
    grad_out[...] = grad_first
    pairs = grad_first.reshape(STRIPS, 2, PART // 2, C)
    gap = jnp.zeros((half, split - C), f32)
    both = jnp.concatenate(
        [pairs[:, 0].reshape(half, C), gap, pairs[:, 1].reshape(half, C), gap], axis=1
    ).astype(bf16)
    packed = dot_nt(both, w_attn[...]).astype(bf16)
    for head in range(HEADS):
        heads_out[head] = packed[:, head * LANES : (head + 1) * LANES]


WIDE_BLOCK = 512
WIDE_STEP = 1024


def attend_back_kernel(
    keys_turned, query_turned, full, packed, probs_in, own_out, other_out,
    grads, left, sums, scores, probs_a, probs_b, sems,
):
    half, count = HALF // 2, HALF // WIDE_BLOCK

    def block(b):
        return pl.ds(pl.multiple_of(b * WIDE_BLOCK, WIDE_BLOCK), WIDE_BLOCK)

    def fetched(b, probs, n):
        return pltpu.make_async_copy(probs_in.at[block(b)], probs, sems.at[n])

    fetched(0, probs_a, 0).start()
    fetched(1, probs_b, 1).start()
    lane = lane_of((half, LANES))
    value_lane = (lane >= VALUE) & (lane < MASK)
    pairs = packed[...].reshape(half, LANES).astype(f32)
    low = jnp.where(value_lane, pltpu.roll(pairs, VALUE, 1), 0.0)
    high = jnp.where(value_lane, pltpu.roll(pairs, VALUE - HEAD, 1), 0.0)
    shape = (CHIPS, 1, PART // 2, LANES)
    upstream = jnp.concatenate([low.reshape(shape), high.reshape(shape)], axis=1)
    upstream = upstream.reshape(HALF, LANES)
    lane = lane_of((HALF, LANES))
    outputs = full[...]
    upstream *= jnp.sum(jnp.where(lane == 0, outputs, 0.0), axis=1, keepdims=True)
    weighted = jnp.sum(upstream * outputs, axis=1, keepdims=True)
    first = weighted.astype(bf16).astype(f32)
    upstream = jnp.where(lane == MASK + 4, -first, upstream)
    upstream = jnp.where(lane == MASK + 5, first - weighted, upstream).astype(bf16)
    grads[...] = upstream
    for b in range(count):
        rows, at = slice(b * WIDE_BLOCK, (b + 1) * WIDE_BLOCK), 2 * b * WIDE_BLOCK
        left[:, at : at + WIDE_BLOCK] = query_turned[:, rows]
        left[:, at + WIDE_BLOCK : at + 2 * WIDE_BLOCK] = jnp.transpose(upstream[rows])
    sums[...] = jnp.zeros_like(sums)

    def work(b, probs):
        rows = block(b)
        upstream = grads[rows, :]
        both = left[:, pl.ds(pl.multiple_of(2 * b * WIDE_BLOCK, 2 * WIDE_BLOCK), 2 * WIDE_BLOCK)]
        for at in range(0, 2 * HALF, WIDE_STEP):
            keys = slice(at, at + WIDE_STEP)
            part = probs[:, keys]
            grad = dot(upstream, keys_turned[:, keys])
            grad = (part.astype(f32) * grad).astype(bf16)
            sums[:, keys] += dot(both, jnp.concatenate([grad, part], axis=0))
            scores[keys, :] = jnp.transpose(grad)
        grad_query = jnp.transpose(dot(keys_turned[...], scores[...])) * SCALE
        own_out[rows, :] = pltpu.roll(grad_query, LANES - KEY, 1)

    def body(i, carry):
        fetched(2 * i, probs_a, 0).wait()
        work(2 * i, probs_a)

        @pl.when(2 * i + 2 < count)
        def _():
            fetched(2 * i + 2, probs_a, 0).start()

        fetched(2 * i + 1, probs_b, 1).wait()
        work(2 * i + 1, probs_b)

        @pl.when(2 * i + 3 < count)
        def _():
            fetched(2 * i + 3, probs_b, 1).start()

        return carry

    lax.fori_loop(0, count // 2, body, 0)
    scale = jnp.where(lane < VALUE, 1.0 / LOG2E, 1.0)
    rest = jnp.where(lane < MASK, jnp.transpose(sums[:, :HALF]) * scale, 0.0)
    own_out[...] = jnp.where(lane < KEY, own_out[...], rest)
    rest = jnp.where(
        (lane >= KEY) & (lane < MASK), jnp.transpose(sums[:, HALF:]) * scale, 0.0
    )
    other_out[...] = rest.astype(bf16)


def join_kernel(w_query, w_key, w_value, joined_out):
    blank = jnp.zeros((C, LANES - MASK), f32)
    parts = [w[...].astype(f32) for w in (w_query, w_key, w_value)]
    for head in range(HEADS):
        at = slice(head * HEAD, (head + 1) * HEAD)
        joined = jnp.concatenate([part[:, at] for part in parts] + [blank], axis=1)
        joined_out[:, head * LANES : (head + 1) * LANES] = joined.astype(bf16)


def unpack_kernel(parcel, result_out, latent_out):
    for item in range(STRIPS):
        tiles = [
            parcel[item, SHARE + PART * t : SHARE + PART * (t + 1), :] for t in range(6)
        ]
        result_out[item] = jnp.concatenate(tiles[:3], axis=1)[:, :C]
        latent_out[item] = jnp.concatenate(tiles[3:], axis=1)[:, :C].astype(f32)


def widen_kernel(w_in, b_in, turned_out):
    wide = jnp.concatenate([w_in[...], bias_rows(b_in[...])], axis=0)
    turned_out[...] = jnp.transpose(wide)


def finish_kernel(
    place, rows, w_qkv, mixed, grad_first, slope, smooth, cond, w_out, result, back_out, parts_out
):
    joined = jnp.concatenate([rows[head] for head in range(HEADS)], axis=1)
    unit, rate = moments(mixed[...])
    latent = grad_first[...] + norm_back(unit, rate, dot_nt(joined, w_qkv[...]))
    branch = latent.astype(bf16)
    blank = jnp.zeros((CELLS, 384 - C), bf16)
    back = jnp.concatenate([result[...], blank, branch, blank], axis=1)
    for t in range(6):
        back_out[:, t] = back[:, t * LANES : (t + 1) * LANES].reshape(STRIPS, PART, LANES)
    back_out.start()
    inner = (dot_nt(branch, w_out[...]) * slope[...]).astype(bf16)
    inner_turned = jnp.transpose(inner)
    branch_turned = jnp.transpose(branch)
    here, there = place[1], 1 - place[1]

    def put(side, at, values):
        values = values.astype(bf16)
        for t in range(0, 3 * LANES, LANES):
            parts_out[side, at : at + C, :] = values[:, t : t + LANES]
            at += C

    lane = lane_of((C, LANES))
    ones = jnp.zeros((C, LANES), f32)
    kept = None
    for n in range(10):
        moment = dot(inner_turned, cond[n]) if n < 9 else dot(branch_turned, cond[4])
        one = pltpu.roll(moment[:, LANES:], 3 * n, 1)
        ones = jnp.where((lane >= 64 + 3 * n) & (lane < 67 + 3 * n), one, ones)
        if n % 2 == 0:
            kept = moment[:, :CIN]
            continue
        both = jnp.concatenate([kept, moment[:, :CIN]], axis=1)
        pair = n // 2
        put(here if pair < 3 else there, 3 * C * (pair % 3), both)
    values = dot(branch_turned, smooth[...])
    last = jnp.concatenate([values[:, 2 * LANES :], ones[:, 64:]], axis=1)
    put(there, 6 * C, jnp.concatenate([values[:, : 2 * LANES], last], axis=1))
    for side in range(2):
        parts_out[side, 9 * C :, :] = jnp.zeros((SUM_ROWS - 9 * C, LANES), bf16)


def weights_kernel(
    place, mine, theirs, w_turned, w_conv, win_out, bin_out, wconv_out, bconv_out, wout_out,
    bout_out, taps, sems,
):
    here = place[1]

    def tile(half, n):
        rows = slice(C * n, C * (n + 1))
        return jnp.where(here == half, mine[rows, :], theirs[rows, :]).astype(f32)

    ones = tile(1, 8)
    lane = lane_of((C, LANES))
    low = lane < 64

    def moment_of(n):
        pair = n // 2
        first, middle, last = [tile(pair // 3, 3 * (pair % 3) + t) for t in range(3)]
        if n % 2:
            middle, last = pltpu.roll(middle, 64, 1), pltpu.roll(last, 64, 1)
            first, middle = jnp.where(low, middle, last), last
        one = jnp.where(lane < 67, pltpu.roll(ones, LANES - 3 * n, 1) if n else ones, 0.0)
        return jnp.concatenate([first, jnp.where(low, middle, one)], axis=1).astype(bf16)

    last = jnp.concatenate([tile(1, 6), tile(1, 7), ones], axis=1)
    last = jnp.transpose(last)
    wout_out[...] = last[:C]
    bconv_out[...] = last[C + 12]
    bout_out[...] = last[C + 27]
    grad_in = jnp.zeros((C, WIDE), f32)
    copies = []
    for n in range(9):
        moment = moment_of(n)
        taps[n] = dot_nt(w_turned[...], moment)
        copy = pltpu.make_async_copy(taps.at[n], wconv_out.at[n], sems.at[n])
        copy.start()
        copies.append(copy)
        grad_in += dot(w_conv[n], moment)
    grad_in = jnp.transpose(grad_in + moment_of(9).astype(f32))
    win_out[...] = grad_in[:CIN]
    bin_out[...] = grad_in[CIN]
    for copy in copies:
        copy.wait()


def swap(array):
    return lax.ppermute(array, "c", [(0, 1), (1, 0)])


def across(blocks, axes):
    return lax.all_to_all(blocks, axes, 0, 0, tiled=True)


def per_device(
    latent, condition, text_states, valid_rows, text_lengths, w_in, b_in, w_conv, b_conv, w_out,
    b_out, w_query, w_key, w_value, w_attn_out, b_attn_out, w_cross_query, w_cross_key,
    w_cross_value, w_cross_out, b_cross_out, w_ff_in, b_ff_in, w_ff_out, b_ff_out, cotangent,
):
    core, column = lax.axis_index("c"), 2 * lax.axis_index("x") + lax.axis_index("c")
    item, lower = lax.axis_index("a"), lax.axis_index("b")
    place = jnp.stack([item, core, column, lower]).astype(jnp.int32)

    wide = [
        jnp.pad(x.reshape(STRIPS, PART, -1), ((0, 0), (0, 0), (0, lanes - x.shape[-1])))
        for x, lanes in ((condition, 256), (latent, 384), (cotangent, 384))
    ]
    cells = across(jnp.concatenate(wide, axis=-1), "a")

    text = lax.dynamic_index_in_dim(text_states, item, 0, keepdims=False)
    text = jnp.pad(text, ((0, TEXT - text.shape[0]), (0, 0)))
    text_keys, text_values = call(
        text_kernel,
        (out(TEXT, 2 * WIDE), out(TEXT, 2 * WIDE)),
        (text, w_cross_key.T, w_cross_value.T),
        "text",
        scratch=[pltpu.VMEM((2 * WIDE, text.shape[1]), bf16)] * 2,
        fetch=(0, 1, 2),
        store=(0, 1),
        cost=pl.CostEstimate(flops=4 * 10**9, bytes_accessed=2 * 10**6, transcendentals=0),
    )
    (w_turned,) = call(
        widen_kernel, (out(C, WIDE),), (w_in, b_in), "widen", fetch=(0, 1), store=(0,)
    )
    cells, text_keys, w_turned = after(cells, text_keys, w_turned)

    here = cells[:, :, :WIDE].reshape(STRIPS, ROWS, COLS, WIDE)
    ends = jnp.concatenate([here[:, :1], here[:, ROWS - 1 :]], axis=1)
    beside = lax.ppermute(ends, "b", [(0, 1), (1, 0)])
    right_way = [(i, i + 1) for i in range(7)]

    def edge(col):
        rows = jnp.concatenate([here[:, :, col], beside[:, :, col]], axis=1)
        return rows.reshape(STRIPS * (ROWS + 2), WIDE)

    left = lax.ppermute(edge(COLS - 1), ("x", "c"), right_way)
    right = lax.ppermute(edge(0), ("x", "c"), [(b, a) for a, b in right_way])
    beside, first_bias = after(beside, b_in)
    (
        w_in_here, b_in_here, taps_here, b_conv_here, w_out_here, b_out_here, w_query_here,
        w_key_here, w_value_here,
    ) = bring(
        [
            w_in, first_bias, w_conv.reshape(9, C, C), b_conv, w_out, b_out, w_query, w_key,
            w_value,
        ],
        "load_adapter",
    )
    rows, mixed, smooth, slope, cond = call(
        adapter_kernel,
        (
            out(HEADS, CELLS, LANES),
            out(CELLS, C, dtype=f32),
            out(CELLS, C),
            out(CELLS, C, dtype=f32),
            out(9, CELLS, WIDE),
        ),
        (
            place, valid_rows, cells, beside, left, right, w_in_here, b_in_here, taps_here,
            b_conv_here, w_out_here, b_out_here, w_query_here, w_key_here, w_value_here,
        ),
        "adapter",
        scalars=2,
        scratch=[pltpu.VMEM((WIDE, C), bf16)],
        vmem=24,
        store=(1, 2, 3, 4),
        near=(0,),
        held=tuple(range(6, 15)),
    )

    own = across(rows, GROUP_OF_ITEM).reshape(HALF, LANES)

    other = swap(own)
    _, attn_weight = after(own, w_attn_out)
    w_cross_query_wide, w_cross_out_wide, w_attn_spread = call(
        form_kernel,
        (out(C, 2 * WIDE), out(2 * WIDE, C), out(HEADS * LANES, 768)),
        (w_cross_query, w_cross_out, attn_weight),
        "form",
        fetch=(2, 0, 1),
        store=(0, 1),
        near=(2,),
    )
    own, w_attn_spread = after(own, w_attn_spread)
    packed, full, probs, keys_turned, query_turned = call(
        attend_kernel,
        (
            out(CHIPS, PART // 2, LANES),
            out(HALF, LANES, dtype=f32),
            out(HALF, 2 * HALF),
            out(LANES, 2 * HALF),
            out(LANES, HALF),
        ),
        (own, other),
        "attend",
        scratch=[
            pltpu.VMEM((2 * HALF, BLOCK), f32),
            pltpu.VMEM((2 * HALF, BLOCK), f32),
            pltpu.VMEM((2 * HALF, BLOCK), bf16),
            pltpu.VMEM((2 * HALF, BLOCK), bf16),
            pltpu.VMEM((BLOCK, 2 * HALF), bf16),
            pltpu.VMEM((BLOCK, 2 * HALF), bf16),
            pltpu.VMEM((LANES, HALF), f32),
            pltpu.SemaphoreType.DMA((2,)),
        ],
        vmem=32,
        store=(1, 3, 4),
        near=(0,),
        far=(4,),
    )

    heads_in = across(packed.reshape(HEADS, CELLS // 2, LANES), GROUP_OF_ITEM)
    result, grad_first, heads_out = call(
        middle_kernel,
        (out(CELLS, C), out(CELLS, C, dtype=f32), out(HEADS, CELLS // 2, LANES)),
        (
            place, text_lengths, heads_in, mixed, cells, text_keys, text_values,
            w_attn_spread, b_attn_out, w_cross_query_wide, w_cross_out_wide, b_cross_out,
            w_ff_in, b_ff_in, w_ff_out.T, b_ff_out,
        ),
        "middle",
        scalars=2,
        scratch=[pltpu.VMEM((CELLS, HEADS * TEXT), f32)],
        vmem=32,
        fetch=(3, 8, 9, 5, 6, 10, 11, 12, 13, 14, 15),
        store=(0, 1),
        near=(2,),
        held=(7,),
    )

    grads_in = across(heads_out, GROUP_OF_ITEM).reshape(CHIPS, PART // 2, LANES)
    own_grads, other_grads = call(
        attend_back_kernel,
        (out(HALF, LANES, dtype=f32), out(HALF, LANES)),
        (keys_turned, query_turned, full, grads_in, probs),
        "attend_back",
        scratch=[
            pltpu.VMEM((HALF, LANES), bf16),
            pltpu.VMEM((LANES, 2 * HALF), bf16),
            pltpu.VMEM((LANES, 2 * HALF), f32),
            pltpu.VMEM((2 * HALF, WIDE_BLOCK), bf16),
            pltpu.VMEM((WIDE_BLOCK, 2 * HALF), bf16),
            pltpu.VMEM((WIDE_BLOCK, 2 * HALF), bf16),
            pltpu.SemaphoreType.DMA((2,)),
        ],
        vmem=36,
        near=(0, 1),
        far=(4,),
    )

    _, query_weight = after(other_grads, w_query)
    (w_joined,) = call(
        join_kernel,
        (out(C, HEADS * LANES),),
        (query_weight, w_key, w_value),
        "join",
        fetch=(0, 1, 2),
        near=(0,),
    )
    own_grads, w_joined = after(own_grads, w_joined)
    row_grads = (own_grads + swap(other_grads).astype(f32)).astype(bf16)
    row_grads = across(row_grads.reshape(HEADS, CELLS, LANES), GROUP_OF_ITEM)
    back, parts = call(
        finish_kernel,
        (out(STRIPS, 6, PART, LANES), out(2, SUM_ROWS, LANES)),
        (
            place, row_grads, w_joined, mixed, grad_first, slope, smooth, cond, w_out, result,
        ),
        "finish",
        scalars=1,
        store=(0,),
    )

    shares = (parts[0].astype(f32) + swap(parts[1]).astype(f32)).astype(bf16)
    shares = shares.reshape(8, 8, SHARE, LANES).transpose(1, 0, 2, 3)
    shares = across(shares.reshape(CHIPS, SHARE, LANES), CHIPS_ALL)
    share = jnp.sum(shares.astype(f32), axis=0).astype(bf16)

    sums = jnp.broadcast_to(share[None], (STRIPS, SHARE, LANES))
    parcel = jnp.concatenate([sums, back.reshape(STRIPS, 6 * PART, LANES)], axis=1)
    parcel = across(parcel, "a")
    sums = parcel[:, :SHARE].reshape(1, STRIPS * SHARE, LANES)
    sums = jnp.broadcast_to(sums, (HEADS,) + sums.shape[1:])
    mine = across(sums, GROUP_OF_ITEM).reshape(SUM_ROWS, LANES)
    mine, parcel, w_turned = after(mine, parcel, w_turned)
    theirs = swap(mine)
    taps_here, w_turned_here = bring([w_conv.reshape(9, C, C), w_turned], "load_weights")
    result, latent_grad = call(
        unpack_kernel,
        (out(STRIPS, PART, C), out(STRIPS, PART, C, dtype=f32)),
        (parcel,),
        "unpack",
        store=(0, 1),
    )
    grad_w_in, grad_b_in, grad_w_conv, grad_b_conv, grad_w_out, grad_b_out = call(
        weights_kernel,
        (
            out(CIN, C, dtype=f32),
            out(C, dtype=f32),
            out(9, C, C, dtype=f32),
            out(C, dtype=f32),
            out(C, C, dtype=f32),
            out(C, dtype=f32),
        ),
        (place, mine, theirs, w_turned_here, taps_here),
        "weights",
        scalars=1,
        scratch=[
            pltpu.VMEM((9, C, C), f32),
            pltpu.SemaphoreType.DMA((9,)),
        ],
        vmem=24,
        store=(0, 4),
        far=(7,),
        held=(3, 4),
        cost=pl.CostEstimate(flops=6 * 10**9, bytes_accessed=2 * 10**7, transcendentals=0),
    )
    grid = (STRIPS, ROWS, COLS, C)
    return (
        result.reshape(grid),
        latent_grad.reshape(grid),
        grad_w_in,
        grad_b_in,
        grad_w_conv.reshape(3, 3, C, C),
        grad_b_conv,
        grad_w_out,
        grad_b_out,
    )


def solution(mesh):
    split = Mesh(mesh.devices.reshape(8, 2, 4, 2), ("a", "b", "x", "c"))
    cells = P(None, ("a", "b"), ("x", "c"), None)
    in_specs = (cells, cells) + (P(),) * 23 + (cells,)
    out_specs = (cells, cells) + (P(),) * 6
    return jax.shard_map(
        per_device, mesh=split, in_specs=in_specs, out_specs=out_specs, check_vma=False
    )
```
